256 devices in a mesh: fibre: 32 (over z, x_lo, core), win: 8 (over x_hi, y).
Axes of the slice: x: 4 (x_hi: 2, x_lo: 2; x = x_hi * 2 + x_lo), y: 4, z: 8, core: 2. Of those that a mesh axis runs over, the one named last changes fastest.
Arguments:
- raw_segments: bfloat16 [64, 512, 4352], P('win', 'fibre'), may hold values from -6 to 6
- offsets: int32 [64], P('win'), may hold values from 0 to 256, as said below
- channel_mask: int32 [512], P('fibre'), may hold values 0 or 1
Outputs:
- correlations: float32 [128, 512, 512], P('win', 'fibre')
The draws below stay inside these ranges and needn't reach their ends.
Inputs may be any that keep to these rules, and one draw needn't show every extreme that they name: Window start offsets; 256 occurs in every draw.
All inputs are finite; a program needn't handle non-finite values. No bound on the sum of `channel_mask` on one device may be relied on, other than what follows from the above.
Results may differ from the reference program's by a relative error of at most 0.004.
Values may be sent and summed in bfloat16 or wider, within the bound.
A program may use at most 128 MiB of HBM per device.

```python
import math
import jax
import jax.numpy as jnp
from jax import lax

L = 4096
BAND_LO = 64
NB = 1024
SMOOTH = 64
LAGS = 512
SPAN = 128
MAXOFF = 256
WIN_DEV = 8
SEG = 4352
CHANNELS = 512
WINDOWS = 64
N_WIN = 8


def draw_offsets(key, part):
    key = jax.random.fold_in(key, 11)
    first, second = jax.random.split(key, 2)
    values = jax.random.randint(first, (WINDOWS,), 0, MAXOFF + 1)
    chosen = jax.random.randint(second, (), 0, WINDOWS)
    values = values.at[chosen].set(MAXOFF)
    return values.astype(jnp.int32)


def place_ends(drawn, own_key, smallest, high):
    spot = [jax.random.randint(jax.random.fold_in(own_key, axis), (), 0, length) for axis, length in enumerate(drawn.shape)]
    longest = drawn.shape.index(max(drawn.shape))
    next_to = spot[:longest] + [(spot[longest] + 1) % drawn.shape[longest]] + spot[longest + 1:]
    return drawn.at[tuple(spot)].set(smallest).at[tuple(next_to)].set(high)


def level_of(key, extent, cuts, least, high):
    level = 1.0
    for dim, shards_of in cuts:
        steps = jax.random.uniform(jax.random.fold_in(jax.random.fold_in(key, 6), dim), (shards_of,), jnp.float32, least / len(cuts), high / len(cuts))
        level = level * jnp.repeat(jnp.exp(steps), extent[dim] // shards_of).reshape((-1,) + (1,) * (len(extent) - 1 - dim))
    return level


def centred(stream_key, shape, width, limit, pieces=(), kind=jnp.bfloat16):
    factor_of = level_of(stream_key, shape, pieces, -0.22, 0.18) if pieces else 1.0
    entries = jax.random.normal(stream_key, shape, jnp.float32) * width * factor_of
    return jnp.minimum(jnp.maximum(entries, -limit), limit).astype(kind)


def setup_inputs(seed: int = 0) -> dict:
    arg_keys = jax.random.split(jax.random.key(seed), 4)
    raw_segments = centred(arg_keys[0], (WINDOWS, CHANNELS, SEG), 1.0, 6.0, ((0, 8), (1, 32)))
    offsets = draw_offsets(jax.random.fold_in(arg_keys[3], 71), 0)
    channel_mask = place_ends((jax.random.randint(arg_keys[2], (CHANNELS,), 0, 8) < 7).astype(jnp.int32), jax.random.fold_in(arg_keys[2], 1), 0, 1)
    return {"raw_segments": raw_segments, "offsets": offsets, "channel_mask": channel_mask}


EPS = 1e-06

def hann_taper():
    position = jnp.arange(L, dtype=jnp.float32)
    return 0.5 - 0.5 * jnp.cos(position * (2.0 * math.pi / L))

def lag_table():
    frequency = BAND_LO + jnp.arange(NB, dtype=jnp.int32)
    lag_index = jnp.arange(LAGS, dtype=jnp.int32) - LAGS // 2
    phase_turns = jnp.mod(frequency[:, None] * lag_index[None, :], L)
    angles = phase_turns.astype(jnp.float32) * (2.0 * math.pi / L)
    return jnp.concatenate([jnp.cos(angles), -jnp.sin(angles)], 0).astype(jnp.bfloat16)

def whitened(raw_segments, offsets, channel_mask):
    taken = jax.vmap(lambda block, begin: lax.dynamic_slice_in_dim(block, begin, L, 1))(raw_segments, offsets.astype(jnp.int32))
    samples = taken.astype(jnp.float32)
    samples = samples - lax.optimization_barrier(jnp.mean(samples, axis=-1, keepdims=True))
    samples = samples * hann_taper()
    spectrum = jnp.fft.rfft(samples, axis=-1)[..., BAND_LO:BAND_LO + NB]
    real_part = jnp.real(spectrum)
    imag_part = jnp.imag(spectrum)
    windows, channels = (real_part.shape[0], real_part.shape[1])
    power = (real_part * real_part + imag_part * imag_part).reshape(windows, channels, NB // SMOOTH, SMOOTH)
    factor = 1.0 / jnp.sqrt(lax.optimization_barrier(jnp.mean(power, axis=-1)) + EPS)
    factor = jnp.repeat(factor, SMOOTH, axis=-1)
    keep = channel_mask.astype(jnp.float32)[None, :, None]
    return (jnp.concatenate([real_part * factor, imag_part * factor], -1) * keep).astype(jnp.bfloat16)

def reference(raw_segments, offsets, channel_mask):
    spectra = whitened(raw_segments, offsets, channel_mask)
    channels = spectra.shape[1]
    grouped = spectra.reshape(N_WIN, WIN_DEV, channels, 2 * NB)
    padded = jnp.pad(grouped, ((0, 0), (0, 0), (0, SPAN), (0, 0)))
    table = lag_table()
    scale = 1.0 / math.sqrt(NB * WIN_DEV * N_WIN)
    own_real = grouped[..., :NB].astype(jnp.float32)
    own_imag = grouped[..., NB:].astype(jnp.float32)

    def per_offset(shift):
        partner = lax.dynamic_slice_in_dim(padded, shift, channels, 2)
        other_real = partner[..., :NB].astype(jnp.float32)
        other_imag = partner[..., NB:].astype(jnp.float32)
        cross_real = lax.optimization_barrier(jnp.sum(own_real * other_real + own_imag * other_imag, axis=1))
        cross_imag = lax.optimization_barrier(jnp.sum(own_imag * other_real - own_real * other_imag, axis=1))
        cross = jnp.concatenate([cross_real, cross_imag], -1).astype(jnp.bfloat16)
        lagged = jnp.dot(cross.reshape(N_WIN * channels, 2 * NB), table, preferred_element_type=jnp.float32)
        return lax.optimization_barrier(jnp.sum(lagged.reshape(N_WIN, channels, LAGS), axis=0)) * scale
    return lax.map(per_offset, jnp.arange(1, SPAN + 1, dtype=jnp.int32))
```

```python
import functools
import math

import jax
import jax.numpy as jnp
import numpy as np
from jax import lax
from jax.experimental import pallas as pl
from jax.experimental.pallas import tpu as pltpu
from jax.sharding import PartitionSpec as P

MESH = pl.DeviceIdType.MESH
L = 4096
BAND_LO = 64
NB = 1024
SMOOTH = 64
LAGS = 512
SPAN = 128
EPS = 1e-06
RADIX = 16
TAIL = L // RADIX
PLANE = 32
WIN = 8
QUAD = 4
BINS = 32
F32 = jnp.float32
BF16 = jnp.bfloat16


def second_stage():
    b = np.arange(TAIL)[:, None]
    lane = np.arange(128)[None, :]
    half, imag, low = lane // 64, (lane // 32) % 2, lane % 32
    angle = 2.0 * np.pi * ((b * (BAND_LO // RADIX + half * 32 + low)) % TAIL) / TAIL
    cos, sin = np.cos(angle), np.sin(angle)
    real = np.concatenate([cos, sin], 0)
    imaginary = np.concatenate([-sin, cos], 0)
    pick = np.concatenate([imag, imag], 1) == 0
    straight = np.where(imag == 0, real, imaginary)
    turned = np.where(imag == 0, -imaginary, real)
    del pick
    whole = np.concatenate([straight, turned], 1).astype(np.float32)
    high = whole.astype(jnp.bfloat16)
    low_part = (whole - high.astype(np.float32)).astype(jnp.bfloat16)
    return high, low_part


def twiddles():
    f = np.arange(RADIX)[:, None]
    b = np.arange(TAIL)[None, :]
    angle = 2.0 * np.pi * (f * b) / L
    return np.cos(angle).astype(np.float32), np.sin(angle).astype(np.float32)


def lag_rows():
    frequency = np.arange(NB, dtype=np.int64) + BAND_LO
    lag_index = np.arange(LAGS, dtype=np.int64) - LAGS // 2
    turns = np.mod(frequency[:, None] * lag_index[None, :], L).astype(np.float32)
    angles = turns * np.float32(2.0 * math.pi / L)
    cos, sin = np.cos(angles.astype(np.float64)), np.sin(angles.astype(np.float64))
    table = np.stack([cos, -sin], 1).astype(np.float32)
    bins = RADIX * np.arange(64)[None, :] + np.arange(RADIX)[:, None]
    return table[bins].reshape(2 * NB, LAGS).astype(jnp.bfloat16)


def real_fft(x):
    n = len(x)
    if n == 2:
        return [(x[0] + x[1], None), (x[0] - x[1], None)]
    even, odd = real_fft(x[0::2]), real_fft(x[1::2])
    half, quarter = n // 2, n // 4
    out = [None] * (half + 1)
    out[0] = (even[0][0] + odd[0][0], None)
    out[half] = (even[0][0] - odd[0][0], None)
    for k in range(1, quarter):
        (er, ei), (orr, oi) = even[k], odd[k]
        c, s = math.cos(2.0 * math.pi * k / n), math.sin(2.0 * math.pi * k / n)
        if 8 * k == n:
            tr, ti = (orr + oi) * c, (oi - orr) * c
        else:
            tr, ti = orr * c + oi * s, oi * c - orr * s
        out[k] = (er + tr, ei + ti)
        out[half - k] = (er - tr, ti - ei)
    out[quarter] = (even[quarter][0], -odd[quarter][0])
    return out


def transform_kernel(offsets, raw, keep, tw_cos, tw_sin, w_hi, w_lo, out, lhs, kept, phase_cos, phase_sin):
    def one_window(w, carry):
        off = offsets[w]
        u = lax.broadcasted_iota(jnp.int32, (RADIX, TAIL), 0) * TAIL + lax.broadcasted_iota(
            jnp.int32, (RADIX, TAIL), 1
        )
        taper = 0.5 - 0.5 * jnp.cos(((u - off) & (L - 1)).astype(F32) * (2.0 * math.pi / L))
        f = lax.broadcasted_iota(jnp.int32, (RADIX, 128), 0)
        lane = lax.broadcasted_iota(jnp.int32, (RADIX, 128), 1)
        k = (BAND_LO // RADIX + (lane // 64) * 32 + lane % 32) * RADIX + f
        angle = ((k * off) & (L - 1)).astype(F32) * (2.0 * math.pi / L)
        phase_cos[w] = jnp.cos(angle)
        phase_sin[w] = jnp.sin(angle)
        samples = raw[w].astype(F32)
        first = jnp.where(
            lax.broadcasted_iota(jnp.int32, (16, TAIL), 1) < off, samples[:, L : L + TAIL], samples[:, :TAIL]
        )
        tiles = [first] + [samples[:, a * TAIL : (a + 1) * TAIL] for a in range(1, RADIX)]
        total = functools.reduce(lambda p, q: p + q, tiles)
        mean = jnp.sum(total, axis=1, keepdims=True) * (1.0 / L)
        tiles = [(tile - mean) * taper[a : a + 1, :] for a, tile in enumerate(tiles)]
        spectrum = real_fft(tiles)
        rows = pl.ds(pl.multiple_of(w * 16, 16), 16)
        for f in range(RADIX):
            re, im = spectrum[f] if f <= RADIX // 2 else spectrum[RADIX - f]
            if f > RADIX // 2:
                im = -im
            if f:
                c, s = tw_cos[f : f + 1, :], tw_sin[f : f + 1, :]
                re, im = (re * c, -re * s) if im is None else (re * c + im * s, im * c - re * s)
            else:
                im = jnp.zeros_like(re)
            for part, value in enumerate((re, im)):
                high = value.astype(BF16)
                lhs[f, rows, part * TAIL : (part + 1) * TAIL] = high
                lhs[f, rows, (2 + part) * TAIL : (3 + part) * TAIL] = (value - high.astype(F32)).astype(BF16)
        return carry

    lax.fori_loop(0, 8, one_window, 0)

    def one_column(f, power):
        high, low = lhs[f, :, : 2 * TAIL], lhs[f, :, 2 * TAIL :]
        both = (
            jnp.dot(high, w_hi[...], preferred_element_type=F32)
            + jnp.dot(high, w_lo[...], preferred_element_type=F32)
            + jnp.dot(low, w_hi[...], preferred_element_type=F32)
        ).reshape(8, 16, 256)
        c = phase_cos[:, pl.ds(f, 1), :]
        s = phase_sin[:, pl.ds(f, 1), :]
        value = (both[:, :, :128] * c + both[:, :, 128:] * s).reshape(128, 128)
        kept[f] = value
        return power + value * value

    power = lax.fori_loop(0, RADIX, one_column, jnp.zeros((128, 128), F32))
    row = lax.broadcasted_iota(jnp.int32, (128, 128), 0)
    col = lax.broadcasted_iota(jnp.int32, (128, 128), 1)
    same = (row // 64 == col // 64) & ((row % 32) // 4 == (col % 32) // 4)
    block = jnp.where(same, 1.0, 0.0).astype(F32)
    mean_power = jnp.dot(power, block, precision=lax.Precision.HIGHEST, preferred_element_type=F32) * (1.0 / SMOOTH)
    flag = jnp.broadcast_to(keep[...].astype(F32)[None], (8, 16, 1)).reshape(128, 1)
    factor = (1.0 / jnp.sqrt(mean_power + EPS)) * flag
    left = lax.broadcasted_iota(jnp.int32, (64, 128), 1) < 64

    def one_store(f, carry):
        value = kept[f] * factor
        top, bottom = value[:64], value[64:]
        out[2 * f] = jnp.where(left, top, pltpu.roll(bottom, 64, 1)).astype(BF16)
        out[2 * f + 1] = jnp.where(left, pltpu.roll(top, 64, 1), bottom).astype(BF16)
        return carry

    lax.fori_loop(0, RADIX, one_store, 0)


def transform(raw, offsets, mask):
    w_hi, w_lo = second_stage()
    tw_cos, tw_sin = twiddles()
    vmem = pl.BlockSpec(memory_space=pltpu.VMEM)
    return pl.pallas_call(
        transform_kernel,
        out_shape=jax.ShapeDtypeStruct((PLANE, 64, 128), BF16),
        in_specs=[pl.BlockSpec(memory_space=pltpu.SMEM)] + [vmem] * 6,
        out_specs=vmem,
        scratch_shapes=[
            pltpu.VMEM((RADIX, 128, 4 * TAIL), BF16),
            pltpu.VMEM((RADIX, 128, 128), F32),
            pltpu.VMEM((8, RADIX, 128), F32),
            pltpu.VMEM((8, RADIX, 128), F32),
        ],
        compiler_params=pltpu.CompilerParams(vmem_limit_bytes=40 * 2**20),
        name="transform",
    )(offsets, raw, mask.reshape(16, 1), tw_cos, tw_sin, w_hi, w_lo)


def place():
    fibre, win = lax.axis_index("fibre"), lax.axis_index("win")
    return fibre // QUAD, win * QUAD + fibre % QUAD


def device(z, s):
    return (z * QUAD + s % QUAD, s // QUAD)


def plane_exchange_kernel(send, recv, send_sem, recv_sem, own_sem):
    z, me = place()
    barrier = pltpu.get_barrier_semaphore()

    def greet(j, carry):
        pl.semaphore_signal(barrier, inc=1, device_id=device(z, (me + j) % PLANE), device_id_type=MESH)
        return carry

    lax.fori_loop(1, PLANE, greet, 0)
    own = pltpu.make_async_copy(send.at[me], recv.at[me], own_sem)
    own.start()
    pl.semaphore_wait(barrier, PLANE - 1)

    def copy(j):
        to = (me + j) % PLANE
        return pltpu.make_async_remote_copy(
            src_ref=send.at[to],
            dst_ref=recv.at[me],
            send_sem=send_sem.at[j],
            recv_sem=recv_sem.at[j],
            device_id=device(z, to),
            device_id_type=MESH,
        )

    def start(j, carry):
        copy(j).start()
        return carry

    def finish(j, carry):
        copy(j).wait()
        return carry

    lax.fori_loop(1, PLANE, start, 0)
    lax.fori_loop(1, PLANE, finish, 0)
    own.wait()


def plane_exchange(send, collective_id, name):
    vmem = pl.BlockSpec(memory_space=pltpu.VMEM)
    return pl.pallas_call(
        plane_exchange_kernel,
        out_shape=jax.ShapeDtypeStruct(send.shape, send.dtype),
        in_specs=[vmem],
        out_specs=vmem,
        scratch_shapes=[
            pltpu.SemaphoreType.DMA((PLANE,)),
            pltpu.SemaphoreType.DMA((PLANE,)),
            pltpu.SemaphoreType.DMA,
        ],
        compiler_params=pltpu.CompilerParams(
            collective_id=collective_id, has_side_effects=True, vmem_limit_bytes=16 * 2**20
        ),
        name=name,
    )(send)


def halo_kernel(planes, own, halo, send_sem, recv_sem):
    z, me = place()
    barrier = pltpu.get_barrier_semaphore()
    for step in (1, 2):
        for to in (z + step, z + planes - step):
            pl.semaphore_signal(barrier, inc=1, device_id=device(to % planes, me), device_id_type=MESH)
    pl.semaphore_wait(barrier, 4)
    copies = [
        pltpu.make_async_remote_copy(
            src_ref=own,
            dst_ref=halo.at[step],
            send_sem=send_sem.at[step],
            recv_sem=recv_sem.at[step],
            device_id=device((z + planes - 1 - step) % planes, me),
            device_id_type=MESH,
        )
        for step in (0, 1)
    ]
    for copy in copies:
        copy.start()
    for copy in copies:
        copy.wait()


def halo_exchange(own, planes):
    vmem = pl.BlockSpec(memory_space=pltpu.VMEM)
    return pl.pallas_call(
        functools.partial(halo_kernel, planes),
        out_shape=jax.ShapeDtypeStruct((2,) + own.shape, own.dtype),
        in_specs=[vmem],
        out_specs=vmem,
        scratch_shapes=[pltpu.SemaphoreType.DMA((2,)), pltpu.SemaphoreType.DMA((2,))],
        compiler_params=pltpu.CompilerParams(
            collective_id=1, has_side_effects=True, vmem_limit_bytes=16 * 2**20
        ),
        name="halo",
    )(own)


def relayout_kernel(recv, own, turned):
    def one(index, carry):
        v, w = index // 2, index % 2
        parts = [
            recv[v * QUAD + q, pl.ds(pl.multiple_of((p * 2 + w) * 16, 16), 16), :]
            for p in range(2)
            for q in range(QUAD)
        ]
        block = jnp.concatenate([part.astype(F32) for part in parts], 0)
        turned[pl.ds(pl.multiple_of(index * 128, 128), 128), :] = block.T
        return carry

    lax.fori_loop(0, 16, one, 0)

    def gather(g, carry):
        real = turned[pl.ds(g, 32, stride=64), :]
        imag = turned[pl.ds(32 + g, 32, stride=64), :]
        own[g] = jnp.concatenate([real, imag], 0).astype(BF16)
        return carry

    lax.fori_loop(0, BINS, gather, 0)


def relayout(recv):
    vmem = pl.BlockSpec(memory_space=pltpu.VMEM)
    return pl.pallas_call(
        relayout_kernel,
        out_shape=jax.ShapeDtypeStruct((BINS, 64, 128), BF16),
        in_specs=[vmem],
        out_specs=vmem,
        scratch_shapes=[pltpu.VMEM((2048, 128), F32)],
        compiler_params=pltpu.CompilerParams(vmem_limit_bytes=16 * 2**20),
        name="relayout",
    )(recv)


def cross_kernel(planes, own, halo, out, near, far, column):
    z, _ = place()
    left = lax.broadcasted_iota(jnp.int32, (64, 128), 1) < 64

    def one_bin(g, carry):
        a = own[g].astype(F32)
        e1 = jnp.where(z + 1 < planes, halo[0, g].astype(F32), 0.0)
        e2 = jnp.where(z + 2 < planes, halo[1, g].astype(F32), 0.0)
        b = jnp.concatenate([a[32:], -a[:32]], 0)
        ra, rb, r1, r2 = (pltpu.roll(x, 64, 1) for x in (a, b, e1, e2))
        lhs = jnp.concatenate([jnp.where(left, a, rb), jnp.where(left, ra, b)], 0)
        rhs = jnp.concatenate([jnp.where(left, a, r1), jnp.where(left, ra, e1)], 0)
        last = jnp.concatenate([e2, r2], 0)
        lhs = lhs.T.astype(BF16)
        rows = pl.ds(pl.multiple_of(g * 128, 128), 128)
        near[rows, :] = jnp.dot(lhs, rhs.astype(BF16), preferred_element_type=F32)
        far[rows, :] = jnp.dot(lhs, last.astype(BF16), preferred_element_type=F32)
        return carry

    lax.fori_loop(0, BINS, one_bin, 0)
    wide = lax.broadcasted_iota(jnp.int32, (128, 128), 1) < 64

    def one_pair(index, carry):
        q, i = index // 8, index % 8
        c = q * 16 + i
        for part, ref in enumerate((near, far)):
            block = jnp.concatenate([ref[pl.ds(c, 64, stride=64), :], ref[pl.ds(c + 8, 64, stride=64), :]], 0)
            column[part * 128 : (part + 1) * 128, :] = block.T
        value = jnp.where(wide, column[pl.ds(c + 1, 128), :], column[pl.ds(c + 9, 128), :]).astype(BF16)
        for v in range(WIN):
            out[v * QUAD + q, pl.ds(pl.multiple_of(i * 16, 16), 16), :] = value[v * 16 : (v + 1) * 16]
        return carry

    lax.fori_loop(0, 32, one_pair, 0)


def cross(own, halo, planes):
    vmem = pl.BlockSpec(memory_space=pltpu.VMEM)
    return pl.pallas_call(
        functools.partial(cross_kernel, planes),
        out_shape=jax.ShapeDtypeStruct((PLANE, 128, 128), BF16),
        in_specs=[vmem, vmem],
        out_specs=vmem,
        scratch_shapes=[pltpu.VMEM((4096, 128), F32), pltpu.VMEM((4096, 128), F32), pltpu.VMEM((256, 128), F32)],
        compiler_params=pltpu.CompilerParams(vmem_limit_bytes=32 * 2**20),
        name="cross",
    )(own, halo)


def lag_kernel(scale, spectra, table, out, lhs):
    left = lax.broadcasted_iota(jnp.int32, (128, 128), 1) < 64
    for f in range(RADIX):
        one, two = spectra[2 * f].astype(F32), spectra[2 * f + 1].astype(F32)
        lhs[:128, f * 128 : (f + 1) * 128] = jnp.where(left, one, pltpu.roll(two, 64, 1)).astype(BF16)
        lhs[128:, f * 128 : (f + 1) * 128] = jnp.where(left, pltpu.roll(one, 64, 1), two).astype(BF16)
    for part in range(LAGS // 128):
        lags = jnp.dot(lhs[...], table[:, part * 128 : (part + 1) * 128], preferred_element_type=F32) * scale
        for c in range(16):
            out[part, pl.ds(c, 16, stride=16), :] = lags[c * 16 : (c + 1) * 16]


def lag_transform(spectra, scale):
    vmem = pl.BlockSpec(memory_space=pltpu.VMEM)
    out = pl.pallas_call(
        functools.partial(lag_kernel, scale),
        out_shape=jax.ShapeDtypeStruct((4, 256, 128), F32),
        in_specs=[vmem, vmem],
        out_specs=vmem,
        scratch_shapes=[pltpu.VMEM((256, 2 * NB), BF16)],
        compiler_params=pltpu.CompilerParams(vmem_limit_bytes=32 * 2**20),
        name="lags",
    )(spectra, lag_rows())
    return out.transpose(1, 0, 2).reshape(16, 16, LAGS)


def body(planes, raw, offsets, mask):
    sent = transform(raw, offsets, mask)
    own = relayout(plane_exchange(sent, 0, "to_bins"))
    halo = halo_exchange(own, planes)
    spectra = plane_exchange(cross(own, halo, planes), 2, "to_offsets")
    return lag_transform(spectra, 1.0 / math.sqrt(NB * 8 * WIN))


def solution(mesh):
    planes = mesh.shape["fibre"] // QUAD
    return jax.shard_map(
        functools.partial(body, planes),
        mesh=mesh,
        in_specs=(P("win", "fibre", None), P("win"), P("fibre")),
        out_specs=P("win", "fibre", None),
        check_vma=False,
    )
```

```python
import functools
import math

import jax
import jax.numpy as jnp
import numpy as np
from jax import lax
from jax.experimental import pallas as pl
from jax.experimental.pallas import tpu as pltpu
from jax.sharding import PartitionSpec as P

MESH = pl.DeviceIdType.MESH
L = 4096
BAND_LO = 64
NB = 1024
SMOOTH = 64
LAGS = 512
SPAN = 128
EPS = 1e-06
RADIX = 16
TAIL = L // RADIX
PLANE = 32
WIN = 8
QUAD = 4
BINS = 32
CHUNK = 8
REL_PITCH = 40
OUT_PITCH = 72
SLOTS = 8
GROUP = 4
F32 = jnp.float32
BF16 = jnp.bfloat16


def second_stage():
    b = np.arange(TAIL)[:, None]
    lane = np.arange(128)[None, :]
    half, imag, low = lane // 64, (lane // 32) % 2, lane % 32
    angle = 2.0 * np.pi * ((b * (BAND_LO // RADIX + half * 32 + low)) % TAIL) / TAIL
    cos, sin = np.cos(angle), np.sin(angle)
    real = np.concatenate([cos, sin], 0)
    imaginary = np.concatenate([-sin, cos], 0)
    straight = np.where(imag == 0, real, imaginary)
    turned = np.where(imag == 0, -imaginary, real)
    whole = np.concatenate([straight, turned], 1).astype(np.float32)
    high = whole.astype(jnp.bfloat16)
    low_part = (whole - high.astype(np.float32)).astype(jnp.bfloat16)
    return high, low_part


def twiddles():
    f = np.arange(RADIX)[:, None]
    b = np.arange(TAIL)[None, :]
    angle = 2.0 * np.pi * (f * b) / L
    return np.cos(angle).astype(np.float32), np.sin(angle).astype(np.float32)


def lag_rows():
    frequency = np.arange(NB, dtype=np.int64) + BAND_LO
    lag_index = np.arange(LAGS, dtype=np.int64) - LAGS // 2
    turns = np.mod(frequency[:, None] * lag_index[None, :], L).astype(np.float32)
    angles = turns * np.float32(2.0 * math.pi / L)
    cos, sin = np.cos(angles.astype(np.float64)), np.sin(angles.astype(np.float64))
    table = np.stack([cos, -sin], 1).astype(np.float32)
    bins = RADIX * np.arange(64)[None, :] + np.arange(RADIX)[:, None]
    return table[bins].reshape(2 * NB, LAGS).astype(jnp.bfloat16)


def real_fft(x):
    n = len(x)
    if n == 2:
        return [(x[0] + x[1], None), (x[0] - x[1], None)]
    even, odd = real_fft(x[0::2]), real_fft(x[1::2])
    half, quarter = n // 2, n // 4
    out = [None] * (half + 1)
    out[0] = (even[0][0] + odd[0][0], None)
    out[half] = (even[0][0] - odd[0][0], None)
    for k in range(1, quarter):
        (er, ei), (orr, oi) = even[k], odd[k]
        c, s = math.cos(2.0 * math.pi * k / n), math.sin(2.0 * math.pi * k / n)
        if 8 * k == n:
            tr, ti = (orr + oi) * c, (oi - orr) * c
        else:
            tr, ti = orr * c + oi * s, oi * c - orr * s
        out[k] = (er + tr, ei + ti)
        out[half - k] = (er - tr, ti - ei)
    out[quarter] = (even[quarter][0], -odd[quarter][0])
    return out


def place():
    fibre, win = lax.axis_index("fibre"), lax.axis_index("win")
    return fibre // QUAD, win * QUAD + fibre % QUAD


def device(z, s):
    return (z * QUAD + s % QUAD, s // QUAD)


def greet_all(planes, z, me):
    barrier = pltpu.get_barrier_semaphore()

    def signal(plane, s):
        pl.semaphore_signal(barrier, inc=1, device_id=device(plane, s), device_id_type=MESH)

    def near(j, carry):
        signal(z, (me + j) % PLANE)
        return carry

    def far(j, carry):
        signal((z + 1) % planes, (me + j) % PLANE)
        return carry

    lax.fori_loop(1, PLANE, near, 0)
    signal((z + 1) % planes, me)
    signal((z + planes - 1) % planes, me)

    @pl.when(me % QUAD + me // QUAD >= WIN - 1)
    def _():
        lax.fori_loop(0, PLANE, far, 0)

    return PLANE - 1 + 2 + 10


def first_stage(offsets, raw, tw_cos, tw_sin, lhs, phase_cos, phase_sin):
    width = 128

    def one_window(w, carry):
        off = offsets[w]
        u = lax.broadcasted_iota(jnp.int32, (RADIX, TAIL), 0) * TAIL + lax.broadcasted_iota(
            jnp.int32, (RADIX, TAIL), 1
        )
        taper = 0.5 - 0.5 * jnp.cos(((u - off) & (L - 1)).astype(F32) * (2.0 * math.pi / L))
        f = lax.broadcasted_iota(jnp.int32, (RADIX, 128), 0)
        lane = lax.broadcasted_iota(jnp.int32, (RADIX, 128), 1)
        k = (BAND_LO // RADIX + (lane // 64) * 32 + lane % 32) * RADIX + f
        angle = ((k * off) & (L - 1)).astype(F32) * (2.0 * math.pi / L)
        phase_cos[w] = jnp.cos(angle)
        phase_sin[w] = jnp.sin(angle)

        def tiles_of(low, size):
            wrapped = lax.broadcasted_iota(jnp.int32, (16, size), 1) + low < off
            first = jnp.where(
                wrapped, raw[w, :, L + low : L + low + size].astype(F32), raw[w, :, low : low + size].astype(F32)
            )
            return [first] + [
                raw[w, :, a * TAIL + low : a * TAIL + low + size].astype(F32) for a in range(1, RADIX)
            ]

        total = functools.reduce(lambda p, q: p + q, tiles_of(0, TAIL))
        mean = jnp.sum(total, axis=1, keepdims=True) * (1.0 / L)
        rows = pl.ds(pl.multiple_of(w * 16, 16), 16)
        for low in range(0, TAIL, width):
            span = slice(low, low + width)
            spectrum = real_fft([(x - mean) * taper[a : a + 1, span] for a, x in enumerate(tiles_of(low, width))])
            for f in range(RADIX):
                re, im = spectrum[f] if f <= RADIX // 2 else spectrum[RADIX - f]
                if f > RADIX // 2:
                    im = -im
                if f:
                    c, s = tw_cos[f : f + 1, span], tw_sin[f : f + 1, span]
                    re, im = (re * c, -re * s) if im is None else (re * c + im * s, im * c - re * s)
                else:
                    im = jnp.zeros_like(re)
                for part, value in enumerate((re, im)):
                    high = value.astype(BF16)
                    start = part * TAIL + low
                    lhs[f, rows, start : start + width] = high
                    start += 2 * TAIL
                    lhs[f, rows, start : start + width] = (value - high.astype(F32)).astype(BF16)
        return carry

    lax.fori_loop(0, 8, one_window, 0)


def second_stage_of(lhs, w_hi, w_lo, kept, phase_cos, phase_sin):
    def some_columns(index, power):
        start = index * GROUP
        whole = lhs[pl.ds(start, GROUP)].reshape(GROUP * 128, 4 * TAIL)
        high, low = whole[:, : 2 * TAIL], whole[:, 2 * TAIL :]
        both = (
            jnp.dot(high, w_hi[...], preferred_element_type=F32)
            + jnp.dot(high, w_lo[...], preferred_element_type=F32)
            + jnp.dot(low, w_hi[...], preferred_element_type=F32)
        )
        for j in range(GROUP):
            c = phase_cos[:, pl.ds(start + j, 1), :]
            s = phase_sin[:, pl.ds(start + j, 1), :]
            one = both[j * 128 : (j + 1) * 128].reshape(8, 16, 256)
            value = (one[:, :, :128] * c + one[:, :, 128:] * s).reshape(128, 128)
            kept[start + j] = value
            power = power + value * value
        return power

    return lax.fori_loop(0, RADIX // GROUP, some_columns, jnp.zeros((128, 128), F32))


def whitening(power, mask):
    row = lax.broadcasted_iota(jnp.int32, (128, 128), 0)
    col = lax.broadcasted_iota(jnp.int32, (128, 128), 1)
    same = (row // 64 == col // 64) & ((row % 32) // 4 == (col % 32) // 4)
    block = jnp.where(same, 1.0, 0.0).astype(F32)
    mean_power = jnp.dot(power, block, precision=lax.Precision.HIGHEST, preferred_element_type=F32) * (1.0 / SMOOTH)
    channel = lax.broadcasted_iota(jnp.int32, (16, 128), 0)
    flag = jnp.zeros((16, 128), F32)
    for c in range(16):
        flag = jnp.where(channel == c, mask[c].astype(F32), flag)
    flag = jnp.broadcast_to(flag[None], (8, 16, 128)).reshape(128, 128)
    return (1.0 / jnp.sqrt(mean_power + EPS)) * flag


def main_kernel(
    planes, offsets, mask, raw_hbm, cos_hbm, sin_hbm, hi_hbm, lo_hbm, got_near, got_far,
    raw, tw_cos, tw_sin, w_hi, w_lo, lhs, kept, phase_cos, phase_sin,
    send, recv, turned, own, halo, near, far, near_col, far_col, send_near, send_far,
    in_sem, own_sem, s_send, s_recv, h_send, h_recv, x_send, x_recv,
):
    z, me = place()
    my_q, my_v = me % QUAD, me // QUAD
    loads = [
        pltpu.make_async_copy(source, target, in_sem.at[i])
        for i, (source, target) in enumerate(
            ((raw_hbm, raw), (cos_hbm, tw_cos), (sin_hbm, tw_sin), (hi_hbm, w_hi), (lo_hbm, w_lo))
        )
    ]
    for load in loads:
        load.start()
    expected = greet_all(planes, z, me)
    for slot in range(SLOTS):
        near_col[slot, 128:, :] = jnp.zeros((128, 128), F32)
        far_col[slot, :128, :] = jnp.zeros((128, 128), F32)
    for load in loads[:3]:
        load.wait()

    first_stage(offsets, raw, tw_cos, tw_sin, lhs, phase_cos, phase_sin)
    for load in loads[3:]:
        load.wait()
    factor = whitening(second_stage_of(lhs, w_hi, w_lo, kept, phase_cos, phase_sin), mask)
    left = lax.broadcasted_iota(jnp.int32, (64, 128), 1) < 64
    pl.semaphore_wait(pltpu.get_barrier_semaphore(), expected)

    def bins_copy(to):
        return pltpu.make_async_remote_copy(
            src_ref=send.at[to],
            dst_ref=recv.at[me],
            send_sem=s_send.at[to],
            recv_sem=s_recv.at[me],
            device_id=device(z, to),
            device_id_type=MESH,
        )

    def bins_wait(source):
        return pltpu.make_async_remote_copy(
            src_ref=send.at[source],
            dst_ref=recv.at[source],
            send_sem=s_send.at[source],
            recv_sem=s_recv.at[source],
            device_id=device(z, source),
            device_id_type=MESH,
        )

    kept_here = pltpu.make_async_copy(send.at[me], recv.at[me], own_sem.at[0])

    def launch(to):
        @pl.when(to != me)
        def _():
            bins_copy(to).start()

        @pl.when(to == me)
        def _():
            kept_here.start()

    def one_store(j, carry):
        f = (me // 2 + j) % RADIX
        value = kept[f] * factor
        top, bottom = value[:64], value[64:]
        send[2 * f] = jnp.where(left, top, pltpu.roll(bottom, 64, 1)).astype(BF16)
        send[2 * f + 1] = jnp.where(left, pltpu.roll(top, 64, 1), bottom).astype(BF16)
        launch(2 * f)
        launch(2 * f + 1)
        return carry

    lax.fori_loop(0, RADIX, one_store, 0)
    kept_here.wait()

    def one_block(j, carry):
        v = (my_v + j) % WIN
        for q in range(QUAD):
            source = v * QUAD + q

            @pl.when(source != me)
            def _():
                bins_wait(source).wait_recv()

        for w in range(2):
            parts = [
                recv[v * QUAD + q, (p * 2 + w) * 16 : (p * 2 + w + 1) * 16, :] for p in range(2) for q in range(QUAD)
            ]
            block = jnp.concatenate([part.astype(F32) for part in parts], 0).T
            for h in range(4):
                start = pl.multiple_of(((v * 2 + w) * 4 + h) * REL_PITCH, 8)
                turned[pl.ds(start, 32), :] = block[h * 32 : (h + 1) * 32]
        return carry

    lax.fori_loop(0, WIN, one_block, 0)

    def halo_copy(way, chunk):
        span = pl.ds(chunk * CHUNK, CHUNK)
        return pltpu.make_async_remote_copy(
            src_ref=own.at[span],
            dst_ref=halo.at[way, span],
            send_sem=h_send.at[way, chunk],
            recv_sem=h_recv.at[way, chunk],
            device_id=device((z + (planes - 1 if way == 0 else 1)) % planes, me),
            device_id_type=MESH,
        )

    def gather(chunk, carry):
        for j in range(CHUNK):
            g = chunk * CHUNK + j
            real = turned[pl.ds(g, 32, stride=2 * REL_PITCH), :]
            imag = turned[pl.ds(REL_PITCH + g, 32, stride=2 * REL_PITCH), :]
            own[g] = jnp.concatenate([real, imag], 0).astype(BF16)
        halo_copy(0, chunk).start()
        halo_copy(1, chunk).start()
        return carry

    lax.fori_loop(0, BINS // CHUNK, gather, 0)

    def operand(x, rx):
        y = jnp.concatenate([x[32:], -x[:32]], 0)
        ry = jnp.concatenate([rx[32:], -rx[:32]], 0)
        return jnp.concatenate([jnp.where(left, x, ry), jnp.where(left, rx, y)], 0).T.astype(BF16)

    def cross(chunk, carry):
        halo_copy(0, chunk).wait_recv()
        halo_copy(1, chunk).wait_recv()
        for j in range(CHUNK):
            g = chunk * CHUNK + j
            a = own[g].astype(F32)
            e = jnp.where(z + 1 < planes, halo[0, g].astype(F32), 0.0)
            m = jnp.where(z > 0, halo[1, g].astype(F32), 0.0)
            ra, re, rm = (pltpu.roll(x, 64, 1) for x in (a, e, m))
            right = jnp.concatenate([jnp.where(left, a, re), jnp.where(left, ra, e)], 0).astype(BF16)
            last = jnp.concatenate([e, re], 0).astype(BF16)
            for ref, value in (
                (near, jnp.dot(operand(a, ra), right, preferred_element_type=F32)),
                (far, jnp.dot(operand(m, rm), last, preferred_element_type=F32)),
            ):
                for part in range(2):
                    start = pl.multiple_of((g * 2 + part) * OUT_PITCH, 8)
                    ref[pl.ds(start, 64), :] = value[part * 64 : (part + 1) * 64]
        return carry

    lax.fori_loop(0, BINS // CHUNK, cross, 0)

    def offsets_copy(kind, to):
        return pltpu.make_async_remote_copy(
            src_ref=(send_near, send_far)[kind].at[to],
            dst_ref=(got_near, got_far)[kind].at[me],
            send_sem=x_send.at[kind, to],
            recv_sem=x_recv.at[kind, me],
            device_id=device(z if kind == 0 else (z + planes - 1) % planes, to),
            device_id_type=MESH,
        )

    def offsets_wait(kind, source):
        return pltpu.make_async_remote_copy(
            src_ref=(send_near, send_far)[kind].at[source],
            dst_ref=(got_near, got_far)[kind].at[source],
            send_sem=x_send.at[kind, source],
            recv_sem=x_recv.at[kind, source],
            device_id=device(z if kind == 0 else (z + 1) % planes, source),
            device_id_type=MESH,
        )

    kept_near = pltpu.make_async_copy(send_near.at[me], got_near.at[me], own_sem.at[1])
    wide = lax.broadcasted_iota(jnp.int32, (128, 128), 1) < 64

    def one_quarter(j, carry):
        q = (my_q + j) % QUAD

        def one_pair(i, carry):
            c = q * 16 + i
            slot = i
            for ref, column, base, size, target in (
                (near, near_col, 0, 128, send_near), (far, far_col, 128, 64, send_far)
            ):
                block = jnp.concatenate(
                    [ref[pl.ds(c, 64, stride=OUT_PITCH), :], ref[pl.ds(c + 8, 64, stride=OUT_PITCH), :]], 0
                )
                column[slot, base : base + size, :] = block.T[:size]
                value = jnp.where(
                    wide, column[slot, pl.ds(c + 1, 128), :], column[slot, pl.ds(c + 9, 128), :]
                ).astype(BF16)
                rows = pl.ds(pl.multiple_of(i * 16, 16), 16)
                for v in range(WIN):
                    target[v * QUAD + q, rows, :] = value[v * 16 : (v + 1) * 16]
            return carry

        lax.fori_loop(0, 8, one_pair, 0, unroll=4)

        def one_send(k, carry):
            v = (my_v + k) % WIN
            to = v * QUAD + q

            @pl.when((v + q < WIN) & (to != me))
            def _():
                offsets_copy(0, to).start()

            @pl.when((v + q < WIN) & (to == me))
            def _():
                kept_near.start()

            @pl.when(v + q >= WIN - 1)
            def _():
                offsets_copy(1, to).start()

            return carry

        lax.fori_loop(0, WIN, one_send, 0)
        return carry

    lax.fori_loop(0, QUAD, one_quarter, 0)

    @pl.when(my_v + my_q < WIN)
    def _():
        def one(j, carry):
            offsets_wait(0, (me + j) % PLANE).wait_recv()
            return carry

        lax.fori_loop(1, PLANE, one, 0)
        kept_near.wait()

    @pl.when(my_v + my_q >= WIN - 1)
    def _():
        def one(source, carry):
            offsets_wait(1, source).wait_recv()
            return carry

        lax.fori_loop(0, PLANE, one, 0)

    def drain(to, carry):
        q, v = to % QUAD, to // QUAD

        @pl.when(to != me)
        def _():
            bins_copy(to).wait_send()

        @pl.when((v + q < WIN) & (to != me))
        def _():
            offsets_copy(0, to).wait_send()

        @pl.when(v + q >= WIN - 1)
        def _():
            offsets_copy(1, to).wait_send()

        return carry

    lax.fori_loop(0, PLANE, drain, 0)

    def drain_halo(chunk, carry):
        halo_copy(0, chunk).wait_send()
        halo_copy(1, chunk).wait_send()
        return carry

    lax.fori_loop(0, BINS // CHUNK, drain_halo, 0)


def cross_spectra(raw, offsets, mask, planes):
    w_hi, w_lo = (jnp.asarray(x) for x in second_stage())
    tw_cos, tw_sin = (jnp.asarray(x) for x in twiddles())
    vmem = pl.BlockSpec(memory_space=pltpu.VMEM)
    smem = pl.BlockSpec(memory_space=pltpu.SMEM)
    anywhere = pl.BlockSpec(memory_space=pltpu.HBM)
    packet = jax.ShapeDtypeStruct((PLANE, 128, 128), BF16)
    dma = pltpu.SemaphoreType.DMA
    return pl.pallas_call(
        functools.partial(main_kernel, planes),
        out_shape=[packet, packet],
        in_specs=[smem, smem] + [anywhere] * 5,
        out_specs=[vmem, vmem],
        scratch_shapes=[
            pltpu.VMEM(raw.shape, BF16),
            pltpu.VMEM(tw_cos.shape, F32),
            pltpu.VMEM(tw_sin.shape, F32),
            pltpu.VMEM(w_hi.shape, BF16),
            pltpu.VMEM(w_lo.shape, BF16),
            pltpu.VMEM((RADIX, 128, 4 * TAIL), BF16),
            pltpu.VMEM((RADIX, 128, 128), F32),
            pltpu.VMEM((8, RADIX, 128), F32),
            pltpu.VMEM((8, RADIX, 128), F32),
            pltpu.VMEM((PLANE, 64, 128), BF16),
            pltpu.VMEM((PLANE, 64, 128), BF16),
            pltpu.VMEM((64 * REL_PITCH, 128), F32),
            pltpu.VMEM((BINS, 64, 128), BF16),
            pltpu.VMEM((2, BINS, 64, 128), BF16),
            pltpu.VMEM((2 * BINS * OUT_PITCH, 128), F32),
            pltpu.VMEM((2 * BINS * OUT_PITCH, 128), F32),
            pltpu.VMEM((SLOTS, 256, 128), F32),
            pltpu.VMEM((SLOTS, 256, 128), F32),
            pltpu.VMEM((PLANE, 128, 128), BF16),
            pltpu.VMEM((PLANE, 128, 128), BF16),
            dma((5,)),
            dma((2,)),
            dma((PLANE,)),
            dma((PLANE,)),
            dma((2, BINS // CHUNK)),
            dma((2, BINS // CHUNK)),
            dma((2, PLANE)),
            dma((2, PLANE)),
        ],
        compiler_params=pltpu.CompilerParams(
            collective_id=0, has_side_effects=True, vmem_limit_bytes=40 * 2**20
        ),
        name="main",
    )(*(pltpu.with_memory_space_constraint(x, pltpu.HBM) for x in (offsets, mask, raw, tw_cos, tw_sin, w_hi, w_lo)))


def lag_kernel(scale, near, far, table, out, lhs):
    _, me = place()
    reach = me % QUAD + me // QUAD
    left = lax.broadcasted_iota(jnp.int32, (128, 128), 1) < 64

    def packet(s):
        return jnp.where(reach < WIN, near[s].astype(F32), 0.0) + jnp.where(
            reach >= WIN - 1, far[s].astype(F32), 0.0
        )

    for f in range(RADIX):
        one, two = packet(2 * f), packet(2 * f + 1)
        lhs[:128, f * 128 : (f + 1) * 128] = jnp.where(left, one, pltpu.roll(two, 64, 1)).astype(BF16)
        lhs[128:, f * 128 : (f + 1) * 128] = jnp.where(left, pltpu.roll(one, 64, 1), two).astype(BF16)
    for part in range(LAGS // 128):
        span = slice(part * 128, (part + 1) * 128)
        lags = jnp.dot(lhs[...], table[:, span], preferred_element_type=F32) * scale
        for c in range(16):
            out[:, c, span] = lags[c * 16 : (c + 1) * 16]


def lag_transform(near, far, scale):
    vmem = pl.BlockSpec(memory_space=pltpu.VMEM)
    return pl.pallas_call(
        functools.partial(lag_kernel, scale),
        out_shape=jax.ShapeDtypeStruct((16, 16, LAGS), F32),
        in_specs=[vmem, vmem, vmem],
        out_specs=vmem,
        scratch_shapes=[pltpu.VMEM((256, 2 * NB), BF16)],
        compiler_params=pltpu.CompilerParams(vmem_limit_bytes=24 * 2**20),
        name="lags",
    )(near, far, lag_rows())


def body(planes, raw, offsets, mask):
    near, far = cross_spectra(raw, offsets, mask, planes)
    return lag_transform(near, far, 1.0 / math.sqrt(NB * 8 * WIN))


def solution(mesh):
    planes = mesh.shape["fibre"] // QUAD
    return jax.shard_map(
        functools.partial(body, planes),
        mesh=mesh,
        in_specs=(P("win", "fibre", None), P("win"), P("fibre")),
        out_specs=P("win", "fibre", None),
        check_vma=False,
    )
```

```python
import functools
import math

import jax
import jax.numpy as jnp
import numpy as np
from jax import lax
from jax.experimental import pallas as pl
from jax.experimental.pallas import tpu as pltpu
from jax.sharding import PartitionSpec as P

MESH = pl.DeviceIdType.MESH
L = 4096
BAND_LO = 64
NB = 1024
SMOOTH = 64
LAGS = 512
SPAN = 128
EPS = 1e-06
RADIX = 16
TAIL = L // RADIX
PLANE = 32
WIN = 8
QUAD = 4
BINS = 32
CHUNK = 8
REL_PITCH = 40
OUT_PITCH = 72
SLOTS = 8
HALVES = 2
ROWS = 128 // HALVES
CHUNKS = BINS // CHUNK
GROUP = 8
F32 = jnp.float32
BF16 = jnp.bfloat16


def second_stage():
    b = np.arange(TAIL)[:, None]
    lane = np.arange(128)[None, :]
    half, imag, low = lane // 64, (lane // 32) % 2, lane % 32
    angle = 2.0 * np.pi * ((b * (BAND_LO // RADIX + half * 32 + low)) % TAIL) / TAIL
    cos, sin = np.cos(angle), np.sin(angle)
    real = np.concatenate([cos, sin], 0)
    imaginary = np.concatenate([-sin, cos], 0)
    straight = np.where(imag == 0, real, imaginary)
    turned = np.where(imag == 0, -imaginary, real)
    whole = np.concatenate([straight, turned], 1).astype(np.float32)
    high = whole.astype(jnp.bfloat16)
    low_part = (whole - high.astype(np.float32)).astype(jnp.bfloat16)
    return high, low_part


def twiddles():
    f = np.arange(RADIX)[:, None]
    b = np.arange(TAIL)[None, :]
    angle = 2.0 * np.pi * (f * b) / L
    return np.cos(angle).astype(np.float32), np.sin(angle).astype(np.float32)


def lag_rows():
    frequency = np.arange(NB, dtype=np.int64) + BAND_LO
    lag_index = np.arange(LAGS, dtype=np.int64) - LAGS // 2
    turns = np.mod(frequency[:, None] * lag_index[None, :], L).astype(np.float32)
    angles = turns * np.float32(2.0 * math.pi / L)
    cos, sin = np.cos(angles.astype(np.float64)), np.sin(angles.astype(np.float64))
    table = np.stack([cos, -sin], 1).astype(np.float32)
    bins = RADIX * np.arange(64)[None, :] + np.arange(RADIX)[:, None]
    return table[bins].reshape(2 * NB, LAGS).astype(jnp.bfloat16)


def real_fft(x):
    n = len(x)
    if n == 2:
        return [(x[0] + x[1], None), (x[0] - x[1], None)]
    even, odd = real_fft(x[0::2]), real_fft(x[1::2])
    half, quarter = n // 2, n // 4
    out = [None] * (half + 1)
    out[0] = (even[0][0] + odd[0][0], None)
    out[half] = (even[0][0] - odd[0][0], None)
    for k in range(1, quarter):
        (er, ei), (orr, oi) = even[k], odd[k]
        c, s = math.cos(2.0 * math.pi * k / n), math.sin(2.0 * math.pi * k / n)
        if 8 * k == n:
            tr, ti = (orr + oi) * c, (oi - orr) * c
        else:
            tr, ti = orr * c + oi * s, oi * c - orr * s
        out[k] = (er + tr, ei + ti)
        out[half - k] = (er - tr, ti - ei)
    out[quarter] = (even[quarter][0], -odd[quarter][0])
    return out


def place():
    fibre, win = lax.axis_index("fibre"), lax.axis_index("win")
    return fibre // QUAD, win * QUAD + fibre % QUAD


def device(z, s):
    return (z * QUAD + s % QUAD, s // QUAD)


def greet_all(planes, z, me):
    barrier = pltpu.get_barrier_semaphore()

    def signal(plane, s):
        pl.semaphore_signal(barrier, inc=1, device_id=device(plane, s), device_id_type=MESH)

    def near(j, carry):
        signal(z, (me + j) % PLANE)
        return carry

    lax.fori_loop(1, PLANE, near, 0)
    signal((z + 1) % planes, me)
    signal((z + planes - 1) % planes, me)
    return PLANE - 1 + 2


def first_stage(half, offsets, raw, tw_cos, tw_sin, lhs, phase_cos, phase_sin):
    width = 128

    def one_window(i, carry):
        w = (i // 2) * 4 + half * 2 + i % 2
        off = offsets[w]
        u = lax.broadcasted_iota(jnp.int32, (RADIX, TAIL), 0) * TAIL + lax.broadcasted_iota(
            jnp.int32, (RADIX, TAIL), 1
        )
        taper = 0.5 - 0.5 * jnp.cos(((u - off) & (L - 1)).astype(F32) * (2.0 * math.pi / L))
        f = lax.broadcasted_iota(jnp.int32, (RADIX, 128), 0)
        lane = lax.broadcasted_iota(jnp.int32, (RADIX, 128), 1)
        k = (BAND_LO // RADIX + (lane // 64) * 32 + lane % 32) * RADIX + f
        angle = ((k * off) & (L - 1)).astype(F32) * (2.0 * math.pi / L)
        phase_cos[i] = jnp.cos(angle)
        phase_sin[i] = jnp.sin(angle)

        def tiles_of(low, size):
            wrapped = lax.broadcasted_iota(jnp.int32, (16, size), 1) + low < off
            first = jnp.where(
                wrapped, raw[w, :, L + low : L + low + size].astype(F32), raw[w, :, low : low + size].astype(F32)
            )
            return [first] + [
                raw[w, :, a * TAIL + low : a * TAIL + low + size].astype(F32) for a in range(1, RADIX)
            ]

        total = functools.reduce(lambda p, q: p + q, tiles_of(0, TAIL))
        mean = jnp.sum(total, axis=1, keepdims=True) * (1.0 / L)
        rows = pl.ds(pl.multiple_of(i * 16, 16), 16)
        for low in range(0, TAIL, width):
            span = slice(low, low + width)
            spectrum = real_fft([(x - mean) * taper[a : a + 1, span] for a, x in enumerate(tiles_of(low, width))])
            for f in range(RADIX):
                re, im = spectrum[f] if f <= RADIX // 2 else spectrum[RADIX - f]
                if f > RADIX // 2:
                    im = -im
                if f:
                    c, s = tw_cos[f : f + 1, span], tw_sin[f : f + 1, span]
                    re, im = (re * c, -re * s) if im is None else (re * c + im * s, im * c - re * s)
                else:
                    im = jnp.zeros_like(re)
                for part, value in enumerate((re, im)):
                    high = value.astype(BF16)
                    start = part * TAIL + low
                    lhs[f, rows, start : start + width] = high
                    start += 2 * TAIL
                    lhs[f, rows, start : start + width] = (value - high.astype(F32)).astype(BF16)
        return carry

    lax.fori_loop(0, ROWS // 16, one_window, 0)


def second_stage_of(lhs, w_hi, w_lo, kept, phase_cos, phase_sin):
    def some_columns(index, power):
        start = index * GROUP
        whole = lhs[pl.ds(start, GROUP)].reshape(GROUP * ROWS, 4 * TAIL)
        both = jnp.dot(whole, w_hi[...], preferred_element_type=F32) + jnp.dot(
            whole[:, : 2 * TAIL], w_lo[...], preferred_element_type=F32
        )
        for j in range(GROUP):
            c = phase_cos[:, pl.ds(start + j, 1), :]
            s = phase_sin[:, pl.ds(start + j, 1), :]
            one = both[j * ROWS : (j + 1) * ROWS].reshape(ROWS // 16, 16, 256)
            value = (one[:, :, :128] * c + one[:, :, 128:] * s).reshape(ROWS, 128)
            kept[start + j] = value
            power = power + value * value
        return power

    return lax.fori_loop(0, RADIX // GROUP, some_columns, jnp.zeros((ROWS, 128), F32))


def whitening(power, mask):
    row = lax.broadcasted_iota(jnp.int32, (128, 128), 0)
    col = lax.broadcasted_iota(jnp.int32, (128, 128), 1)
    same = (row // 64 == col // 64) & ((row % 32) // 4 == (col % 32) // 4)
    block = jnp.where(same, 1.0, 0.0).astype(F32)
    mean_power = jnp.dot(power, block, precision=lax.Precision.HIGHEST, preferred_element_type=F32) * (1.0 / SMOOTH)
    channel = lax.broadcasted_iota(jnp.int32, (16, 128), 0)
    flag = jnp.zeros((16, 128), F32)
    for c in range(16):
        flag = jnp.where(channel == c, mask[c].astype(F32), flag)
    flag = jnp.broadcast_to(flag[None], (ROWS // 16, 16, 128)).reshape(ROWS, 128)
    return (1.0 / jnp.sqrt(mean_power + EPS)) * flag


def main_kernel(
    planes, scale, offsets, mask, raw_hbm, cos_hbm, sin_hbm, hi_hbm, lo_hbm, table_hbm, out,
    raw, tw_cos, tw_sin, w_hi, w_lo, table, lhs, kept, phase_cos, phase_sin,
    send, recv, turned, own, halo, near, far, near_col, far_col, send_near, send_far, got_far, got, lag_lhs,
    in_sem, own_sem, s_send, s_recv, h_send, h_recv, x_send, x_recv, f_send, f_recv,
):
    z, me = place()
    my_q, my_v = me % QUAD, me // QUAD
    above, below = (z + 1) % planes, (z + planes - 1) % planes
    loads = [
        pltpu.make_async_copy(source, target, in_sem.at[i])
        for i, (source, target) in enumerate(
            (
                (raw_hbm, raw),
                (cos_hbm, tw_cos),
                (sin_hbm, tw_sin),
                (hi_hbm, w_hi),
                (lo_hbm, w_lo),
                (table_hbm, table),
            )
        )
    ]
    for load in loads:
        load.start()
    expected = greet_all(planes, z, me)
    for slot in range(SLOTS):
        near_col[slot, 128:, :] = jnp.zeros((128, 128), F32)
        far_col[slot, :128, :] = jnp.zeros((128, 128), F32)
    for load in loads[:3]:
        load.wait()
    left = lax.broadcasted_iota(jnp.int32, (64, 128), 1) < 64

    def bins_copy(half, to, source):
        return pltpu.make_async_remote_copy(
            src_ref=send.at[half, to],
            dst_ref=recv.at[half, source],
            send_sem=s_send.at[half, to],
            recv_sem=s_recv.at[half, source],
            device_id=device(z, to),
            device_id_type=MESH,
        )

    def own_copy(half):
        return pltpu.make_async_copy(send.at[half, me], recv.at[half, me], own_sem.at[half])

    for half in range(HALVES):
        first_stage(half, offsets, raw, tw_cos, tw_sin, lhs, phase_cos, phase_sin)
        if half == 0:
            for load in loads[3:5]:
                load.wait()
        factor = whitening(second_stage_of(lhs, w_hi, w_lo, kept, phase_cos, phase_sin), mask)
        if half == 0:
            pl.semaphore_wait(pltpu.get_barrier_semaphore(), expected)

        def launch(to, half=half):
            @pl.when(to != me)
            def _():
                bins_copy(half, to, me).start()

            @pl.when(to == me)
            def _():
                own_copy(half).start()

        def one_store(j, carry, half=half, factor=factor, launch=launch):
            for k in range(2):
                f = (me // 2 + 2 * j + k) % RADIX
                value = kept[f] * factor
                top, bottom = value[:32], value[32:]
                send[half, 2 * f] = jnp.where(left[:32], top, pltpu.roll(bottom, 64, 1)).astype(BF16)
                send[half, 2 * f + 1] = jnp.where(left[:32], pltpu.roll(top, 64, 1), bottom).astype(BF16)
                launch(2 * f)
                launch(2 * f + 1)
            return carry

        lax.fori_loop(0, RADIX // 2, one_store, 0)

    def halo_copy(way, half, chunk):
        span = pl.ds(chunk * CHUNK, CHUNK)
        return pltpu.make_async_remote_copy(
            src_ref=own.at[half, span],
            dst_ref=halo.at[way, half, span],
            send_sem=h_send.at[way, half, chunk],
            recv_sem=h_recv.at[way, half, chunk],
            device_id=device(below if way == 0 else above, me),
            device_id_type=MESH,
        )

    for half in range(HALVES):
        own_copy(half).wait()

        def one_block(j, carry, half=half):
            v = (my_v + j) % WIN
            for q in range(QUAD):
                source = v * QUAD + q

                @pl.when(source != me)
                def _():
                    bins_copy(half, source, source).wait_recv()

            parts = [recv[half, v * QUAD + q, p * 16 : (p + 1) * 16, :] for p in range(2) for q in range(QUAD)]
            block = jnp.concatenate([part.astype(F32) for part in parts], 0).T
            for h in range(4):
                wh, ri = h // 2, h % 2
                start = pl.multiple_of(((half * 2 + ri) * 16 + v * 2 + wh) * REL_PITCH, 8)
                turned[pl.ds(start, 32), :] = block[h * 32 : (h + 1) * 32]
            return carry

        lax.fori_loop(0, WIN, one_block, 0)

        def gather(chunk, carry, half=half):
            for j in range(CHUNK):
                g = chunk * CHUNK + j
                real = turned[pl.ds(half * 32 * REL_PITCH + g, 16, stride=REL_PITCH), :]
                imag = turned[pl.ds((half * 32 + 16) * REL_PITCH + g, 16, stride=REL_PITCH), :]
                own[half, g] = jnp.concatenate([real, imag], 0).astype(BF16)
            halo_copy(0, half, chunk).start()
            halo_copy(1, half, chunk).start()
            return carry

        lax.fori_loop(0, CHUNKS, gather, 0)

    def operand(x, rx):
        def turn(u):
            return jnp.concatenate([u[16:32], -u[:16], u[48:], -u[32:48]], 0)

        return jnp.concatenate([jnp.where(left, x, turn(rx)), jnp.where(left, rx, turn(x))], 0).T.astype(BF16)

    def cross(chunk, carry):
        for way in range(2):
            for half in range(HALVES):
                halo_copy(way, half, chunk).wait_recv()
        for j in range(CHUNK):
            g = chunk * CHUNK + j
            a = jnp.concatenate([own[half, g].astype(F32) for half in range(HALVES)], 0)
            e = jnp.concatenate([halo[0, half, g].astype(F32) for half in range(HALVES)], 0)
            m = jnp.concatenate([halo[1, half, g].astype(F32) for half in range(HALVES)], 0)
            e = jnp.where(z + 1 < planes, e, 0.0)
            m = jnp.where(z > 0, m, 0.0)
            ra, re, rm = (pltpu.roll(x, 64, 1) for x in (a, e, m))
            right = jnp.concatenate([jnp.where(left, a, re), jnp.where(left, ra, e)], 0).astype(BF16)
            last = jnp.concatenate([e, re], 0).astype(BF16)
            for ref, value in (
                (near, jnp.dot(operand(a, ra), right, preferred_element_type=F32)),
                (far, jnp.dot(operand(m, rm), last, preferred_element_type=F32)),
            ):
                for part in range(2):
                    start = pl.multiple_of((g * 2 + part) * OUT_PITCH, 8)
                    ref[pl.ds(start, 64), :] = value[part * 64 : (part + 1) * 64]
        return carry

    lax.fori_loop(0, CHUNKS, cross, 0)

    def far_copy(to):
        return pltpu.make_async_remote_copy(
            src_ref=send_far.at[to],
            dst_ref=got_far.at[to],
            send_sem=f_send.at[to],
            recv_sem=f_recv.at[to],
            device_id=device(below, me),
            device_id_type=MESH,
        )

    def offsets_copy(ref, to, source):
        return pltpu.make_async_remote_copy(
            src_ref=ref.at[to],
            dst_ref=got.at[source],
            send_sem=x_send.at[to],
            recv_sem=x_recv.at[source],
            device_id=device(z, to),
            device_id_type=MESH,
        )

    def own_packet(ref):
        return pltpu.make_async_copy(ref.at[me], got.at[me], own_sem.at[HALVES])

    def ship(ref, to):
        @pl.when(to != me)
        def _():
            offsets_copy(ref, to, me).start()

        @pl.when(to == me)
        def _():
            own_packet(ref).start()

    wide = lax.broadcasted_iota(jnp.int32, (128, 128), 1) < 64

    def one_quarter(j, carry):
        q = (my_q + j) % QUAD

        def one_pair(i, carry):
            c = q * 16 + i
            for ref, column, base, size, target in (
                (near, near_col, 0, 128, send_near), (far, far_col, 128, 64, send_far)
            ):
                block = jnp.concatenate(
                    [ref[pl.ds(c, 64, stride=OUT_PITCH), :], ref[pl.ds(c + 8, 64, stride=OUT_PITCH), :]], 0
                )
                column[i, base : base + size, :] = block.T[:size]
                value = jnp.where(
                    wide, column[i, pl.ds(c + 1, 128), :], column[i, pl.ds(c + 9, 128), :]
                ).astype(BF16)
                rows = pl.ds(pl.multiple_of(i * 16, 16), 16)
                for v in range(WIN):
                    target[v * QUAD + q, rows, :] = value[v * 16 : (v + 1) * 16]
            return carry

        lax.fori_loop(0, 8, one_pair, 0, unroll=4)

        def one_send(k, carry):
            v = (my_v + k) % WIN
            to = v * QUAD + q

            @pl.when(v + q >= WIN - 1)
            def _():
                far_copy(to).start()

            @pl.when(v + q < WIN - 1)
            def _():
                ship(send_near, to)

            return carry

        lax.fori_loop(0, WIN, one_send, 0)
        return carry

    lax.fori_loop(0, QUAD, one_quarter, 0)

    def late_quarter(j, carry):
        q = (my_q + j) % QUAD

        def one_send(k, carry):
            v = (my_v + k) % WIN
            to = v * QUAD + q

            @pl.when(v + q >= WIN - 1)
            def _():
                far_copy(to).wait_recv()

            @pl.when(v + q == WIN - 1)
            def _():
                send_near[to] = (send_near[to].astype(F32) + got_far[to].astype(F32)).astype(BF16)
                ship(send_near, to)

            @pl.when(v + q >= WIN)
            def _():
                ship(got_far, to)

            return carry

        lax.fori_loop(0, WIN, one_send, 0)
        return carry

    lax.fori_loop(0, QUAD, late_quarter, 0)

    loads[5].wait()
    own_packet(send_near).wait()

    def arrived(j, carry):
        source = (me + j) % PLANE
        offsets_copy(send_near, source, source).wait_recv()
        return carry

    lax.fori_loop(1, PLANE, arrived, 0)

    def one_pair(f, carry):
        one, two = got[2 * f].astype(F32), got[2 * f + 1].astype(F32)
        span = pl.ds(pl.multiple_of(f * 128, 128), 128)
        lag_lhs[:128, span] = jnp.where(wide, one, pltpu.roll(two, 64, 1)).astype(BF16)
        lag_lhs[128:, span] = jnp.where(wide, pltpu.roll(one, 64, 1), two).astype(BF16)
        return carry

    lax.fori_loop(0, RADIX, one_pair, 0, unroll=8)
    for part in range(LAGS // 256):
        span = slice(part * 256, (part + 1) * 256)
        lags = jnp.dot(lag_lhs[...], table[:, span], preferred_element_type=F32) * scale
        for c in range(16):
            out[:, c, span] = lags[c * 16 : (c + 1) * 16]

    def drain(to, carry):
        @pl.when(to != me)
        def _():
            for half in range(HALVES):
                bins_copy(half, to, me).wait_send()
            offsets_copy(send_near, to, me).wait_send()

        @pl.when(to % QUAD + to // QUAD >= WIN - 1)
        def _():
            far_copy(to).wait_send()

        return carry

    lax.fori_loop(0, PLANE, drain, 0)

    def drain_halo(chunk, carry):
        for way in range(2):
            for half in range(HALVES):
                halo_copy(way, half, chunk).wait_send()
        return carry

    lax.fori_loop(0, CHUNKS, drain_halo, 0)


def body(planes, raw, offsets, mask):
    w_hi, w_lo = second_stage()
    tw_cos, tw_sin = twiddles()
    operands = [offsets, mask, raw, tw_cos, tw_sin, np.concatenate([w_hi, w_hi], 0), w_lo, lag_rows()]
    smem = pl.BlockSpec(memory_space=pltpu.SMEM)
    far_away = pl.BlockSpec(memory_space=pltpu.HBM)
    dma = pltpu.SemaphoreType.DMA
    vmem = pltpu.VMEM
    packets = vmem((PLANE, 128, 128), BF16)
    spectra = vmem((2 * BINS * OUT_PITCH, 128), F32)
    return pl.pallas_call(
        functools.partial(main_kernel, planes, 1.0 / math.sqrt(NB * 8 * WIN)),
        out_shape=jax.ShapeDtypeStruct((16, 16, LAGS), F32),
        in_specs=[smem, smem] + [far_away] * 6,
        out_specs=pl.BlockSpec(memory_space=pltpu.VMEM),
        scratch_shapes=[vmem(x.shape, x.dtype) for x in operands[2:]]
        + [
            vmem((RADIX, ROWS, 4 * TAIL), BF16),
            vmem((RADIX, ROWS, 128), F32),
            vmem((ROWS // 16, RADIX, 128), F32),
            vmem((ROWS // 16, RADIX, 128), F32),
            vmem((HALVES, PLANE, 32, 128), BF16),
            vmem((HALVES, PLANE, 32, 128), BF16),
            vmem((64 * REL_PITCH, 128), F32),
            vmem((HALVES, BINS, 32, 128), BF16),
            vmem((2, HALVES, BINS, 32, 128), BF16),
            spectra,
            spectra,
            vmem((SLOTS, 256, 128), F32),
            vmem((SLOTS, 256, 128), F32),
            packets,
            packets,
            packets,
            packets,
            vmem((256, 2 * NB), BF16),
            dma((6,)),
            dma((HALVES + 1,)),
            dma((HALVES, PLANE)),
            dma((HALVES, PLANE)),
            dma((2, HALVES, CHUNKS)),
            dma((2, HALVES, CHUNKS)),
            dma((PLANE,)),
            dma((PLANE,)),
            dma((PLANE,)),
            dma((PLANE,)),
        ],
        compiler_params=pltpu.CompilerParams(
            collective_id=0, has_side_effects=True, vmem_limit_bytes=48 * 2**20
        ),
        name="main",
    )(*(pltpu.with_memory_space_constraint(jnp.asarray(x), pltpu.HBM) for x in operands))


def solution(mesh):
    planes = mesh.shape["fibre"] // QUAD
    return jax.shard_map(
        functools.partial(body, planes),
        mesh=mesh,
        in_specs=(P("win", "fibre", None), P("win"), P("fibre")),
        out_specs=P("win", "fibre", None),
        check_vma=False,
    )
```

```python
import functools
import math

import jax
import jax.numpy as jnp
import numpy as np
from jax import lax
from jax.experimental import pallas as pl
from jax.experimental.pallas import tpu as pltpu
from jax.sharding import PartitionSpec as P

MESH = pl.DeviceIdType.MESH
L = 4096
BAND_LO = 64
NB = 1024
SMOOTH = 64
LAGS = 512
SPAN = 128
EPS = 1e-06
RADIX = 16
TAIL = L // RADIX
PLANE = 32
WIN = 8
QUAD = 4
BINS = 32
CHUNK = 8
REL_PITCH = 40
OUT_PITCH = 72
SLOTS = 8
HALVES = 2
ROWS = 128 // HALVES
CHUNKS = BINS // CHUNK
MEAN_UNROLL = 4
FFT_UNROLL = 2
GROUP = 16
F32 = jnp.float32
BF16 = jnp.bfloat16


def second_stage():
    b = np.arange(TAIL)[:, None]
    lane = np.arange(128)[None, :]
    half, imag, low = lane // 64, (lane // 32) % 2, lane % 32
    angle = 2.0 * np.pi * ((b * (BAND_LO // RADIX + half * 32 + low)) % TAIL) / TAIL
    cos, sin = np.cos(angle), np.sin(angle)
    whole = np.where(imag == 0, np.concatenate([cos, sin], 0), np.concatenate([-sin, cos], 0)).astype(np.float32)
    high = whole.astype(jnp.bfloat16)
    return np.concatenate([high, (whole - high.astype(np.float32)).astype(jnp.bfloat16)], 1)


def first_tables():
    f = np.arange(RADIX)[:, None]
    b = np.arange(TAIL)[None, :]
    twiddle, spot = 2.0 * np.pi * (f * b) / L, 2.0 * np.pi * (TAIL * f + b) / L
    return np.stack([np.cos(twiddle), np.sin(twiddle), np.cos(spot), np.sin(spot)]).astype(np.float32)


def lag_rows():
    frequency = np.arange(NB, dtype=np.int64) + BAND_LO
    lag_index = np.arange(LAGS, dtype=np.int64) - LAGS // 2
    turns = np.mod(frequency[:, None] * lag_index[None, :], L).astype(np.float32)
    angles = turns * np.float32(2.0 * math.pi / L)
    cos, sin = np.cos(angles.astype(np.float64)), np.sin(angles.astype(np.float64))
    table = np.stack([cos, -sin], 1).astype(np.float32)
    bins = RADIX * np.arange(64)[None, :] + np.arange(RADIX)[:, None]
    return table[bins].reshape(2 * NB, LAGS).astype(jnp.bfloat16)


def real_fft(x):
    n = len(x)
    if n == 2:
        return [(x[0] + x[1], None), (x[0] - x[1], None)]
    even, odd = real_fft(x[0::2]), real_fft(x[1::2])
    half, quarter = n // 2, n // 4
    out = [None] * (half + 1)
    out[0] = (even[0][0] + odd[0][0], None)
    out[half] = (even[0][0] - odd[0][0], None)
    for k in range(1, quarter):
        (er, ei), (orr, oi) = even[k], odd[k]
        c, s = math.cos(2.0 * math.pi * k / n), math.sin(2.0 * math.pi * k / n)
        if 8 * k == n:
            tr, ti = (orr + oi) * c, (oi - orr) * c
        else:
            tr, ti = orr * c + oi * s, oi * c - orr * s
        out[k] = (er + tr, ei + ti)
        out[half - k] = (er - tr, ti - ei)
    out[quarter] = (even[quarter][0], -odd[quarter][0])
    return out


def place():
    fibre, win = lax.axis_index("fibre"), lax.axis_index("win")
    return fibre // QUAD, win * QUAD + fibre % QUAD


def device(z, s):
    return (z * QUAD + s % QUAD, s // QUAD)


def greet_all(planes, z, me):
    barrier = pltpu.get_barrier_semaphore()

    def signal(plane, s):
        pl.semaphore_signal(barrier, inc=1, device_id=device(plane, s), device_id_type=MESH)

    def near(j, carry):
        signal(z, (me + j) % PLANE)
        return carry

    lax.fori_loop(1, PLANE, near, 0)
    signal((z + 1) % planes, me)
    signal((z + planes - 1) % planes, me)
    return PLANE - 1 + 2


def window_of(half, i):
    return (i // 2) * 4 + half * 2 + i % 2


def shifts(offsets, turn_f, turn_g):
    def one_window(w, carry):
        f = lax.broadcasted_iota(jnp.int32, (RADIX, 128), 0)
        angle = ((f * offsets[w]) & (L - 1)).astype(F32) * (2.0 * math.pi / L)
        turn_f[0, w] = jnp.cos(angle)
        turn_f[1, w] = jnp.sin(angle)
        return carry

    lax.fori_loop(0, 8, one_window, 0, unroll=2)
    row = lax.broadcasted_iota(jnp.int32, (8, 128), 0)
    lane = lax.broadcasted_iota(jnp.int32, (8, 128), 1)
    start = jnp.zeros((8, 128), jnp.int32)
    for w in range(8):
        start = jnp.where(row == w, offsets[w], start)
    k = (BAND_LO // RADIX + (lane // 64) * 32 + lane % 32) * RADIX
    angle = ((k * start) & (L - 1)).astype(F32) * (2.0 * math.pi / L)
    turn_g[0] = jnp.cos(angle)
    turn_g[1] = jnp.where((lane // 32) % 2 == 0, -jnp.sin(angle), jnp.sin(angle))


def first_stage(half, offsets, raw, tables, lhs, turn_f, means):
    width = 128
    lane = lax.broadcasted_iota(jnp.int32, (16, width), 1)

    def sample(w, a, low):
        here = raw[w, :, pl.ds(a * TAIL + low, width)].astype(F32)
        if a:
            return here
        return jnp.where(lane + low < offsets[w], raw[w, :, pl.ds(L + low, width)].astype(F32), here)

    def one_mean(i, carry):
        w = window_of(half, i)
        total = functools.reduce(lambda p, q: p + q, [sample(w, a, low) for a in range(RADIX) for low in (0, width)])
        means[i] = jnp.broadcast_to(jnp.sum(total, axis=1, keepdims=True) * (1.0 / L), (16, width))
        return carry

    lax.fori_loop(0, ROWS // 16, one_mean, 0, unroll=MEAN_UNROLL)

    def one_window(index, carry):
        i, column = index // 2, index % 2
        w = window_of(half, i)
        mean = means[i]
        rows = pl.ds(pl.multiple_of(i * 16, 16), 16)
        low = pl.multiple_of(column * width, width)
        span = pl.ds(low, width)
        turn_cos, turn_sin = turn_f[0, w], turn_f[1, w]
        cosine, sine = tables[0, :, span], tables[1, :, span]
        cosine, sine = cosine * turn_cos + sine * turn_sin, sine * turn_cos - cosine * turn_sin
        taper = 0.5 - 0.5 * (tables[2, :, span] * turn_cos[1:2] + tables[3, :, span] * turn_sin[1:2])
        spectrum = real_fft([(sample(w, a, low) - mean) * taper[a : a + 1] for a in range(RADIX)])
        for f in range(RADIX):
            re, im = spectrum[f] if f <= RADIX // 2 else spectrum[RADIX - f]
            if f > RADIX // 2:
                im = -im
            if f:
                c, s = cosine[f : f + 1], sine[f : f + 1]
                re, im = (re * c, -re * s) if im is None else (re * c + im * s, im * c - re * s)
            else:
                im = jnp.zeros_like(re)
            for part, value in enumerate((re, im)):
                high = value.astype(BF16)
                lhs[f, rows, pl.ds(low + part * TAIL, width)] = high
                lhs[f, rows, pl.ds(low + (2 + part) * TAIL, width)] = (value - high.astype(F32)).astype(BF16)
        return carry

    lax.fori_loop(0, ROWS // 8, one_window, 0, unroll=FFT_UNROLL)


def second_stage_of(half, lhs, weights, kept, turn_g):
    lane = lax.broadcasted_iota(jnp.int32, (ROWS, 128), 1)
    real = (lane // 32) % 2 == 0
    turn = [
        jnp.concatenate(
            [jnp.broadcast_to(turn_g[part, w : w + 1], (16, 128)) for w in (window_of(half, i) for i in range(ROWS // 16))],
            0,
        )
        for part in range(2)
    ]
    power = jnp.zeros((ROWS, 128), F32)
    for start in range(0, RADIX, GROUP):
        whole = lhs[start : start + GROUP].reshape(GROUP * ROWS, 4 * TAIL)
        first = jnp.dot(whole[:, : 2 * TAIL], weights[...], preferred_element_type=F32)
        second = jnp.dot(whole[:, 2 * TAIL :], weights[:, :128], preferred_element_type=F32)
        both = (first[:, :128] + first[:, 128:] + second).reshape(GROUP, ROWS, 128)
        for j in range(GROUP):
            one = both[j]
            power = power + one * one
            other = jnp.where(real, pltpu.roll(one, 96, 1), pltpu.roll(one, 32, 1))
            kept[start + j] = one * turn[0] + other * turn[1]
    return power


def whitening(power, mask):
    row = lax.broadcasted_iota(jnp.int32, (128, 128), 0)
    col = lax.broadcasted_iota(jnp.int32, (128, 128), 1)
    same = (row // 64 == col // 64) & ((row % 32) // 4 == (col % 32) // 4)
    block = jnp.where(same, 1.0, 0.0).astype(F32)
    mean_power = jnp.dot(power, block, precision=lax.Precision.HIGHEST, preferred_element_type=F32) * (1.0 / SMOOTH)
    channel = lax.broadcasted_iota(jnp.int32, (16, 128), 0)
    flag = jnp.zeros((16, 128), F32)
    for c in range(16):
        flag = jnp.where(channel == c, mask[c].astype(F32), flag)
    flag = jnp.broadcast_to(flag[None], (ROWS // 16, 16, 128)).reshape(ROWS, 128)
    return (1.0 / jnp.sqrt(mean_power + EPS)) * flag


def main_kernel(
    planes, scale, offsets, mask, raw_hbm, tables_hbm, weights_hbm, table_hbm, out,
    raw, tables, weights, table, lhs, kept, turn_f, turn_g, means,
    send, recv, turned, own, halo, near, far, near_col, far_col, send_near, send_far, got_far, got, lag_lhs,
    in_sem, own_sem, s_send, s_recv, h_send, h_recv, x_send, x_recv, f_send, f_recv,
):
    z, me = place()
    my_q, my_v = me % QUAD, me // QUAD
    above, below = (z + 1) % planes, (z + planes - 1) % planes
    pairs = [
        (raw_hbm.at[pl.ds(start, 2)], raw.at[pl.ds(start, 2)]) for start in (0, 4, 2, 6)
    ] + [(tables_hbm, tables), (weights_hbm, weights), (table_hbm, table)]
    pairs = [pairs[i] for i in (4, 0, 1, 2, 3, 5, 6)]
    loads = [pltpu.make_async_copy(source, target, in_sem.at[i]) for i, (source, target) in enumerate(pairs)]
    for load in loads[:6]:
        load.start()
    expected = greet_all(planes, z, me)
    shifts(offsets, turn_f, turn_g)
    for slot in range(SLOTS):
        near_col[slot, 128:, :] = jnp.zeros((128, 128), F32)
        far_col[slot, :128, :] = jnp.zeros((128, 128), F32)
    left = lax.broadcasted_iota(jnp.int32, (64, 128), 1) < 64

    def bins_copy(half, to, source):
        return pltpu.make_async_remote_copy(
            src_ref=send.at[half, to],
            dst_ref=recv.at[half, source],
            send_sem=s_send.at[half],
            recv_sem=s_recv.at[half],
            device_id=device(z, to),
            device_id_type=MESH,
        )

    def all_bins(half):
        return pltpu.make_async_remote_copy(
            src_ref=send.at[half, pl.ds(0, PLANE - 1)],
            dst_ref=recv.at[half, pl.ds(0, PLANE - 1)],
            send_sem=s_send.at[half],
            recv_sem=s_recv.at[half],
            device_id=device(z, (me + 1) % PLANE),
            device_id_type=MESH,
        )

    def own_copy(half):
        return pltpu.make_async_copy(send.at[half, me], recv.at[half, me], own_sem.at[half])

    for half in range(HALVES):
        for load in loads[:3] if half == 0 else loads[3:5]:
            load.wait()
        first_stage(half, offsets, raw, tables, lhs, turn_f, means)
        if half == 0:
            loads[5].wait()
        factor = whitening(second_stage_of(half, lhs, weights, kept, turn_g), mask)
        if half == 0:
            pl.semaphore_wait(pltpu.get_barrier_semaphore(), expected)

        for f in range(RADIX):
            value = kept[f] * factor
            top, bottom = value[:32], value[32:]
            send[half, 2 * f] = jnp.where(left[:32], top, pltpu.roll(bottom, 64, 1)).astype(BF16)
            send[half, 2 * f + 1] = jnp.where(left[:32], pltpu.roll(top, 64, 1), bottom).astype(BF16)
        own_copy(half).start()

        def launch(j, carry, half=half):
            bins_copy(half, (me + j) % PLANE, me).start()
            return carry

        lax.fori_loop(1, PLANE, launch, 0)

    loads[6].start()

    def halo_copy(way, half, chunk):
        span = pl.ds(chunk * CHUNK, CHUNK)
        return pltpu.make_async_remote_copy(
            src_ref=own.at[half, span],
            dst_ref=halo.at[way, half, span],
            send_sem=h_send.at[way, half, chunk],
            recv_sem=h_recv.at[way, half, chunk],
            device_id=device(below if way == 0 else above, me),
            device_id_type=MESH,
        )

    for half in range(HALVES):
        own_copy(half).wait()
        all_bins(half).wait_recv()

        def one_block(v, carry, half=half):
            parts = [recv[half, v * QUAD + q, p * 16 : (p + 1) * 16, :] for p in range(2) for q in range(QUAD)]
            block = jnp.concatenate([part.astype(F32) for part in parts], 0).T
            for h in range(4):
                wh, ri = h // 2, h % 2
                start = pl.multiple_of(((half * 2 + ri) * 16 + v * 2 + wh) * REL_PITCH, 8)
                turned[pl.ds(start, 32), :] = block[h * 32 : (h + 1) * 32]
            return carry

        lax.fori_loop(0, WIN, one_block, 0, unroll=4)

        def gather(chunk, carry, half=half):
            for j in range(CHUNK):
                g = chunk * CHUNK + j
                real = turned[pl.ds(half * 32 * REL_PITCH + g, 16, stride=REL_PITCH), :]
                imag = turned[pl.ds((half * 32 + 16) * REL_PITCH + g, 16, stride=REL_PITCH), :]
                own[half, g] = jnp.concatenate([real, imag], 0).astype(BF16)
            halo_copy(0, half, chunk).start()
            halo_copy(1, half, chunk).start()
            return carry

        lax.fori_loop(0, CHUNKS, gather, 0)

    for half in range(HALVES):
        all_bins(half).wait_send()

    def operand(x, rx):
        def turn(u):
            return jnp.concatenate([u[16:32], -u[:16], u[48:], -u[32:48]], 0)

        return jnp.concatenate([jnp.where(left, x, turn(rx)), jnp.where(left, rx, turn(x))], 0).T.astype(BF16)

    def cross(chunk, carry):
        for way in range(2):
            for half in range(HALVES):
                halo_copy(way, half, chunk).wait_recv()
        for j in range(CHUNK):
            g = chunk * CHUNK + j
            a = jnp.concatenate([own[half, g].astype(F32) for half in range(HALVES)], 0)
            e = jnp.concatenate([halo[0, half, g].astype(F32) for half in range(HALVES)], 0)
            m = jnp.concatenate([halo[1, half, g].astype(F32) for half in range(HALVES)], 0)
            e = jnp.where(z + 1 < planes, e, 0.0)
            m = jnp.where(z > 0, m, 0.0)
            ra, re, rm = (pltpu.roll(x, 64, 1) for x in (a, e, m))
            right = jnp.concatenate([jnp.where(left, a, re), jnp.where(left, ra, e)], 0).astype(BF16)
            last = jnp.concatenate([e, re], 0).astype(BF16)
            for ref, value in (
                (near, jnp.dot(operand(a, ra), right, preferred_element_type=F32)),
                (far, jnp.dot(operand(m, rm), last, preferred_element_type=F32)),
            ):
                for part in range(2):
                    start = pl.multiple_of((g * 2 + part) * OUT_PITCH, 8)
                    ref[pl.ds(start, 64), :] = value[part * 64 : (part + 1) * 64]
        return carry

    lax.fori_loop(0, CHUNKS, cross, 0)

    def far_copy(to):
        return pltpu.make_async_remote_copy(
            src_ref=send_far.at[to],
            dst_ref=got_far.at[to],
            send_sem=f_send.at[to],
            recv_sem=f_recv.at[to],
            device_id=device(below, me),
            device_id_type=MESH,
        )

    def offsets_copy(ref, to, source):
        return pltpu.make_async_remote_copy(
            src_ref=ref.at[to],
            dst_ref=got.at[source],
            send_sem=x_send.at[0],
            recv_sem=x_recv.at[0],
            device_id=device(z, to),
            device_id_type=MESH,
        )

    def all_offsets():
        return pltpu.make_async_remote_copy(
            src_ref=send_near.at[pl.ds(0, PLANE - 1)],
            dst_ref=got.at[pl.ds(0, PLANE - 1)],
            send_sem=x_send.at[0],
            recv_sem=x_recv.at[0],
            device_id=device(z, (me + 1) % PLANE),
            device_id_type=MESH,
        )

    def own_packet(ref):
        return pltpu.make_async_copy(ref.at[me], got.at[me], own_sem.at[HALVES])

    def ship(ref, to):
        @pl.when(to != me)
        def _():
            offsets_copy(ref, to, me).start()

        @pl.when(to == me)
        def _():
            own_packet(ref).start()

    wide = lax.broadcasted_iota(jnp.int32, (128, 128), 1) < 64

    def pair_of(ref, column, base, size, target, q):
        def one_pair(i, carry):
            c = q * 16 + i
            block = jnp.concatenate(
                [ref[pl.ds(c, 64, stride=OUT_PITCH), :], ref[pl.ds(c + 8, 64, stride=OUT_PITCH), :]], 0
            )
            column[i, base : base + size, :] = block.T[:size]
            value = jnp.where(
                wide, column[i, pl.ds(c + 1, 128), :], column[i, pl.ds(c + 9, 128), :]
            ).astype(BF16)
            rows = pl.ds(pl.multiple_of(i * 16, 16), 16)
            for v in range(WIN):
                target[v * QUAD + q, rows, :] = value[v * 16 : (v + 1) * 16]
            return carry

        lax.fori_loop(0, 8, one_pair, 0, unroll=4)

    def far_quarter(j, carry):
        q = (my_q + j) % QUAD
        pair_of(far, far_col, 128, 64, send_far, q)

        def one_send(k, carry):
            far_copy((WIN - 1 - k) * QUAD + q).start()
            return carry

        lax.fori_loop(0, q + 1, one_send, 0)
        return carry

    lax.fori_loop(0, QUAD, far_quarter, 0)

    def near_quarter(j, carry):
        q = (my_q + j) % QUAD
        pair_of(near, near_col, 0, 128, send_near, q)

        def one_send(k, carry):
            v = (my_v + k) % WIN

            @pl.when(v + q < WIN - 1)
            def _():
                ship(send_near, v * QUAD + q)

            return carry

        lax.fori_loop(0, WIN, one_send, 0)
        return carry

    lax.fori_loop(0, QUAD, near_quarter, 0)

    def late_quarter(j, carry):
        q = (my_q + j) % QUAD

        def one_send(k, carry):
            to = (WIN - 1 - k) * QUAD + q
            far_copy(to).wait_recv()

            @pl.when(k == q)
            def _():
                send_near[to] = (send_near[to].astype(F32) + got_far[to].astype(F32)).astype(BF16)
                ship(send_near, to)

            @pl.when(k != q)
            def _():
                ship(got_far, to)

            return carry

        lax.fori_loop(0, q + 1, one_send, 0)
        return carry

    lax.fori_loop(0, QUAD, late_quarter, 0)

    def drain_halo(chunk, carry):
        for way in range(2):
            for half in range(HALVES):
                halo_copy(way, half, chunk).wait_send()
        return carry

    lax.fori_loop(0, CHUNKS, drain_halo, 0)

    def drain_far(q, carry):
        def one(k, carry):
            far_copy((WIN - 1 - k) * QUAD + q).wait_send()
            return carry

        return lax.fori_loop(0, q + 1, one, carry)

    lax.fori_loop(0, QUAD, drain_far, 0)
    loads[6].wait()
    own_packet(send_near).wait()
    all_offsets().wait()

    for f in range(RADIX):
        one, two = got[2 * f].astype(F32), got[2 * f + 1].astype(F32)
        span = slice(f * 128, (f + 1) * 128)
        lag_lhs[:128, span] = jnp.where(wide, one, pltpu.roll(two, 64, 1)).astype(BF16)
        lag_lhs[128:, span] = jnp.where(wide, pltpu.roll(one, 64, 1), two).astype(BF16)
    lags = jnp.dot(lag_lhs[...], table[...], preferred_element_type=F32) * scale
    for c in range(16):
        out[:, c, :] = lags[c * 16 : (c + 1) * 16]


def body(planes, raw, offsets, mask):
    operands = [offsets, mask, raw, first_tables(), second_stage(), lag_rows()]
    smem = pl.BlockSpec(memory_space=pltpu.SMEM)
    far_away = pl.BlockSpec(memory_space=pltpu.HBM)
    dma = pltpu.SemaphoreType.DMA
    vmem = pltpu.VMEM
    packets = vmem((PLANE, 128, 128), BF16)
    spectra = vmem((2 * BINS * OUT_PITCH, 128), F32)
    return pl.pallas_call(
        functools.partial(main_kernel, planes, 1.0 / math.sqrt(NB * 8 * WIN)),
        out_shape=jax.ShapeDtypeStruct((16, 16, LAGS), F32),
        in_specs=[smem, smem] + [far_away] * 4,
        out_specs=pl.BlockSpec(memory_space=pltpu.VMEM),
        scratch_shapes=[vmem(x.shape, x.dtype) for x in operands[2:]]
        + [
            vmem((RADIX, ROWS, 4 * TAIL), BF16),
            vmem((RADIX, ROWS, 128), F32),
            vmem((2, 8, RADIX, 128), F32),
            vmem((2, 8, 128), F32),
            vmem((ROWS // 16, 16, 128), F32),
            vmem((HALVES, PLANE, 32, 128), BF16),
            vmem((HALVES, PLANE, 32, 128), BF16),
            vmem((64 * REL_PITCH, 128), F32),
            vmem((HALVES, BINS, 32, 128), BF16),
            vmem((2, HALVES, BINS, 32, 128), BF16),
            spectra,
            spectra,
            vmem((SLOTS, 256, 128), F32),
            vmem((SLOTS, 256, 128), F32),
            packets,
            packets,
            packets,
            packets,
            vmem((256, 2 * NB), BF16),
            dma((7,)),
            dma((HALVES + 1,)),
            dma((HALVES,)),
            dma((HALVES,)),
            dma((2, HALVES, CHUNKS)),
            dma((2, HALVES, CHUNKS)),
            dma((1,)),
            dma((1,)),
            dma((PLANE,)),
            dma((PLANE,)),
        ],
        compiler_params=pltpu.CompilerParams(
            collective_id=0, has_side_effects=True, vmem_limit_bytes=48 * 2**20
        ),
        name="main",
    )(*(pltpu.with_memory_space_constraint(jnp.asarray(x), pltpu.HBM) for x in operands))


def solution(mesh):
    planes = mesh.shape["fibre"] // QUAD
    return jax.shard_map(
        functools.partial(body, planes),
        mesh=mesh,
        in_specs=(P("win", "fibre", None), P("win"), P("fibre")),
        out_specs=P("win", "fibre", None),
        check_vma=False,
    )
```

```python
import functools
import math

import jax
import jax.numpy as jnp
import numpy as np
from jax import lax
from jax.experimental import pallas as pl
from jax.experimental.pallas import tpu as pltpu
from jax.sharding import PartitionSpec as P

MESH = pl.DeviceIdType.MESH
L = 4096
BAND_LO = 64
NB = 1024
SMOOTH = 64
LAGS = 512
SPAN = 128
EPS = 1e-06
RADIX = 16
TAIL = L // RADIX
PLANE = 32
WIN = 8
QUAD = 4
BINS = 32
CHUNK = 8
REL_PITCH = 40
OUT_PITCH = 72
SLOTS = 4
FARTHEST_FIRST = ((1, 2), (1, 1), (1, 3), (1, 0), (0, 2), (0, 1), (0, 3), (0, 0))
HALVES = 2
ROWS = 128 // HALVES
CHUNKS = BINS // CHUNK
MEAN_UNROLL = 4
FFT_UNROLL = 2
GROUP = 16
F32 = jnp.float32
BF16 = jnp.bfloat16


def second_stage():
    b = np.arange(TAIL)[:, None]
    lane = np.arange(128)[None, :]
    half, imag, low = lane // 64, (lane // 32) % 2, lane % 32
    angle = 2.0 * np.pi * ((b * (BAND_LO // RADIX + half * 32 + low)) % TAIL) / TAIL
    cos, sin = np.cos(angle), np.sin(angle)
    whole = np.where(imag == 0, np.concatenate([cos, sin], 0), np.concatenate([-sin, cos], 0)).astype(np.float32)
    high = whole.astype(jnp.bfloat16)
    return np.concatenate([high, (whole - high.astype(np.float32)).astype(jnp.bfloat16)], 1)


def first_tables():
    f = np.arange(RADIX)[:, None]
    b = np.arange(TAIL)[None, :]
    twiddle, spot = 2.0 * np.pi * (f * b) / L, 2.0 * np.pi * (TAIL * f + b) / L
    return np.stack([np.cos(twiddle), np.sin(twiddle), np.cos(spot), np.sin(spot)]).astype(np.float32)


def lag_rows():
    frequency = np.arange(NB, dtype=np.int64) + BAND_LO
    lag_index = np.arange(LAGS, dtype=np.int64) - LAGS // 2
    turns = np.mod(frequency[:, None] * lag_index[None, :], L).astype(np.float32)
    angles = turns * np.float32(2.0 * math.pi / L)
    cos, sin = np.cos(angles.astype(np.float64)), np.sin(angles.astype(np.float64))
    table = np.stack([cos, -sin], 1).astype(np.float32)
    bins = RADIX * np.arange(64)[None, :] + np.arange(RADIX)[:, None]
    table = table[bins].reshape(RADIX, 2, 2, 16, 2, LAGS)
    return table.transpose(2, 0, 1, 3, 4, 5).reshape(2 * NB, LAGS).astype(jnp.bfloat16)


def real_fft(x):
    n = len(x)
    if n == 2:
        return [(x[0] + x[1], None), (x[0] - x[1], None)]
    even, odd = real_fft(x[0::2]), real_fft(x[1::2])
    half, quarter = n // 2, n // 4
    out = [None] * (half + 1)
    out[0] = (even[0][0] + odd[0][0], None)
    out[half] = (even[0][0] - odd[0][0], None)
    for k in range(1, quarter):
        (er, ei), (orr, oi) = even[k], odd[k]
        c, s = math.cos(2.0 * math.pi * k / n), math.sin(2.0 * math.pi * k / n)
        if 8 * k == n:
            tr, ti = (orr + oi) * c, (oi - orr) * c
        else:
            tr, ti = orr * c + oi * s, oi * c - orr * s
        out[k] = (er + tr, ei + ti)
        out[half - k] = (er - tr, ti - ei)
    out[quarter] = (even[quarter][0], -odd[quarter][0])
    return out


def place():
    fibre, win = lax.axis_index("fibre"), lax.axis_index("win")
    return fibre // QUAD, win * QUAD + fibre % QUAD


def device(z, s):
    return (z * QUAD + s % QUAD, s // QUAD)


def greet_all(planes, z, me):
    barrier = pltpu.get_barrier_semaphore()

    def signal(plane, s):
        pl.semaphore_signal(barrier, inc=1, device_id=device(plane, s), device_id_type=MESH)

    def near(j, carry):
        signal(z, (me + j) % PLANE)
        return carry

    lax.fori_loop(1, PLANE, near, 0)
    signal((z + 1) % planes, me)
    signal((z + planes - 1) % planes, me)
    return PLANE - 1 + 2


def window_of(half, i):
    return (i // 2) * 4 + half * 2 + i % 2


def shifts(offsets, turn_f, turn_g):
    def one_window(w, carry):
        f = lax.broadcasted_iota(jnp.int32, (RADIX, 128), 0)
        angle = ((f * offsets[w]) & (L - 1)).astype(F32) * (2.0 * math.pi / L)
        turn_f[0, w] = jnp.cos(angle)
        turn_f[1, w] = jnp.sin(angle)
        return carry

    lax.fori_loop(0, 8, one_window, 0, unroll=2)
    row = lax.broadcasted_iota(jnp.int32, (8, 128), 0)
    lane = lax.broadcasted_iota(jnp.int32, (8, 128), 1)
    start = jnp.zeros((8, 128), jnp.int32)
    for w in range(8):
        start = jnp.where(row == w, offsets[w], start)
    k = (BAND_LO // RADIX + (lane // 64) * 32 + lane % 32) * RADIX
    angle = ((k * start) & (L - 1)).astype(F32) * (2.0 * math.pi / L)
    turn_g[0] = jnp.cos(angle)
    turn_g[1] = jnp.where((lane // 32) % 2 == 0, -jnp.sin(angle), jnp.sin(angle))


def first_stage(half, offsets, raw, tables, lhs, turn_f, means):
    width = 128
    lane = lax.broadcasted_iota(jnp.int32, (16, width), 1)

    def sample(w, a, low):
        here = raw[w, :, pl.ds(a * TAIL + low, width)].astype(F32)
        if a:
            return here
        return jnp.where(lane + low < offsets[w], raw[w, :, pl.ds(L + low, width)].astype(F32), here)

    def one_mean(i, carry):
        w = window_of(half, i)
        total = functools.reduce(lambda p, q: p + q, [sample(w, a, low) for a in range(RADIX) for low in (0, width)])
        means[i] = jnp.broadcast_to(jnp.sum(total, axis=1, keepdims=True) * (1.0 / L), (16, width))
        return carry

    lax.fori_loop(0, ROWS // 16, one_mean, 0, unroll=MEAN_UNROLL)

    def one_window(index, carry):
        i, column = index // 2, index % 2
        w = window_of(half, i)
        mean = means[i]
        rows = pl.ds(pl.multiple_of(i * 16, 16), 16)
        low = pl.multiple_of(column * width, width)
        span = pl.ds(low, width)
        turn_cos, turn_sin = turn_f[0, w], turn_f[1, w]
        cosine, sine = tables[0, :, span], tables[1, :, span]
        cosine, sine = cosine * turn_cos + sine * turn_sin, sine * turn_cos - cosine * turn_sin
        taper = 0.5 - 0.5 * (tables[2, :, span] * turn_cos[1:2] + tables[3, :, span] * turn_sin[1:2])
        spectrum = real_fft([(sample(w, a, low) - mean) * taper[a : a + 1] for a in range(RADIX)])
        for f in range(RADIX):
            re, im = spectrum[f] if f <= RADIX // 2 else spectrum[RADIX - f]
            if f > RADIX // 2:
                im = -im
            if f:
                c, s = cosine[f : f + 1], sine[f : f + 1]
                re, im = (re * c, -re * s) if im is None else (re * c + im * s, im * c - re * s)
            else:
                im = jnp.zeros_like(re)
            for part, value in enumerate((re, im)):
                high = value.astype(BF16)
                lhs[f, rows, pl.ds(low + part * TAIL, width)] = high
                lhs[f, rows, pl.ds(low + (2 + part) * TAIL, width)] = (value - high.astype(F32)).astype(BF16)
        return carry

    lax.fori_loop(0, ROWS // 8, one_window, 0, unroll=FFT_UNROLL)


def second_stage_of(half, lhs, weights, kept, turn_g):
    lane = lax.broadcasted_iota(jnp.int32, (ROWS, 128), 1)
    real = (lane // 32) % 2 == 0
    turn = [
        jnp.concatenate(
            [jnp.broadcast_to(turn_g[part, w : w + 1], (16, 128)) for w in (window_of(half, i) for i in range(ROWS // 16))],
            0,
        )
        for part in range(2)
    ]
    power = jnp.zeros((ROWS, 128), F32)
    for start in range(0, RADIX, GROUP):
        whole = lhs[start : start + GROUP].reshape(GROUP * ROWS, 4 * TAIL)
        first = jnp.dot(whole[:, : 2 * TAIL], weights[...], preferred_element_type=F32)
        second = jnp.dot(whole[:, 2 * TAIL :], weights[:, :128], preferred_element_type=F32)
        both = (first[:, :128] + first[:, 128:] + second).reshape(GROUP, ROWS, 128)
        for j in range(GROUP):
            one = both[j]
            power = power + one * one
            other = jnp.where(real, pltpu.roll(one, 96, 1), pltpu.roll(one, 32, 1))
            kept[start + j] = one * turn[0] + other * turn[1]
    return power


def whitening(power, mask):
    row = lax.broadcasted_iota(jnp.int32, (128, 128), 0)
    col = lax.broadcasted_iota(jnp.int32, (128, 128), 1)
    same = (row // 64 == col // 64) & ((row % 32) // 4 == (col % 32) // 4)
    block = jnp.where(same, 1.0, 0.0).astype(F32)
    mean_power = jnp.dot(power, block, precision=lax.Precision.HIGHEST, preferred_element_type=F32) * (1.0 / SMOOTH)
    channel = lax.broadcasted_iota(jnp.int32, (16, 128), 0)
    flag = jnp.zeros((16, 128), F32)
    for c in range(16):
        flag = jnp.where(channel == c, mask[c].astype(F32), flag)
    flag = jnp.broadcast_to(flag[None], (ROWS // 16, 16, 128)).reshape(ROWS, 128)
    return (1.0 / jnp.sqrt(mean_power + EPS)) * flag


def main_kernel(
    planes, scale, offsets, mask, raw_hbm, tables_hbm, weights_hbm, table_hbm, out,
    raw, tables, weights, table, lhs, kept, turn_f, turn_g, means,
    send, recv, turned, own, halo, near, far, near_col, far_col, send_own, send_near, send_far, got_far, got, lag_lhs, first_lags, own_left,
    in_sem, own_sem, s_send, s_recv, h_send, h_recv, x_send, x_recv, f_send, f_recv,
):
    z, me = place()
    my_q, my_v = me % QUAD, me // QUAD
    above, below = (z + 1) % planes, (z + planes - 1) % planes
    pairs = [
        (raw_hbm.at[pl.ds(start, 2)], raw.at[pl.ds(start, 2)]) for start in (0, 4, 2, 6)
    ] + [(tables_hbm, tables), (weights_hbm, weights), (table_hbm, table)]
    pairs = [pairs[i] for i in (4, 0, 1, 2, 3, 5, 6)]
    loads = [pltpu.make_async_copy(source, target, in_sem.at[i]) for i, (source, target) in enumerate(pairs)]
    for load in loads[:6]:
        load.start()
    expected = greet_all(planes, z, me)
    shifts(offsets, turn_f, turn_g)
    for slot in range(SLOTS):
        near_col[slot, 128:, :] = jnp.zeros((128, 128), F32)
        far_col[slot, :128, :] = jnp.zeros((128, 128), F32)
    left = lax.broadcasted_iota(jnp.int32, (64, 128), 1) < 64

    def bins_copy(half, to, source):
        return pltpu.make_async_remote_copy(
            src_ref=send.at[half, to],
            dst_ref=recv.at[half, source],
            send_sem=s_send.at[half],
            recv_sem=s_recv.at[half],
            device_id=device(z, to),
            device_id_type=MESH,
        )

    def all_bins(half):
        return pltpu.make_async_remote_copy(
            src_ref=send.at[half, pl.ds(0, PLANE - 1)],
            dst_ref=recv.at[half, pl.ds(0, PLANE - 1)],
            send_sem=s_send.at[half],
            recv_sem=s_recv.at[half],
            device_id=device(z, (me + 1) % PLANE),
            device_id_type=MESH,
        )

    def own_copy(half):
        return pltpu.make_async_copy(send.at[half, me], recv.at[half, me], own_sem.at[half])

    for half in range(HALVES):
        for load in loads[:3] if half == 0 else loads[3:5]:
            load.wait()
        first_stage(half, offsets, raw, tables, lhs, turn_f, means)
        if half == 0:
            loads[5].wait()
        factor = whitening(second_stage_of(half, lhs, weights, kept, turn_g), mask)
        if half == 0:
            pl.semaphore_wait(pltpu.get_barrier_semaphore(), expected)

        for f in range(RADIX):
            value = kept[f] * factor
            top, bottom = value[:32], value[32:]
            send[half, 2 * f] = jnp.where(left[:32], top, pltpu.roll(bottom, 64, 1)).astype(BF16)
            send[half, 2 * f + 1] = jnp.where(left[:32], pltpu.roll(top, 64, 1), bottom).astype(BF16)
        own_copy(half).start()

        for far_x, far_y in FARTHEST_FIRST:

            def launch(j, carry, half=half, far_x=far_x, far_y=far_y):
                to = ((my_v // 4 + far_x) % 2 * 4 + (my_v + far_y) % 4) * QUAD + (my_q + j) % QUAD
                bins_copy(half, to, me).start()
                return carry

            lax.fori_loop(0 if far_x + far_y else 1, QUAD, launch, 0)

    loads[6].start()

    def halo_copy(way, half, chunk):
        span = pl.ds(chunk * CHUNK, CHUNK)
        return pltpu.make_async_remote_copy(
            src_ref=own.at[half, span],
            dst_ref=halo.at[way, half, span],
            send_sem=h_send.at[way, half, chunk],
            recv_sem=h_recv.at[way, half, chunk],
            device_id=device(below if way == 0 else above, me),
            device_id_type=MESH,
        )

    for half in range(HALVES):
        own_copy(half).wait()
        all_bins(half).wait_recv()

        def one_block(v, carry, half=half):
            parts = [recv[half, v * QUAD + q, p * 16 : (p + 1) * 16, :] for p in range(2) for q in range(QUAD)]
            block = jnp.concatenate([part.astype(F32) for part in parts], 0).T
            for h in range(4):
                wh, ri = h // 2, h % 2
                start = pl.multiple_of(((half * 2 + ri) * 16 + v * 2 + wh) * REL_PITCH, 8)
                turned[pl.ds(start, 32), :] = block[h * 32 : (h + 1) * 32]
            return carry

        lax.fori_loop(0, WIN, one_block, 0, unroll=4)

        def gather(chunk, carry, half=half):
            for j in range(CHUNK):
                g = chunk * CHUNK + j
                real = turned[pl.ds(half * 32 * REL_PITCH + g, 16, stride=REL_PITCH), :]
                imag = turned[pl.ds((half * 32 + 16) * REL_PITCH + g, 16, stride=REL_PITCH), :]
                own[half, g] = jnp.concatenate([real, imag], 0).astype(BF16)
            halo_copy(0, half, chunk).start()
            halo_copy(1, half, chunk).start()
            return carry

        lax.fori_loop(0, CHUNKS, gather, 0)

    for half in range(HALVES):
        all_bins(half).wait_send()

    def operand(x, rx):
        def turn(u):
            return jnp.concatenate([u[16:32], -u[:16], u[48:], -u[32:48]], 0)

        return jnp.concatenate([jnp.where(left, x, turn(rx)), jnp.where(left, rx, turn(x))], 0).T.astype(BF16)

    def own_rows(g):
        return jnp.concatenate([own[half, g].astype(F32) for half in range(HALVES)], 0)

    def keep(ref, g, value):
        for part in range(2):
            start = pl.multiple_of((g * 2 + part) * OUT_PITCH, 8)
            ref[pl.ds(start, 64), :] = value[part * 64 : (part + 1) * 64]

    def own_operand(g, carry):
        a = own_rows(g)
        ra = pltpu.roll(a, 64, 1)
        mine = operand(a, ra)
        own_left[g] = mine
        keep(near, g, jnp.dot(mine, jnp.concatenate([a, ra], 0).astype(BF16), preferred_element_type=F32))
        return carry

    lax.fori_loop(0, BINS, own_operand, 0, unroll=4)

    def cross(chunk, carry):
        for way in range(2):
            for half in range(HALVES):
                halo_copy(way, half, chunk).wait_recv()
        for j in range(CHUNK):
            g = chunk * CHUNK + j
            a = own_rows(g)
            e = jnp.concatenate([halo[0, half, g].astype(F32) for half in range(HALVES)], 0)
            m = jnp.concatenate([halo[1, half, g].astype(F32) for half in range(HALVES)], 0)
            e = jnp.where(z + 1 < planes, e, 0.0)
            m = jnp.where(z > 0, m, 0.0)
            ra, re, rm = (pltpu.roll(x, 64, 1) for x in (a, e, m))
            right = jnp.concatenate([jnp.where(left, a, re), jnp.where(left, ra, e)], 0).astype(BF16)
            last = jnp.concatenate([e, re], 0).astype(BF16)
            keep(near, g, jnp.dot(own_left[g], right, preferred_element_type=F32))
            keep(far, g, jnp.dot(operand(m, rm), last, preferred_element_type=F32))
        return carry

    def far_copy(part, to):
        return pltpu.make_async_remote_copy(
            src_ref=send_far.at[part, to],
            dst_ref=got_far.at[part, to],
            send_sem=f_send.at[part, to],
            recv_sem=f_recv.at[part, to],
            device_id=device(below, me),
            device_id_type=MESH,
        )

    def offsets_copy(ref, part, to):
        return pltpu.make_async_remote_copy(
            src_ref=ref.at[part, to],
            dst_ref=got.at[part, me],
            send_sem=x_send.at[part],
            recv_sem=x_recv.at[part],
            device_id=device(z, to),
            device_id_type=MESH,
        )

    def all_offsets(part):
        return pltpu.make_async_remote_copy(
            src_ref=send_near.at[part, pl.ds(0, PLANE - 1)],
            dst_ref=got.at[part, pl.ds(0, PLANE - 1)],
            send_sem=x_send.at[part],
            recv_sem=x_recv.at[part],
            device_id=device(z, (me + 1) % PLANE),
            device_id_type=MESH,
        )

    def own_packet(ref, part):
        return pltpu.make_async_copy(ref.at[part, me], got.at[part, me], own_sem.at[HALVES + part])

    def ship(ref, part, to):
        @pl.when(to != me)
        def _():
            offsets_copy(ref, part, to).start()

        @pl.when(to == me)
        def _():
            own_packet(ref, part).start()

    lane = lax.broadcasted_iota(jnp.int32, (128, 128), 1)

    def packets_of(ref, column, base, size, target, part, q):
        def one_group(i, carry):
            c = q * 16 + i
            start = part * BINS * OUT_PITCH
            block = jnp.concatenate(
                [ref[pl.ds(start + c + 4 * k, BINS, stride=OUT_PITCH), :] for k in range(4)], 0
            )
            column[i, base : base + size, :] = block.T[:size]
            value = column[i, pl.ds(c + 13, 128), :]
            for k in (2, 1, 0):
                value = jnp.where(lane < 32 * k + 32, column[i, pl.ds(c + 4 * k + 1, 128), :], value)
            value = value.astype(BF16)
            rows = pl.ds(pl.multiple_of(i * 16, 16), 16)
            for v in range(WIN):
                target[part, v * QUAD + q, rows, :] = value[v * 16 : (v + 1) * 16]
            return carry

        lax.fori_loop(0, 4, one_group, 0, unroll=4)

    def early_part(part, carry):
        def early_quarter(q, carry):
            packets_of(near, near_col, 0, 128, send_own, part, q)
            for far_x, far_y in FARTHEST_FIRST:
                v = (my_v // 4 + far_x) % 2 * 4 + (my_v + far_y) % 4

                @pl.when(v + q < 3)
                def _(v=v):
                    ship(send_own, part, v * QUAD + q)

            return carry

        return lax.fori_loop(0, 3, early_quarter, carry)

    lax.fori_loop(0, 2, early_part, 0)

    def late_part(part, carry):
        def late_quarter(j, carry):
            q = (my_q + j) % QUAD

            def one_send(k, carry):
                to = (WIN - 1 - k) * QUAD + q
                far_copy(part, to).wait_recv()

                @pl.when(k == q)
                def _():
                    send_near[part, to] = (
                        send_near[part, to].astype(F32) + got_far[part, to].astype(F32)
                    ).astype(BF16)
                    ship(send_near, part, to)

                @pl.when(k != q)
                def _():
                    ship(got_far, part, to)

                return carry

            return lax.fori_loop(0, q + 1, one_send, carry)

        return lax.fori_loop(0, QUAD, late_quarter, carry)

    def one_part(part, carry):
        lax.fori_loop(part * (CHUNKS // 2), (part + 1) * (CHUNKS // 2), cross, 0)

        def far_quarter(j, carry):
            q = (my_q + j) % QUAD
            packets_of(far, far_col, 128, 64, send_far, part, q)

            def one_send(k, carry):
                far_copy(part, (WIN - 1 - k) * QUAD + q).start()
                return carry

            return lax.fori_loop(0, q + 1, one_send, carry)

        lax.fori_loop(0, QUAD, far_quarter, 0)

        def near_quarter(j, carry):
            q = (my_q + j) % QUAD
            packets_of(near, near_col, 0, 128, send_near, part, q)

            for far_x, far_y in FARTHEST_FIRST:
                v = (my_v // 4 + far_x) % 2 * 4 + (my_v + far_y) % 4

                @pl.when((v + q > 2) & (v + q < WIN - 1))
                def _(v=v):
                    ship(send_near, part, v * QUAD + q)

            return carry

        lax.fori_loop(0, QUAD, near_quarter, 0)
        return late_part(part, carry)

    lax.fori_loop(0, 2, one_part, 0)


    def drain_halo(chunk, carry):
        for way in range(2):
            for half in range(HALVES):
                halo_copy(way, half, chunk).wait_send()
        return carry

    lax.fori_loop(0, CHUNKS, drain_halo, 0)

    def drain_far(q, carry):
        def one(k, carry):
            for part in range(2):
                far_copy(part, (WIN - 1 - k) * QUAD + q).wait_send()
            return carry

        return lax.fori_loop(0, q + 1, one, carry)

    lax.fori_loop(0, QUAD, drain_far, 0)

    loads[6].wait()
    low64 = lax.broadcasted_iota(jnp.int32, (64, 128), 1) < 64
    even32 = (lax.broadcasted_iota(jnp.int32, (64, 128), 1) // 32) % 2 == 0

    def low_high(one, two):
        return jnp.where(low64, one, pltpu.roll(two, 64, 1)), jnp.where(low64, pltpu.roll(one, 64, 1), two)

    def even_odd(one, two):
        return jnp.where(even32, one, pltpu.roll(two, 32, 1)), jnp.where(even32, pltpu.roll(one, 96, 1), two)

    for part in range(2):
        own_packet(send_near, part).wait()
        all_offsets(part).wait_recv()
        for f in range(PLANE // 4):
            packets = [got[part, 4 * f + k].astype(F32) for k in range(4)]
            one, three = low_high(packets[0], packets[2])
            two, four = low_high(packets[1], packets[3])
            span = slice(f * 128, (f + 1) * 128)
            for k, value in enumerate(even_odd(one, two) + even_odd(three, four)):
                lag_lhs[k * 64 : (k + 1) * 64, span] = value.astype(BF16)
        lags = jnp.dot(lag_lhs[...], table[part * NB : (part + 1) * NB, :], preferred_element_type=F32) * scale
        if part == 0:
            first_lags[...] = lags
        else:
            lags = lags + first_lags[...]
            for c in range(16):
                out[:, c, :] = lags[c * 16 : (c + 1) * 16]
    for part in range(2):
        all_offsets(part).wait_send()


def body(planes, raw, offsets, mask):
    operands = [offsets, mask, raw, first_tables(), second_stage(), lag_rows()]
    smem = pl.BlockSpec(memory_space=pltpu.SMEM)
    far_away = pl.BlockSpec(memory_space=pltpu.HBM)
    dma = pltpu.SemaphoreType.DMA
    vmem = pltpu.VMEM
    packets = vmem((2, PLANE, 64, 128), BF16)
    spectra = vmem((2 * BINS * OUT_PITCH, 128), F32)
    return pl.pallas_call(
        functools.partial(main_kernel, planes, 1.0 / math.sqrt(NB * 8 * WIN)),
        out_shape=jax.ShapeDtypeStruct((16, 16, LAGS), F32),
        in_specs=[smem, smem] + [far_away] * 4,
        out_specs=pl.BlockSpec(memory_space=pltpu.VMEM),
        scratch_shapes=[vmem(x.shape, x.dtype) for x in operands[2:]]
        + [
            vmem((RADIX, ROWS, 4 * TAIL), BF16),
            vmem((RADIX, ROWS, 128), F32),
            vmem((2, 8, RADIX, 128), F32),
            vmem((2, 8, 128), F32),
            vmem((ROWS // 16, 16, 128), F32),
            vmem((HALVES, PLANE, 32, 128), BF16),
            vmem((HALVES, PLANE, 32, 128), BF16),
            vmem((64 * REL_PITCH, 128), F32),
            vmem((HALVES, BINS, 32, 128), BF16),
            vmem((2, HALVES, BINS, 32, 128), BF16),
            spectra,
            spectra,
            vmem((SLOTS, 256, 128), F32),
            vmem((SLOTS, 256, 128), F32),
            packets,
            packets,
            packets,
            packets,
            packets,
            vmem((256, NB), BF16),
            vmem((256, LAGS), F32),
            vmem((BINS, 128, 128), BF16),
            dma((7,)),
            dma((HALVES + 2,)),
            dma((HALVES,)),
            dma((HALVES,)),
            dma((2, HALVES, CHUNKS)),
            dma((2, HALVES, CHUNKS)),
            dma((2,)),
            dma((2,)),
            dma((2, PLANE)),
            dma((2, PLANE)),
        ],
        compiler_params=pltpu.CompilerParams(
            collective_id=0, has_side_effects=True, vmem_limit_bytes=48 * 2**20
        ),
        name="main",
    )(*(pltpu.with_memory_space_constraint(jnp.asarray(x), pltpu.HBM) for x in operands))


def solution(mesh):
    planes = mesh.shape["fibre"] // QUAD
    return jax.shard_map(
        functools.partial(body, planes),
        mesh=mesh,
        in_specs=(P("win", "fibre", None), P("win"), P("fibre")),
        out_specs=P("win", "fibre", None),
        check_vma=False,
    )
```

```python
import functools
import math

import jax
import jax.numpy as jnp
import numpy as np
from jax import lax
from jax.experimental import pallas as pl
from jax.experimental.pallas import tpu as pltpu
from jax.sharding import PartitionSpec as P

MESH = pl.DeviceIdType.MESH
L = 4096
BAND_LO = 64
NB = 1024
SMOOTH = 64
LAGS = 512
SPAN = 128
EPS = 1e-06
RADIX = 16
TAIL = L // RADIX
PLANE = 32
WIN = 8
QUAD = 4
BINS = 32
CHUNK = 8
REL_PITCH = 40
OUT_PITCH = 72
SLOTS = 4
PARTS = 2
SIDE = 16 // (2 * PARTS)
FARTHEST_FIRST = ((1, 2), (1, 1), (1, 3), (1, 0), (0, 2), (0, 1), (0, 3), (0, 0))
HALVES = 2
ROWS = 128 // HALVES
CHUNKS = BINS // CHUNK
MEAN_UNROLL = 4
FFT_UNROLL = 2
GROUP = 16
F32 = jnp.float32
BF16 = jnp.bfloat16


def second_stage():
    b = np.arange(TAIL)[:, None]
    lane = np.arange(128)[None, :]
    half, imag, low = lane // 64, (lane // 32) % 2, lane % 32
    angle = 2.0 * np.pi * ((b * (BAND_LO // RADIX + half * 32 + low)) % TAIL) / TAIL
    cos, sin = np.cos(angle), np.sin(angle)
    whole = np.where(imag == 0, np.concatenate([cos, sin], 0), np.concatenate([-sin, cos], 0)).astype(np.float32)
    high = whole.astype(jnp.bfloat16)
    return np.concatenate([high, (whole - high.astype(np.float32)).astype(jnp.bfloat16)], 1)


def first_tables():
    f = np.arange(RADIX)[:, None]
    b = np.arange(TAIL)[None, :]
    twiddle, spot = 2.0 * np.pi * (f * b) / L, 2.0 * np.pi * (TAIL * f + b) / L
    return np.stack([np.cos(twiddle), np.sin(twiddle), np.cos(spot), np.sin(spot)]).astype(np.float32)


def lag_rows():
    frequency = np.arange(NB, dtype=np.int64) + BAND_LO
    lag_index = np.arange(LAGS, dtype=np.int64) - LAGS // 2
    turns = np.mod(frequency[:, None] * lag_index[None, :], L).astype(np.float32)
    angles = turns * np.float32(2.0 * math.pi / L)
    cos, sin = np.cos(angles.astype(np.float64)), np.sin(angles.astype(np.float64))
    table = np.stack([cos, -sin], 1).astype(np.float32)
    bins = RADIX * np.arange(64)[None, :] + np.arange(RADIX)[:, None]
    table = table[bins].reshape(RADIX, 2, PARTS, BINS // PARTS, 2, LAGS)
    return table.transpose(2, 0, 1, 3, 4, 5).reshape(2 * NB, LAGS).astype(jnp.bfloat16)


def real_fft(x):
    n = len(x)
    if n == 2:
        return [(x[0] + x[1], None), (x[0] - x[1], None)]
    even, odd = real_fft(x[0::2]), real_fft(x[1::2])
    half, quarter = n // 2, n // 4
    out = [None] * (half + 1)
    out[0] = (even[0][0] + odd[0][0], None)
    out[half] = (even[0][0] - odd[0][0], None)
    for k in range(1, quarter):
        (er, ei), (orr, oi) = even[k], odd[k]
        c, s = math.cos(2.0 * math.pi * k / n), math.sin(2.0 * math.pi * k / n)
        if 8 * k == n:
            tr, ti = (orr + oi) * c, (oi - orr) * c
        else:
            tr, ti = orr * c + oi * s, oi * c - orr * s
        out[k] = (er + tr, ei + ti)
        out[half - k] = (er - tr, ti - ei)
    out[quarter] = (even[quarter][0], -odd[quarter][0])
    return out


def place():
    fibre, win = lax.axis_index("fibre"), lax.axis_index("win")
    return fibre // QUAD, win * QUAD + fibre % QUAD


def device(z, s):
    return (z * QUAD + s % QUAD, s // QUAD)


def greet_all(planes, z, me):
    barrier = pltpu.get_barrier_semaphore()

    def signal(plane, s):
        pl.semaphore_signal(barrier, inc=1, device_id=device(plane, s), device_id_type=MESH)

    for far_x, far_y in FARTHEST_FIRST:
        v = (me // QUAD // 4 + far_x) % 2 * 4 + (me // QUAD + far_y) % 4

        def one(j, carry, v=v):
            signal(z, v * QUAD + (me + j) % QUAD)
            return carry

        lax.fori_loop(0 if far_x + far_y else 1, QUAD, one, 0, unroll=True)
    signal((z + 1) % planes, me)
    signal((z + planes - 1) % planes, me)
    return PLANE - 1 + 2


def window_of(half, i):
    return (i // 2) * 4 + half * 2 + i % 2


def shifts(offsets, turn_f, turn_g):
    def one_window(w, carry):
        f = lax.broadcasted_iota(jnp.int32, (RADIX, 128), 0)
        angle = ((f * offsets[w]) & (L - 1)).astype(F32) * (2.0 * math.pi / L)
        turn_f[0, w] = jnp.cos(angle)
        turn_f[1, w] = jnp.sin(angle)
        return carry

    lax.fori_loop(0, 8, one_window, 0, unroll=2)
    row = lax.broadcasted_iota(jnp.int32, (8, 128), 0)
    lane = lax.broadcasted_iota(jnp.int32, (8, 128), 1)
    start = jnp.zeros((8, 128), jnp.int32)
    for w in range(8):
        start = jnp.where(row == w, offsets[w], start)
    k = (BAND_LO // RADIX + (lane // 64) * 32 + lane % 32) * RADIX
    angle = ((k * start) & (L - 1)).astype(F32) * (2.0 * math.pi / L)
    turn_g[0] = jnp.cos(angle)
    turn_g[1] = jnp.where((lane // 32) % 2 == 0, -jnp.sin(angle), jnp.sin(angle))


def first_stage(half, offsets, raw, tables, lhs, turn_f, means):
    width = 128
    lane = lax.broadcasted_iota(jnp.int32, (16, width), 1)

    def sample(w, a, low):
        here = raw[w, :, pl.ds(a * TAIL + low, width)].astype(F32)
        if a:
            return here
        return jnp.where(lane + low < offsets[w], raw[w, :, pl.ds(L + low, width)].astype(F32), here)

    def one_mean(i, carry):
        w = window_of(half, i)
        total = functools.reduce(lambda p, q: p + q, [sample(w, a, low) for a in range(RADIX) for low in (0, width)])
        means[i] = jnp.broadcast_to(jnp.sum(total, axis=1, keepdims=True) * (1.0 / L), (16, width))
        return carry

    lax.fori_loop(0, ROWS // 16, one_mean, 0, unroll=MEAN_UNROLL)

    def one_window(index, carry):
        i, column = index // 2, index % 2
        w = window_of(half, i)
        mean = means[i]
        rows = pl.ds(pl.multiple_of(i * 16, 16), 16)
        low = pl.multiple_of(column * width, width)
        span = pl.ds(low, width)
        turn_cos, turn_sin = turn_f[0, w], turn_f[1, w]
        cosine, sine = tables[0, :, span], tables[1, :, span]
        cosine, sine = cosine * turn_cos + sine * turn_sin, sine * turn_cos - cosine * turn_sin
        taper = 0.5 - 0.5 * (tables[2, :, span] * turn_cos[1:2] + tables[3, :, span] * turn_sin[1:2])
        spectrum = real_fft([(sample(w, a, low) - mean) * taper[a : a + 1] for a in range(RADIX)])
        for f in range(RADIX):
            re, im = spectrum[f] if f <= RADIX // 2 else spectrum[RADIX - f]
            if f > RADIX // 2:
                im = -im
            if f:
                c, s = cosine[f : f + 1], sine[f : f + 1]
                re, im = (re * c, -re * s) if im is None else (re * c + im * s, im * c - re * s)
            else:
                im = jnp.zeros_like(re)
            for part, value in enumerate((re, im)):
                high = value.astype(BF16)
                lhs[f, rows, pl.ds(low + part * TAIL, width)] = high
                lhs[f, rows, pl.ds(low + (2 + part) * TAIL, width)] = (value - high.astype(F32)).astype(BF16)
        return carry

    lax.fori_loop(0, ROWS // 8, one_window, 0, unroll=FFT_UNROLL)


def second_stage_of(half, lhs, weights, kept, turn_g):
    lane = lax.broadcasted_iota(jnp.int32, (ROWS, 128), 1)
    real = (lane // 32) % 2 == 0
    turn = [
        jnp.concatenate(
            [jnp.broadcast_to(turn_g[part, w : w + 1], (16, 128)) for w in (window_of(half, i) for i in range(ROWS // 16))],
            0,
        )
        for part in range(2)
    ]
    power = jnp.zeros((ROWS, 128), F32)
    for start in range(0, RADIX, GROUP):
        whole = lhs[start : start + GROUP].reshape(GROUP * ROWS, 4 * TAIL)
        first = jnp.dot(whole[:, : 2 * TAIL], weights[...], preferred_element_type=F32)
        second = jnp.dot(whole[:, 2 * TAIL :], weights[:, :128], preferred_element_type=F32)
        both = (first[:, :128] + first[:, 128:] + second).reshape(GROUP, ROWS, 128)
        for j in range(GROUP):
            one = both[j]
            power = power + one * one
            other = jnp.where(real, pltpu.roll(one, 96, 1), pltpu.roll(one, 32, 1))
            kept[start + j] = one * turn[0] + other * turn[1]
    return power


def whitening(power, mask):
    row = lax.broadcasted_iota(jnp.int32, (128, 128), 0)
    col = lax.broadcasted_iota(jnp.int32, (128, 128), 1)
    same = (row // 64 == col // 64) & ((row % 32) // 4 == (col % 32) // 4)
    block = jnp.where(same, 1.0, 0.0).astype(F32)
    mean_power = jnp.dot(power, block, precision=lax.Precision.HIGHEST, preferred_element_type=F32) * (1.0 / SMOOTH)
    channel = lax.broadcasted_iota(jnp.int32, (16, 128), 0)
    flag = jnp.zeros((16, 128), F32)
    for c in range(16):
        flag = jnp.where(channel == c, mask[c].astype(F32), flag)
    flag = jnp.broadcast_to(flag[None], (ROWS // 16, 16, 128)).reshape(ROWS, 128)
    return (1.0 / jnp.sqrt(mean_power + EPS)) * flag


def main_kernel(
    planes, scale, offsets, mask, raw_hbm, tables_hbm, weights_hbm, table_hbm, out,
    raw, tables, weights, table, lhs, kept, turn_f, turn_g, means,
    send, recv, turned, own, halo, near, far, near_col, far_col, send_own, send_near, send_far, got_far, got, lag_lhs, first_lags, own_left,
    in_sem, own_sem, s_send, s_recv, h_send, h_recv, x_send, x_recv, f_send, f_recv,
):
    z, me = place()
    my_q, my_v = me % QUAD, me // QUAD
    above, below = (z + 1) % planes, (z + planes - 1) % planes
    pairs = [
        (raw_hbm.at[pl.ds(start, 2)], raw.at[pl.ds(start, 2)]) for start in (0, 4, 2, 6)
    ] + [(tables_hbm, tables), (weights_hbm, weights), (table_hbm, table)]
    pairs = [pairs[i] for i in (4, 0, 1, 2, 3, 5, 6)]
    loads = [pltpu.make_async_copy(source, target, in_sem.at[i]) for i, (source, target) in enumerate(pairs)]
    for load in loads[:3]:
        load.start()
    expected = greet_all(planes, z, me)
    for load in loads[3:6]:
        load.start()
    shifts(offsets, turn_f, turn_g)
    for slot in range(SLOTS):
        near_col[slot, 128:, :] = jnp.zeros((128, 128), F32)
        far_col[slot, :128, :] = jnp.zeros((128, 128), F32)
    left = lax.broadcasted_iota(jnp.int32, (64, 128), 1) < 64

    def bins_copy(half, to, source):
        return pltpu.make_async_remote_copy(
            src_ref=send.at[half, to],
            dst_ref=recv.at[half, source],
            send_sem=s_send.at[half],
            recv_sem=s_recv.at[half],
            device_id=device(z, to),
            device_id_type=MESH,
        )

    def all_bins(half):
        return pltpu.make_async_remote_copy(
            src_ref=send.at[half, pl.ds(0, PLANE - 1)],
            dst_ref=recv.at[half, pl.ds(0, PLANE - 1)],
            send_sem=s_send.at[half],
            recv_sem=s_recv.at[half],
            device_id=device(z, (me + 1) % PLANE),
            device_id_type=MESH,
        )

    def own_copy(half):
        return pltpu.make_async_copy(send.at[half, me], recv.at[half, me], own_sem.at[half])

    for half in range(HALVES):
        for load in loads[:3] if half == 0 else loads[3:5]:
            load.wait()
        first_stage(half, offsets, raw, tables, lhs, turn_f, means)
        if half == 0:
            loads[5].wait()
        factor = whitening(second_stage_of(half, lhs, weights, kept, turn_g), mask)
        if half == 0:
            pl.semaphore_wait(pltpu.get_barrier_semaphore(), expected)

        for f in range(RADIX):
            value = kept[f] * factor
            top, bottom = value[:32], value[32:]
            send[half, 2 * f] = jnp.where(left[:32], top, pltpu.roll(bottom, 64, 1)).astype(BF16)
            send[half, 2 * f + 1] = jnp.where(left[:32], pltpu.roll(top, 64, 1), bottom).astype(BF16)
        if half:
            all_bins(half - 1).wait_send()
        own_copy(half).start()

        for far_x, far_y in FARTHEST_FIRST:

            def launch(j, carry, half=half, far_x=far_x, far_y=far_y):
                to = ((my_v // 4 + far_x) % 2 * 4 + (my_v + far_y) % 4) * QUAD + (my_q + j) % QUAD
                bins_copy(half, to, me).start()
                return carry

            lax.fori_loop(0 if far_x + far_y else 1, QUAD, launch, 0)

    def halo_copy(way, half, chunk):
        span = pl.ds(chunk * CHUNK, CHUNK)
        return pltpu.make_async_remote_copy(
            src_ref=own.at[half, span],
            dst_ref=halo.at[way, half, span],
            send_sem=h_send.at[way, half, chunk],
            recv_sem=h_recv.at[way, half, chunk],
            device_id=device(below if way == 0 else above, me),
            device_id_type=MESH,
        )

    for half in range(HALVES):
        own_copy(half).wait()
        all_bins(half).wait_recv()

        def one_block(v, carry, half=half):
            parts = [recv[half, v * QUAD + q, p * 16 : (p + 1) * 16, :] for p in range(2) for q in range(QUAD)]
            block = jnp.concatenate([part.astype(F32) for part in parts], 0).T
            for h in range(4):
                wh, ri = h // 2, h % 2
                start = pl.multiple_of(((half * 2 + ri) * 16 + v * 2 + wh) * REL_PITCH, 8)
                turned[pl.ds(start, 32), :] = block[h * 32 : (h + 1) * 32]
            return carry

        lax.fori_loop(0, WIN, one_block, 0, unroll=4)

        def gather(chunk, carry, half=half):
            for j in range(CHUNK):
                g = chunk * CHUNK + j
                real = turned[pl.ds(half * 32 * REL_PITCH + g, 16, stride=REL_PITCH), :]
                imag = turned[pl.ds((half * 32 + 16) * REL_PITCH + g, 16, stride=REL_PITCH), :]
                own[half, g] = jnp.concatenate([real, imag], 0).astype(BF16)
            halo_copy(0, half, chunk).start()
            halo_copy(1, half, chunk).start()
            return carry

        lax.fori_loop(0, CHUNKS, gather, 0)

    all_bins(HALVES - 1).wait_send()

    def operand(x, rx):
        def turn(u):
            return jnp.concatenate([u[16:32], -u[:16], u[48:], -u[32:48]], 0)

        return jnp.concatenate([jnp.where(left, x, turn(rx)), jnp.where(left, rx, turn(x))], 0).T.astype(BF16)

    def own_rows(g):
        return jnp.concatenate([own[half, g].astype(F32) for half in range(HALVES)], 0)

    def keep(ref, g, value):
        for part in range(2):
            start = pl.multiple_of((g * 2 + part) * OUT_PITCH, 8)
            ref[pl.ds(start, 64), :] = value[part * 64 : (part + 1) * 64]

    def own_operand(g, carry):
        a = own_rows(g)
        ra = pltpu.roll(a, 64, 1)
        mine = operand(a, ra)
        own_left[g] = mine
        keep(near, g, jnp.dot(mine, jnp.concatenate([a, ra], 0).astype(BF16), preferred_element_type=F32))
        return carry

    lax.fori_loop(0, BINS, own_operand, 0, unroll=4)

    def cross(chunk, carry):
        for way in range(2):
            for half in range(HALVES):
                halo_copy(way, half, chunk).wait_recv()
        for j in range(CHUNK):
            g = chunk * CHUNK + j
            a = own_rows(g)
            e = jnp.concatenate([halo[0, half, g].astype(F32) for half in range(HALVES)], 0)
            m = jnp.concatenate([halo[1, half, g].astype(F32) for half in range(HALVES)], 0)
            e = jnp.where(z + 1 < planes, e, 0.0)
            m = jnp.where(z > 0, m, 0.0)
            ra, re, rm = (pltpu.roll(x, 64, 1) for x in (a, e, m))
            right = jnp.concatenate([jnp.where(left, a, re), jnp.where(left, ra, e)], 0).astype(BF16)
            last = jnp.concatenate([e, re], 0).astype(BF16)
            keep(near, g, jnp.dot(own_left[g], right, preferred_element_type=F32))
            keep(far, g, jnp.dot(operand(m, rm), last, preferred_element_type=F32))
        return carry

    def far_copy(part, to):
        return pltpu.make_async_remote_copy(
            src_ref=send_far.at[part, to],
            dst_ref=got_far.at[part, to],
            send_sem=f_send.at[part, to],
            recv_sem=f_recv.at[part, to],
            device_id=device(below, me),
            device_id_type=MESH,
        )

    def offsets_copy(ref, part, to):
        return pltpu.make_async_remote_copy(
            src_ref=ref.at[part, to],
            dst_ref=got.at[part, me],
            send_sem=x_send.at[part],
            recv_sem=x_recv.at[part],
            device_id=device(z, to),
            device_id_type=MESH,
        )

    def all_offsets(part):
        return pltpu.make_async_remote_copy(
            src_ref=send_near.at[part, pl.ds(0, PLANE - 1)],
            dst_ref=got.at[part, pl.ds(0, PLANE - 1)],
            send_sem=x_send.at[part],
            recv_sem=x_recv.at[part],
            device_id=device(z, (me + 1) % PLANE),
            device_id_type=MESH,
        )

    def own_packet(ref, part):
        return pltpu.make_async_copy(ref.at[part, me], got.at[part, me], own_sem.at[HALVES + part])

    def ship(ref, part, to):
        @pl.when(to != me)
        def _():
            offsets_copy(ref, part, to).start()

        @pl.when(to == me)
        def _():
            own_packet(ref, part).start()

    lane = lax.broadcasted_iota(jnp.int32, (128, 128), 1)

    def packets_of(ref, column, base, size, target, part, q):
        def one_group(i, carry):
            c = q * 16 + i
            start = part * (2 * BINS // PARTS) * OUT_PITCH
            block = jnp.concatenate(
                [
                    ref[pl.ds(start + c + SIDE * k, 2 * BINS // PARTS, stride=OUT_PITCH), :]
                    for k in range(2 * PARTS)
                ],
                0,
            )
            column[i, base : base + size, :] = block.T[:size]
            value = column[i, pl.ds(c + SIDE * (2 * PARTS - 1) + 1, 128), :]
            for k in reversed(range(2 * PARTS - 1)):
                here = column[i, pl.ds(c + SIDE * k + 1, 128), :]
                value = jnp.where(lane < (k + 1) * (2 * BINS // PARTS), here, value)
            value = value.astype(BF16)
            rows = pl.ds(pl.multiple_of(i * 16, 16), 16)
            for v in range(WIN):
                target[part, v * QUAD + q, rows, :] = value[v * 16 : (v + 1) * 16]
            return carry

        lax.fori_loop(0, SIDE, one_group, 0, unroll=True)

    def early_part(part, carry):
        def early_quarter(q, carry):
            packets_of(near, near_col, 0, 128, send_own, part, q)
            for far_x, far_y in FARTHEST_FIRST:
                v = (my_v // 4 + far_x) % 2 * 4 + (my_v + far_y) % 4

                @pl.when(v + q < 3)
                def _(v=v):
                    ship(send_own, part, v * QUAD + q)

            return carry

        return lax.fori_loop(0, 3, early_quarter, carry)

    lax.fori_loop(0, PARTS, early_part, 0)
    loads[6].start()

    def late_part(part, carry):
        def late_quarter(j, carry):
            q = (my_q + j) % QUAD

            def one_send(k, carry):
                to = (WIN - 1 - k) * QUAD + q
                far_copy(part, to).wait_recv()

                @pl.when(k == q)
                def _():
                    send_near[part, to] = (
                        send_near[part, to].astype(F32) + got_far[part, to].astype(F32)
                    ).astype(BF16)
                    ship(send_near, part, to)

                @pl.when(k != q)
                def _():
                    ship(got_far, part, to)

                return carry

            return lax.fori_loop(0, q + 1, one_send, carry)

        return lax.fori_loop(0, QUAD, late_quarter, carry)

    def one_part(part, carry):
        lax.fori_loop(part * (CHUNKS // PARTS), (part + 1) * (CHUNKS // PARTS), cross, 0)

        def far_quarter(j, carry):
            q = (my_q + j) % QUAD
            packets_of(far, far_col, 128, 64, send_far, part, q)

            def one_send(k, carry):
                far_copy(part, (WIN - 1 - k) * QUAD + q).start()
                return carry

            return lax.fori_loop(0, q + 1, one_send, carry)

        lax.fori_loop(0, QUAD, far_quarter, 0)

        def near_quarter(j, carry):
            q = (my_q + j) % QUAD
            packets_of(near, near_col, 0, 128, send_near, part, q)

            for far_x, far_y in FARTHEST_FIRST:
                v = (my_v // 4 + far_x) % 2 * 4 + (my_v + far_y) % 4

                @pl.when((v + q > 2) & (v + q < WIN - 1))
                def _(v=v):
                    ship(send_near, part, v * QUAD + q)

            return carry

        lax.fori_loop(0, QUAD, near_quarter, 0)
        return late_part(part, carry)

    lax.fori_loop(0, PARTS, one_part, 0)


    def drain_halo(chunk, carry):
        for way in range(2):
            for half in range(HALVES):
                halo_copy(way, half, chunk).wait_send()
        return carry

    lax.fori_loop(0, CHUNKS, drain_halo, 0)

    def drain_far(q, carry):
        def one(k, carry):
            for part in range(PARTS):
                far_copy(part, (WIN - 1 - k) * QUAD + q).wait_send()
            return carry

        return lax.fori_loop(0, q + 1, one, carry)

    lax.fori_loop(0, QUAD, drain_far, 0)

    loads[6].wait()
    row_lane = lax.broadcasted_iota(jnp.int32, (SIDE * 16, 128), 1)

    def swap(one, two, width):
        even = (row_lane // width) % 2 == 0
        return (
            jnp.where(even, one, pltpu.roll(two, width, 1)),
            jnp.where(even, pltpu.roll(one, 128 - width, 1), two),
        )

    count = 2 * PARTS
    depth = 2 * NB // PARTS
    for part in range(PARTS):
        own_packet(send_near, part).wait()
        all_offsets(part).wait_recv()
        for f in range(PLANE // count):
            blocks = [got[part, count * f + k].astype(F32) for k in range(count)]
            step = count // 2
            while step:
                for k in range(count):
                    if not k & step:
                        blocks[k], blocks[k + step] = swap(blocks[k], blocks[k + step], step * (128 // count))
                step //= 2
            span = slice(part * depth + f * 128, part * depth + (f + 1) * 128)
            for k in range(count):
                lag_lhs[k * SIDE * 16 : (k + 1) * SIDE * 16, span] = blocks[k].astype(BF16)
        if part == PARTS - 2:
            first_lags[...] = jnp.dot(
                lag_lhs[:, : (part + 1) * depth], table[: (part + 1) * depth, :], preferred_element_type=F32
            )
    last = (PARTS - 1) * depth
    lags = jnp.dot(lag_lhs[:, last:], table[last:, :], preferred_element_type=F32)
    lags = (lags + first_lags[...]) * scale
    for c in range(16):
        out[:, c, :] = lags[c * 16 : (c + 1) * 16]
    for part in range(PARTS):
        all_offsets(part).wait_send()


def body(planes, raw, offsets, mask):
    operands = [offsets, mask, raw, first_tables(), second_stage(), lag_rows()]
    smem = pl.BlockSpec(memory_space=pltpu.SMEM)
    far_away = pl.BlockSpec(memory_space=pltpu.HBM)
    dma = pltpu.SemaphoreType.DMA
    vmem = pltpu.VMEM
    packets = vmem((PARTS, PLANE, SIDE * 16, 128), BF16)
    spectra = vmem(((2 * BINS + 1) * OUT_PITCH, 128), F32)
    return pl.pallas_call(
        functools.partial(main_kernel, planes, 1.0 / math.sqrt(NB * 8 * WIN)),
        out_shape=jax.ShapeDtypeStruct((16, 16, LAGS), F32),
        in_specs=[smem, smem] + [far_away] * 4,
        out_specs=pl.BlockSpec(memory_space=pltpu.VMEM),
        scratch_shapes=[vmem(x.shape, x.dtype) for x in operands[2:]]
        + [
            vmem((RADIX, ROWS, 4 * TAIL), BF16),
            vmem((RADIX, ROWS, 128), F32),
            vmem((2, 8, RADIX, 128), F32),
            vmem((2, 8, 128), F32),
            vmem((ROWS // 16, 16, 128), F32),
            vmem((HALVES, PLANE, 32, 128), BF16),
            vmem((HALVES, PLANE, 32, 128), BF16),
            vmem((65 * REL_PITCH, 128), F32),
            vmem((HALVES, BINS, 32, 128), BF16),
            vmem((2, HALVES, BINS, 32, 128), BF16),
            spectra,
            spectra,
            vmem((SLOTS, 256, 128), F32),
            vmem((SLOTS, 256, 128), F32),
            packets,
            packets,
            packets,
            packets,
            packets,
            vmem((256, 2 * NB), BF16),
            vmem((256, LAGS), F32),
            vmem((BINS, 128, 128), BF16),
            dma((7,)),
            dma((HALVES + PARTS,)),
            dma((HALVES,)),
            dma((HALVES,)),
            dma((2, HALVES, CHUNKS)),
            dma((2, HALVES, CHUNKS)),
            dma((PARTS,)),
            dma((PARTS,)),
            dma((PARTS, PLANE)),
            dma((PARTS, PLANE)),
        ],
        compiler_params=pltpu.CompilerParams(
            collective_id=0, has_side_effects=True, vmem_limit_bytes=48 * 2**20
        ),
        name="main",
    )(*(pltpu.with_memory_space_constraint(jnp.asarray(x), pltpu.HBM) for x in operands))


def solution(mesh):
    planes = mesh.shape["fibre"] // QUAD
    return jax.shard_map(
        functools.partial(body, planes),
        mesh=mesh,
        in_specs=(P("win", "fibre", None), P("win"), P("fibre")),
        out_specs=P("win", "fibre", None),
        check_vma=False,
    )
```

```python
import functools
import math

import jax
import jax.numpy as jnp
import numpy as np
from jax import lax
from jax.experimental import pallas as pl
from jax.experimental.pallas import tpu as pltpu
from jax.sharding import PartitionSpec as P

MESH = pl.DeviceIdType.MESH
L = 4096
BAND_LO = 64
NB = 1024
SMOOTH = 64
LAGS = 512
SPAN = 128
EPS = 1e-06
RADIX = 16
TAIL = L // RADIX
PLANE = 32
WIN = 8
QUAD = 4
BINS = 32
CHUNK = 8
REL_PITCH = 40
OUT_PITCH = 72
SLOTS = 4
PARTS = 2
SIDE = 16 // (2 * PARTS)
FARTHEST_FIRST = ((1, 2), (1, 1), (1, 3), (1, 0), (0, 2), (0, 1), (0, 3), (0, 0))
HALVES = 2
ROWS = 128 // HALVES
CHUNKS = BINS // CHUNK
MEAN_UNROLL = 4
FFT_UNROLL = 2
GROUP = 16
F32 = jnp.float32
BF16 = jnp.bfloat16


def second_stage():
    b = np.arange(TAIL)[:, None]
    lane = np.arange(128)[None, :]
    half, imag, low = lane // 64, (lane // 32) % 2, lane % 32
    angle = 2.0 * np.pi * ((b * (BAND_LO // RADIX + half * 32 + low)) % TAIL) / TAIL
    cos, sin = np.cos(angle), np.sin(angle)
    whole = np.where(imag == 0, np.concatenate([cos, sin], 0), np.concatenate([-sin, cos], 0)).astype(np.float32)
    high = whole.astype(jnp.bfloat16)
    return np.concatenate([high, (whole - high.astype(np.float32)).astype(jnp.bfloat16)], 1)


def first_tables():
    f = np.arange(RADIX)[:, None]
    b = np.arange(TAIL)[None, :]
    twiddle, spot = 2.0 * np.pi * (f * b) / L, 2.0 * np.pi * (TAIL * f + b) / L
    return np.stack([np.cos(twiddle), np.sin(twiddle), np.cos(spot), np.sin(spot)]).astype(np.float32)


def lag_rows():
    frequency = np.arange(NB, dtype=np.int64) + BAND_LO
    lag_index = np.arange(LAGS, dtype=np.int64) - LAGS // 2
    turns = np.mod(frequency[:, None] * lag_index[None, :], L).astype(np.float32)
    angles = turns * np.float32(2.0 * math.pi / L)
    cos, sin = np.cos(angles.astype(np.float64)), np.sin(angles.astype(np.float64))
    table = np.stack([cos, -sin], 1).astype(np.float32)
    bins = RADIX * np.arange(64)[None, :] + np.arange(RADIX)[:, None]
    table = table[bins].reshape(RADIX, 2, PARTS, BINS // PARTS, 2, LAGS)
    return table.transpose(2, 0, 1, 3, 4, 5).reshape(2 * NB, LAGS).astype(jnp.bfloat16)


def real_fft(x):
    n = len(x)
    if n == 2:
        return [(x[0] + x[1], None), (x[0] - x[1], None)]
    even, odd = real_fft(x[0::2]), real_fft(x[1::2])
    half, quarter = n // 2, n // 4
    out = [None] * (half + 1)
    out[0] = (even[0][0] + odd[0][0], None)
    out[half] = (even[0][0] - odd[0][0], None)
    for k in range(1, quarter):
        (er, ei), (orr, oi) = even[k], odd[k]
        c, s = math.cos(2.0 * math.pi * k / n), math.sin(2.0 * math.pi * k / n)
        if 8 * k == n:
            tr, ti = (orr + oi) * c, (oi - orr) * c
        else:
            tr, ti = orr * c + oi * s, oi * c - orr * s
        out[k] = (er + tr, ei + ti)
        out[half - k] = (er - tr, ti - ei)
    out[quarter] = (even[quarter][0], -odd[quarter][0])
    return out


def place():
    fibre, win = lax.axis_index("fibre"), lax.axis_index("win")
    return fibre // QUAD, win * QUAD + fibre % QUAD


def device(z, s):
    return (z * QUAD + s % QUAD, s // QUAD)


def greet_all(planes, z, me):
    barrier = pltpu.get_barrier_semaphore()

    def signal(plane, s):
        pl.semaphore_signal(barrier, inc=1, device_id=device(plane, s), device_id_type=MESH)

    for far_x, far_y in FARTHEST_FIRST:
        v = (me // QUAD // 4 + far_x) % 2 * 4 + (me // QUAD + far_y) % 4

        def one(j, carry, v=v):
            signal(z, v * QUAD + (me + j) % QUAD)
            return carry

        lax.fori_loop(0 if far_x + far_y else 1, QUAD, one, 0, unroll=True)
    signal((z + 1) % planes, me)
    signal((z + planes - 1) % planes, me)
    return PLANE - 1 + 2


def window_of(half, i):
    return (i // 2) * 4 + half * 2 + i % 2


def shifts(offsets, turn_f, turn_g):
    def one_window(w, carry):
        f = lax.broadcasted_iota(jnp.int32, (RADIX, 128), 0)
        angle = ((f * offsets[w]) & (L - 1)).astype(F32) * (2.0 * math.pi / L)
        turn_f[0, w] = jnp.cos(angle)
        turn_f[1, w] = jnp.sin(angle)
        return carry

    lax.fori_loop(0, 8, one_window, 0, unroll=2)
    row = lax.broadcasted_iota(jnp.int32, (8, 128), 0)
    lane = lax.broadcasted_iota(jnp.int32, (8, 128), 1)
    start = jnp.zeros((8, 128), jnp.int32)
    for w in range(8):
        start = jnp.where(row == w, offsets[w], start)
    k = (BAND_LO // RADIX + (lane // 64) * 32 + lane % 32) * RADIX
    angle = ((k * start) & (L - 1)).astype(F32) * (2.0 * math.pi / L)
    turn_g[0] = jnp.cos(angle)
    turn_g[1] = jnp.where((lane // 32) % 2 == 0, -jnp.sin(angle), jnp.sin(angle))


def first_stage(half, offsets, raw, tables, lhs, turn_f, means):
    width = 128
    lane = lax.broadcasted_iota(jnp.int32, (16, width), 1)

    def sample(w, a, low):
        here = raw[w, :, pl.ds(a * TAIL + low, width)].astype(F32)
        if a:
            return here
        return jnp.where(lane + low < offsets[w], raw[w, :, pl.ds(L + low, width)].astype(F32), here)

    def one_mean(i, carry):
        w = window_of(half, i)
        total = functools.reduce(lambda p, q: p + q, [sample(w, a, low) for a in range(RADIX) for low in (0, width)])
        means[i] = jnp.broadcast_to(jnp.sum(total, axis=1, keepdims=True) * (1.0 / L), (16, width))
        return carry

    lax.fori_loop(0, ROWS // 16, one_mean, 0, unroll=MEAN_UNROLL)

    def one_window(index, carry):
        i, column = index // 2, index % 2
        w = window_of(half, i)
        mean = means[i]
        rows = pl.ds(pl.multiple_of(i * 16, 16), 16)
        low = pl.multiple_of(column * width, width)
        span = pl.ds(low, width)
        turn_cos, turn_sin = turn_f[0, w], turn_f[1, w]
        cosine, sine = tables[0, :, span], tables[1, :, span]
        cosine, sine = cosine * turn_cos + sine * turn_sin, sine * turn_cos - cosine * turn_sin
        taper = 0.5 - 0.5 * (tables[2, :, span] * turn_cos[1:2] + tables[3, :, span] * turn_sin[1:2])
        spectrum = real_fft([(sample(w, a, low) - mean) * taper[a : a + 1] for a in range(RADIX)])
        for f in range(RADIX):
            re, im = spectrum[f] if f <= RADIX // 2 else spectrum[RADIX - f]
            if f > RADIX // 2:
                im = -im
            if f:
                c, s = cosine[f : f + 1], sine[f : f + 1]
                re, im = (re * c, -re * s) if im is None else (re * c + im * s, im * c - re * s)
            else:
                im = jnp.zeros_like(re)
            for part, value in enumerate((re, im)):
                high = value.astype(BF16)
                lhs[f, rows, pl.ds(low + part * TAIL, width)] = high
                lhs[f, rows, pl.ds(low + (2 + part) * TAIL, width)] = (value - high.astype(F32)).astype(BF16)
        return carry

    lax.fori_loop(0, ROWS // 8, one_window, 0, unroll=FFT_UNROLL)


def second_stage_of(half, lhs, weights, kept, turn_g):
    lane = lax.broadcasted_iota(jnp.int32, (ROWS, 128), 1)
    real = (lane // 32) % 2 == 0
    turn = [
        jnp.concatenate(
            [jnp.broadcast_to(turn_g[part, w : w + 1], (16, 128)) for w in (window_of(half, i) for i in range(ROWS // 16))],
            0,
        )
        for part in range(2)
    ]
    power = jnp.zeros((ROWS, 128), F32)
    for start in range(0, RADIX, GROUP):
        whole = lhs[start : start + GROUP].reshape(GROUP * ROWS, 4 * TAIL)
        first = jnp.dot(whole[:, : 2 * TAIL], weights[...], preferred_element_type=F32)
        second = jnp.dot(whole[:, 2 * TAIL :], weights[:, :128], preferred_element_type=F32)
        both = (first[:, :128] + first[:, 128:] + second).reshape(GROUP, ROWS, 128)
        for j in range(GROUP):
            one = both[j]
            power = power + one * one
            other = jnp.where(real, pltpu.roll(one, 96, 1), pltpu.roll(one, 32, 1))
            kept[start + j] = one * turn[0] + other * turn[1]
    return power


def whitening(power, mask):
    row = lax.broadcasted_iota(jnp.int32, (128, 128), 0)
    col = lax.broadcasted_iota(jnp.int32, (128, 128), 1)
    same = (row // 64 == col // 64) & ((row % 32) // 4 == (col % 32) // 4)
    block = jnp.where(same, 1.0, 0.0).astype(F32)
    mean_power = jnp.dot(power, block, precision=lax.Precision.HIGHEST, preferred_element_type=F32) * (1.0 / SMOOTH)
    channel = lax.broadcasted_iota(jnp.int32, (16, 128), 0)
    flag = jnp.zeros((16, 128), F32)
    for c in range(16):
        flag = jnp.where(channel == c, mask[c].astype(F32), flag)
    flag = jnp.broadcast_to(flag[None], (ROWS // 16, 16, 128)).reshape(ROWS, 128)
    return (1.0 / jnp.sqrt(mean_power + EPS)) * flag


def main_kernel(
    planes, scale, offsets, mask, raw_hbm, tables_hbm, weights_hbm, table_hbm, out,
    raw, tables, weights, table, lhs, kept, turn_f, turn_g, means,
    send, recv, turned, own, halo, near, far, near_col, far_col, send_own, send_near, send_far, got_far, got, lag_lhs, first_lags, own_left,
    in_sem, own_sem, s_send, s_recv, h_send, h_recv, x_send, x_recv, f_send, f_recv,
):
    z, me = place()
    my_q, my_v = me % QUAD, me // QUAD
    above, below = (z + 1) % planes, (z + planes - 1) % planes
    pairs = [
        (raw_hbm.at[pl.ds(start, 2)], raw.at[pl.ds(start, 2)]) for start in (0, 4, 2, 6)
    ] + [(tables_hbm, tables), (weights_hbm, weights), (table_hbm, table)]
    pairs = [pairs[i] for i in (4, 0, 1, 2, 3, 5, 6)]
    loads = [pltpu.make_async_copy(source, target, in_sem.at[i]) for i, (source, target) in enumerate(pairs)]
    for load in loads[:3]:
        load.start()
    expected = greet_all(planes, z, me)
    for load in loads[3:6]:
        load.start()
    shifts(offsets, turn_f, turn_g)
    for slot in range(SLOTS):
        near_col[slot, 128:, :] = jnp.zeros((128, 128), F32)
        far_col[slot, :128, :] = jnp.zeros((128, 128), F32)
    left = lax.broadcasted_iota(jnp.int32, (64, 128), 1) < 64

    def at_ends(down, up, do):
        @pl.when(z > 0)
        def _():
            do(down)

        @pl.when(z + 1 < planes)
        def _():
            do(up)

    @pl.when(z + 1 == planes)
    def _():
        def clear(to, carry):
            for part in range(PARTS):
                got_far[part, to] = jnp.zeros((SIDE * 16, 128), BF16)
            return carry

        lax.fori_loop(0, PLANE, clear, 0)

    def bins_copy(half, to, source):
        return pltpu.make_async_remote_copy(
            src_ref=send.at[half, to],
            dst_ref=recv.at[half, source],
            send_sem=s_send.at[half],
            recv_sem=s_recv.at[half],
            device_id=device(z, to),
            device_id_type=MESH,
        )

    def all_bins(half):
        return pltpu.make_async_remote_copy(
            src_ref=send.at[half, pl.ds(0, PLANE - 1)],
            dst_ref=recv.at[half, pl.ds(0, PLANE - 1)],
            send_sem=s_send.at[half],
            recv_sem=s_recv.at[half],
            device_id=device(z, (me + 1) % PLANE),
            device_id_type=MESH,
        )

    def own_copy(half):
        return pltpu.make_async_copy(send.at[half, me], recv.at[half, me], own_sem.at[half])

    for half in range(HALVES):
        for load in loads[:3] if half == 0 else loads[3:5]:
            load.wait()
        first_stage(half, offsets, raw, tables, lhs, turn_f, means)
        if half == 0:
            loads[5].wait()
        factor = whitening(second_stage_of(half, lhs, weights, kept, turn_g), mask)
        if half == 0:
            pl.semaphore_wait(pltpu.get_barrier_semaphore(), expected)

        for f in range(RADIX):
            value = kept[f] * factor
            top, bottom = value[:32], value[32:]
            send[half, 2 * f] = jnp.where(left[:32], top, pltpu.roll(bottom, 64, 1)).astype(BF16)
            send[half, 2 * f + 1] = jnp.where(left[:32], pltpu.roll(top, 64, 1), bottom).astype(BF16)
        if half:
            all_bins(half - 1).wait_send()
        own_copy(half).start()

        for far_x, far_y in FARTHEST_FIRST:

            def launch(j, carry, half=half, far_x=far_x, far_y=far_y):
                to = ((my_v // 4 + far_x) % 2 * 4 + (my_v + far_y) % 4) * QUAD + (my_q + j) % QUAD
                bins_copy(half, to, me).start()
                return carry

            lax.fori_loop(0 if far_x + far_y else 1, QUAD, launch, 0)

    def halo_copy(way, half, chunk):
        span = pl.ds(chunk * CHUNK, CHUNK)
        return pltpu.make_async_remote_copy(
            src_ref=own.at[half, span],
            dst_ref=halo.at[way, half, span],
            send_sem=h_send.at[way, half, chunk],
            recv_sem=h_recv.at[way, half, chunk],
            device_id=device(below if way == 0 else above, me),
            device_id_type=MESH,
        )

    for half in range(HALVES):
        own_copy(half).wait()
        all_bins(half).wait_recv()

        def one_block(v, carry, half=half):
            parts = [recv[half, v * QUAD + q, p * 16 : (p + 1) * 16, :] for p in range(2) for q in range(QUAD)]
            block = jnp.concatenate([part.astype(F32) for part in parts], 0).T
            for h in range(4):
                wh, ri = h // 2, h % 2
                start = pl.multiple_of(((half * 2 + ri) * 16 + v * 2 + wh) * REL_PITCH, 8)
                turned[pl.ds(start, 32), :] = block[h * 32 : (h + 1) * 32]
            return carry

        lax.fori_loop(0, WIN, one_block, 0, unroll=4)

        def gather(chunk, carry, half=half):
            for j in range(CHUNK):
                g = chunk * CHUNK + j
                real = turned[pl.ds(half * 32 * REL_PITCH + g, 16, stride=REL_PITCH), :]
                imag = turned[pl.ds((half * 32 + 16) * REL_PITCH + g, 16, stride=REL_PITCH), :]
                own[half, g] = jnp.concatenate([real, imag], 0).astype(BF16)
            at_ends(0, 1, lambda way: halo_copy(way, half, chunk).start())
            return carry

        lax.fori_loop(0, CHUNKS, gather, 0)

    all_bins(HALVES - 1).wait_send()

    def operand(x, rx):
        def turn(u):
            return jnp.concatenate([u[16:32], -u[:16], u[48:], -u[32:48]], 0)

        return jnp.concatenate([jnp.where(left, x, turn(rx)), jnp.where(left, rx, turn(x))], 0).T.astype(BF16)

    def own_rows(g):
        return jnp.concatenate([own[half, g].astype(F32) for half in range(HALVES)], 0)

    def keep(ref, g, value):
        for part in range(2):
            start = pl.multiple_of((g * 2 + part) * OUT_PITCH, 8)
            ref[pl.ds(start, 64), :] = value[part * 64 : (part + 1) * 64]

    def own_operand(g, carry):
        a = own_rows(g)
        ra = pltpu.roll(a, 64, 1)
        mine = operand(a, ra)
        own_left[g] = mine
        keep(near, g, jnp.dot(mine, jnp.concatenate([a, ra], 0).astype(BF16), preferred_element_type=F32))
        return carry

    lax.fori_loop(0, BINS, own_operand, 0, unroll=4)

    def cross(chunk, carry):
        for half in range(HALVES):
            at_ends(1, 0, lambda way, half=half: halo_copy(way, half, chunk).wait_recv())
        for j in range(CHUNK):
            g = chunk * CHUNK + j
            a = own_rows(g)
            e = jnp.concatenate([halo[0, half, g].astype(F32) for half in range(HALVES)], 0)
            m = jnp.concatenate([halo[1, half, g].astype(F32) for half in range(HALVES)], 0)
            e = jnp.where(z + 1 < planes, e, 0.0)
            m = jnp.where(z > 0, m, 0.0)
            ra, re, rm = (pltpu.roll(x, 64, 1) for x in (a, e, m))
            right = jnp.concatenate([jnp.where(left, a, re), jnp.where(left, ra, e)], 0).astype(BF16)
            last = jnp.concatenate([e, re], 0).astype(BF16)
            keep(near, g, jnp.dot(own_left[g], right, preferred_element_type=F32))
            keep(far, g, jnp.dot(operand(m, rm), last, preferred_element_type=F32))
        return carry

    def far_copy(part, to):
        return pltpu.make_async_remote_copy(
            src_ref=send_far.at[part, to],
            dst_ref=got_far.at[part, to],
            send_sem=f_send.at[part, to],
            recv_sem=f_recv.at[part, to],
            device_id=device(below, me),
            device_id_type=MESH,
        )

    def offsets_copy(ref, part, to):
        return pltpu.make_async_remote_copy(
            src_ref=ref.at[part, to],
            dst_ref=got.at[part, me],
            send_sem=x_send.at[part],
            recv_sem=x_recv.at[part],
            device_id=device(z, to),
            device_id_type=MESH,
        )

    def all_offsets(part):
        return pltpu.make_async_remote_copy(
            src_ref=send_near.at[part, pl.ds(0, PLANE - 1)],
            dst_ref=got.at[part, pl.ds(0, PLANE - 1)],
            send_sem=x_send.at[part],
            recv_sem=x_recv.at[part],
            device_id=device(z, (me + 1) % PLANE),
            device_id_type=MESH,
        )

    def own_packet(ref, part):
        return pltpu.make_async_copy(ref.at[part, me], got.at[part, me], own_sem.at[HALVES + part])

    def ship(ref, part, to):
        @pl.when(to != me)
        def _():
            offsets_copy(ref, part, to).start()

        @pl.when(to == me)
        def _():
            own_packet(ref, part).start()

    lane = lax.broadcasted_iota(jnp.int32, (128, 128), 1)

    def packets_of(ref, column, base, size, target, part, q):
        def one_group(i, carry):
            c = q * 16 + i
            start = part * (2 * BINS // PARTS) * OUT_PITCH
            block = jnp.concatenate(
                [
                    ref[pl.ds(start + c + SIDE * k, 2 * BINS // PARTS, stride=OUT_PITCH), :]
                    for k in range(2 * PARTS)
                ],
                0,
            )
            column[i, base : base + size, :] = block.T[:size]
            value = column[i, pl.ds(c + SIDE * (2 * PARTS - 1) + 1, 128), :]
            for k in reversed(range(2 * PARTS - 1)):
                here = column[i, pl.ds(c + SIDE * k + 1, 128), :]
                value = jnp.where(lane < (k + 1) * (2 * BINS // PARTS), here, value)
            value = value.astype(BF16)
            rows = pl.ds(pl.multiple_of(i * 16, 16), 16)
            for v in range(WIN):
                target[part, v * QUAD + q, rows, :] = value[v * 16 : (v + 1) * 16]
            return carry

        lax.fori_loop(0, SIDE, one_group, 0, unroll=True)

    def early_part(part, carry):
        def early_quarter(q, carry):
            packets_of(near, near_col, 0, 128, send_own, part, q)
            for far_x, far_y in FARTHEST_FIRST:
                v = (my_v // 4 + far_x) % 2 * 4 + (my_v + far_y) % 4

                @pl.when(v + q < 3)
                def _(v=v):
                    ship(send_own, part, v * QUAD + q)

            return carry

        return lax.fori_loop(0, 3, early_quarter, carry)

    lax.fori_loop(0, PARTS, early_part, 0)
    loads[6].start()

    def late_part(part, carry):
        def late_quarter(j, carry):
            q = (my_q + j) % QUAD

            def one_send(k, carry):
                to = (WIN - 1 - k) * QUAD + q

                @pl.when(z + 1 < planes)
                def _():
                    far_copy(part, to).wait_recv()


                @pl.when(k == q)
                def _():
                    send_near[part, to] = (
                        send_near[part, to].astype(F32) + got_far[part, to].astype(F32)
                    ).astype(BF16)
                    ship(send_near, part, to)

                @pl.when(k != q)
                def _():
                    ship(got_far, part, to)

                return carry

            return lax.fori_loop(0, q + 1, one_send, carry)

        return lax.fori_loop(0, QUAD, late_quarter, carry)

    def one_part(part, carry):
        lax.fori_loop(part * (CHUNKS // PARTS), (part + 1) * (CHUNKS // PARTS), cross, 0)

        def far_quarter(j, carry):
            q = (my_q + j) % QUAD
            packets_of(far, far_col, 128, 64, send_far, part, q)

            def one_send(k, carry):

                @pl.when(z > 0)
                def _():
                    far_copy(part, (WIN - 1 - k) * QUAD + q).start()

                return carry

            return lax.fori_loop(0, q + 1, one_send, carry)

        lax.fori_loop(0, QUAD, far_quarter, 0)

        def near_quarter(j, carry):
            q = (my_q + j) % QUAD
            packets_of(near, near_col, 0, 128, send_near, part, q)

            for far_x, far_y in FARTHEST_FIRST:
                v = (my_v // 4 + far_x) % 2 * 4 + (my_v + far_y) % 4

                @pl.when((v + q > 2) & (v + q < WIN - 1))
                def _(v=v):
                    ship(send_near, part, v * QUAD + q)

            return carry

        lax.fori_loop(0, QUAD, near_quarter, 0)
        return late_part(part, carry)

    lax.fori_loop(0, PARTS, one_part, 0)


    def drain_halo(chunk, carry):
        for half in range(HALVES):
            at_ends(0, 1, lambda way, half=half: halo_copy(way, half, chunk).wait_send())
        return carry

    lax.fori_loop(0, CHUNKS, drain_halo, 0)

    def drain_far(q, carry):
        def one(k, carry):
            for part in range(PARTS):
                far_copy(part, (WIN - 1 - k) * QUAD + q).wait_send()
            return carry

        return lax.fori_loop(0, q + 1, one, carry)

    @pl.when(z > 0)
    def _():
        lax.fori_loop(0, QUAD, drain_far, 0)


    loads[6].wait()
    row_lane = lax.broadcasted_iota(jnp.int32, (SIDE * 16, 128), 1)

    def swap(one, two, width):
        even = (row_lane // width) % 2 == 0
        return (
            jnp.where(even, one, pltpu.roll(two, width, 1)),
            jnp.where(even, pltpu.roll(one, 128 - width, 1), two),
        )

    count = 2 * PARTS
    depth = 2 * NB // PARTS
    for part in range(PARTS):
        own_packet(send_near, part).wait()
        all_offsets(part).wait_recv()
        for f in range(PLANE // count):
            blocks = [got[part, count * f + k].astype(F32) for k in range(count)]
            step = count // 2
            while step:
                for k in range(count):
                    if not k & step:
                        blocks[k], blocks[k + step] = swap(blocks[k], blocks[k + step], step * (128 // count))
                step //= 2
            span = slice(part * depth + f * 128, part * depth + (f + 1) * 128)
            for k in range(count):
                lag_lhs[k * SIDE * 16 : (k + 1) * SIDE * 16, span] = blocks[k].astype(BF16)
        if part == PARTS - 2:
            first_lags[...] = jnp.dot(
                lag_lhs[:, : (part + 1) * depth], table[: (part + 1) * depth, :], preferred_element_type=F32
            )
    last = (PARTS - 1) * depth
    lags = jnp.dot(lag_lhs[:, last:], table[last:, :], preferred_element_type=F32)
    lags = (lags + first_lags[...]) * scale
    for c in range(16):
        out[:, c, :] = lags[c * 16 : (c + 1) * 16]
    for part in range(PARTS):
        all_offsets(part).wait_send()


def body(planes, raw, offsets, mask):
    operands = [offsets, mask, raw, first_tables(), second_stage(), lag_rows()]
    smem = pl.BlockSpec(memory_space=pltpu.SMEM)
    far_away = pl.BlockSpec(memory_space=pltpu.HBM)
    dma = pltpu.SemaphoreType.DMA
    vmem = pltpu.VMEM
    packets = vmem((PARTS, PLANE, SIDE * 16, 128), BF16)
    spectra = vmem(((2 * BINS + 1) * OUT_PITCH, 128), F32)
    return pl.pallas_call(
        functools.partial(main_kernel, planes, 1.0 / math.sqrt(NB * 8 * WIN)),
        out_shape=jax.ShapeDtypeStruct((16, 16, LAGS), F32),
        in_specs=[smem, smem] + [far_away] * 4,
        out_specs=pl.BlockSpec(memory_space=pltpu.VMEM),
        scratch_shapes=[vmem(x.shape, x.dtype) for x in operands[2:]]
        + [
            vmem((RADIX, ROWS, 4 * TAIL), BF16),
            vmem((RADIX, ROWS, 128), F32),
            vmem((2, 8, RADIX, 128), F32),
            vmem((2, 8, 128), F32),
            vmem((ROWS // 16, 16, 128), F32),
            vmem((HALVES, PLANE, 32, 128), BF16),
            vmem((HALVES, PLANE, 32, 128), BF16),
            vmem((65 * REL_PITCH, 128), F32),
            vmem((HALVES, BINS, 32, 128), BF16),
            vmem((2, HALVES, BINS, 32, 128), BF16),
            spectra,
            spectra,
            vmem((SLOTS, 256, 128), F32),
            vmem((SLOTS, 256, 128), F32),
            packets,
            packets,
            packets,
            packets,
            packets,
            vmem((256, 2 * NB), BF16),
            vmem((256, LAGS), F32),
            vmem((BINS, 128, 128), BF16),
            dma((7,)),
            dma((HALVES + PARTS,)),
            dma((HALVES,)),
            dma((HALVES,)),
            dma((2, HALVES, CHUNKS)),
            dma((2, HALVES, CHUNKS)),
            dma((PARTS,)),
            dma((PARTS,)),
            dma((PARTS, PLANE)),
            dma((PARTS, PLANE)),
        ],
        compiler_params=pltpu.CompilerParams(
            collective_id=0, has_side_effects=True, vmem_limit_bytes=48 * 2**20
        ),
        name="main",
    )(*(pltpu.with_memory_space_constraint(jnp.asarray(x), pltpu.HBM) for x in operands))


def solution(mesh):
    planes = mesh.shape["fibre"] // QUAD
    return jax.shard_map(
        functools.partial(body, planes),
        mesh=mesh,
        in_specs=(P("win", "fibre", None), P("win"), P("fibre")),
        out_specs=P("win", "fibre", None),
        check_vma=False,
    )
```

```python
import functools
import math

import jax
import jax.numpy as jnp
import numpy as np
from jax import lax
from jax.experimental import pallas as pl
from jax.experimental.pallas import tpu as pltpu
from jax.sharding import PartitionSpec as P

MESH = pl.DeviceIdType.MESH
L = 4096
BAND_LO = 64
NB = 1024
SMOOTH = 64
LAGS = 512
SPAN = 128
EPS = 1e-06
RADIX = 16
TAIL = L // RADIX
PLANE = 32
WIN = 8
QUAD = 4
BINS = 32
CHUNK = 8
REL_PITCH = 40
OUT_PITCH = 72
SLOTS = 4
PARTS = 2
SIDE = 16 // (2 * PARTS)
FARTHEST_FIRST = ((1, 2), (1, 1), (1, 3), (1, 0), (0, 2), (0, 1), (0, 3), (0, 0))
HALVES = 2
ROWS = 128 // HALVES
CHUNKS = BINS // CHUNK
MEAN_UNROLL = 4
FFT_UNROLL = 2
GROUP = 16
F32 = jnp.float32
BF16 = jnp.bfloat16


def second_stage():
    b = np.arange(TAIL)[:, None]
    lane = np.arange(128)[None, :]
    half, imag, low = lane // 64, (lane // 32) % 2, lane % 32
    angle = 2.0 * np.pi * ((b * (BAND_LO // RADIX + half * 32 + low)) % TAIL) / TAIL
    cos, sin = np.cos(angle), np.sin(angle)
    whole = np.where(imag == 0, np.concatenate([cos, sin], 0), np.concatenate([-sin, cos], 0)).astype(np.float32)
    high = whole.astype(jnp.bfloat16)
    return np.concatenate([high, (whole - high.astype(np.float32)).astype(jnp.bfloat16)], 1)


def first_tables():
    f = np.arange(RADIX)[:, None]
    b = np.arange(TAIL)[None, :]
    twiddle, spot = 2.0 * np.pi * (f * b) / L, 2.0 * np.pi * (TAIL * f + b) / L
    return np.stack([np.cos(twiddle), np.sin(twiddle), np.cos(spot), np.sin(spot)]).astype(np.float32)


def lag_rows():
    frequency = np.arange(NB, dtype=np.int64) + BAND_LO
    lag_index = np.arange(LAGS, dtype=np.int64) - LAGS // 2
    turns = np.mod(frequency[:, None] * lag_index[None, :], L).astype(np.float32)
    angles = turns * np.float32(2.0 * math.pi / L)
    cos, sin = np.cos(angles.astype(np.float64)), np.sin(angles.astype(np.float64))
    table = np.stack([cos, -sin], 1).astype(np.float32)
    bins = RADIX * np.arange(64)[None, :] + np.arange(RADIX)[:, None]
    table = table[bins].reshape(RADIX, 2, PARTS, BINS // PARTS, 2, LAGS)
    return table.transpose(2, 0, 1, 3, 4, 5).reshape(2 * NB, LAGS).astype(jnp.bfloat16)


def real_fft(x):
    n = len(x)
    if n == 2:
        return [(x[0] + x[1], None), (x[0] - x[1], None)]
    even, odd = real_fft(x[0::2]), real_fft(x[1::2])
    half, quarter = n // 2, n // 4
    out = [None] * (half + 1)
    out[0] = (even[0][0] + odd[0][0], None)
    out[half] = (even[0][0] - odd[0][0], None)
    for k in range(1, quarter):
        (er, ei), (orr, oi) = even[k], odd[k]
        c, s = math.cos(2.0 * math.pi * k / n), math.sin(2.0 * math.pi * k / n)
        if 8 * k == n:
            tr, ti = (orr + oi) * c, (oi - orr) * c
        else:
            tr, ti = orr * c + oi * s, oi * c - orr * s
        out[k] = (er + tr, ei + ti)
        out[half - k] = (er - tr, ti - ei)
    out[quarter] = (even[quarter][0], -odd[quarter][0])
    return out


def place():
    fibre, win = lax.axis_index("fibre"), lax.axis_index("win")
    return fibre // QUAD, win * QUAD + fibre % QUAD


def device(z, s):
    return (z * QUAD + s % QUAD, s // QUAD)


def greet_all(planes, z, me):
    barrier = pltpu.get_barrier_semaphore()

    def signal(plane, s):
        pl.semaphore_signal(barrier, inc=1, device_id=device(plane, s), device_id_type=MESH)

    for far_x, far_y in FARTHEST_FIRST:
        v = (me // QUAD // 4 + far_x) % 2 * 4 + (me // QUAD + far_y) % 4

        def one(j, carry, v=v):
            signal(z, v * QUAD + (me + j) % QUAD)
            return carry

        lax.fori_loop(0 if far_x + far_y else 1, QUAD, one, 0, unroll=True)

    @pl.when(z + 1 < planes)
    def _():
        signal((z + 1) % planes, me)

    @pl.when(z > 0)
    def _():
        signal((z + planes - 1) % planes, me)

    return PLANE - 1 + jnp.where(z > 0, 1, 0) + jnp.where(z + 1 < planes, 1, 0)


def window_of(half, i):
    return (i // 2) * 4 + half * 2 + i % 2


def shifts(offsets, turn_f, turn_g):
    def one_window(w, carry):
        f = lax.broadcasted_iota(jnp.int32, (RADIX, 128), 0)
        angle = ((f * offsets[w]) & (L - 1)).astype(F32) * (2.0 * math.pi / L)
        turn_f[0, w] = jnp.cos(angle)
        turn_f[1, w] = jnp.sin(angle)
        return carry

    lax.fori_loop(0, 8, one_window, 0, unroll=2)
    row = lax.broadcasted_iota(jnp.int32, (8, 128), 0)
    lane = lax.broadcasted_iota(jnp.int32, (8, 128), 1)
    start = jnp.zeros((8, 128), jnp.int32)
    for w in range(8):
        start = jnp.where(row == w, offsets[w], start)
    k = (BAND_LO // RADIX + (lane // 64) * 32 + lane % 32) * RADIX
    angle = ((k * start) & (L - 1)).astype(F32) * (2.0 * math.pi / L)
    turn_g[0] = jnp.cos(angle)
    turn_g[1] = jnp.where((lane // 32) % 2 == 0, -jnp.sin(angle), jnp.sin(angle))


def first_stage(half, offsets, raw, tables, lhs, turn_f, means):
    width = 128
    lane = lax.broadcasted_iota(jnp.int32, (16, width), 1)

    def sample(w, a, low):
        here = raw[w, :, pl.ds(a * TAIL + low, width)].astype(F32)
        if a:
            return here
        return jnp.where(lane + low < offsets[w], raw[w, :, pl.ds(L + low, width)].astype(F32), here)

    def one_mean(i, carry):
        w = window_of(half, i)
        total = functools.reduce(lambda p, q: p + q, [sample(w, a, low) for a in range(RADIX) for low in (0, width)])
        means[i] = jnp.broadcast_to(jnp.sum(total, axis=1, keepdims=True) * (1.0 / L), (16, width))
        return carry

    lax.fori_loop(0, ROWS // 16, one_mean, 0, unroll=MEAN_UNROLL)

    def one_window(index, carry):
        i, column = index // 2, index % 2
        w = window_of(half, i)
        mean = means[i]
        rows = pl.ds(pl.multiple_of(i * 16, 16), 16)
        low = pl.multiple_of(column * width, width)
        span = pl.ds(low, width)
        turn_cos, turn_sin = turn_f[0, w], turn_f[1, w]
        cosine, sine = tables[0, :, span], tables[1, :, span]
        cosine, sine = cosine * turn_cos + sine * turn_sin, sine * turn_cos - cosine * turn_sin
        taper = 0.5 - 0.5 * (tables[2, :, span] * turn_cos[1:2] + tables[3, :, span] * turn_sin[1:2])
        spectrum = real_fft([(sample(w, a, low) - mean) * taper[a : a + 1] for a in range(RADIX)])
        for f in range(RADIX):
            re, im = spectrum[f] if f <= RADIX // 2 else spectrum[RADIX - f]
            if f > RADIX // 2:
                im = -im
            if f:
                c, s = cosine[f : f + 1], sine[f : f + 1]
                re, im = (re * c, -re * s) if im is None else (re * c + im * s, im * c - re * s)
            else:
                im = jnp.zeros_like(re)
            for part, value in enumerate((re, im)):
                high = value.astype(BF16)
                lhs[f, rows, pl.ds(low + part * TAIL, width)] = high
                lhs[f, rows, pl.ds(low + (2 + part) * TAIL, width)] = (value - high.astype(F32)).astype(BF16)
        return carry

    lax.fori_loop(0, ROWS // 8, one_window, 0, unroll=FFT_UNROLL)


def second_stage_of(half, lhs, weights, kept, turn_g):
    lane = lax.broadcasted_iota(jnp.int32, (ROWS, 128), 1)
    real = (lane // 32) % 2 == 0
    turn = [
        jnp.concatenate(
            [jnp.broadcast_to(turn_g[part, w : w + 1], (16, 128)) for w in (window_of(half, i) for i in range(ROWS // 16))],
            0,
        )
        for part in range(2)
    ]
    power = jnp.zeros((ROWS, 128), F32)
    for start in range(0, RADIX, GROUP):
        whole = lhs[start : start + GROUP].reshape(GROUP * ROWS, 4 * TAIL)
        first = jnp.dot(whole[:, : 2 * TAIL], weights[...], preferred_element_type=F32)
        second = jnp.dot(whole[:, 2 * TAIL :], weights[:, :128], preferred_element_type=F32)
        both = (first[:, :128] + first[:, 128:] + second).reshape(GROUP, ROWS, 128)
        for j in range(GROUP):
            one = both[j]
            power = power + one * one
            other = jnp.where(real, pltpu.roll(one, 96, 1), pltpu.roll(one, 32, 1))
            kept[start + j] = one * turn[0] + other * turn[1]
    return power


def whitening(power, mask):
    row = lax.broadcasted_iota(jnp.int32, (128, 128), 0)
    col = lax.broadcasted_iota(jnp.int32, (128, 128), 1)
    same = (row // 64 == col // 64) & ((row % 32) // 4 == (col % 32) // 4)
    block = jnp.where(same, 1.0, 0.0).astype(F32)
    mean_power = jnp.dot(power, block, precision=lax.Precision.HIGHEST, preferred_element_type=F32) * (1.0 / SMOOTH)
    channel = lax.broadcasted_iota(jnp.int32, (16, 128), 0)
    flag = jnp.zeros((16, 128), F32)
    for c in range(16):
        flag = jnp.where(channel == c, mask[c].astype(F32), flag)
    flag = jnp.broadcast_to(flag[None], (ROWS // 16, 16, 128)).reshape(ROWS, 128)
    return (1.0 / jnp.sqrt(mean_power + EPS)) * flag


def main_kernel(
    planes, scale, offsets, mask, raw_hbm, tables_hbm, weights_hbm, table_hbm, out,
    raw, tables, weights, table, lhs, kept, turn_f, turn_g, means,
    send, recv, turned, own, halo, near, far, near_col, far_col, send_own, send_near, send_far, got_far, got, lag_lhs, first_lags, own_left,
    in_sem, own_sem, s_send, s_recv, h_send, h_recv, x_send, x_recv, f_send, f_recv,
):
    z, me = place()
    my_q, my_v = me % QUAD, me // QUAD
    above, below = (z + 1) % planes, (z + planes - 1) % planes
    pairs = [
        (raw_hbm.at[pl.ds(start, 2)], raw.at[pl.ds(start, 2)]) for start in (0, 4, 2, 6)
    ] + [(tables_hbm, tables), (weights_hbm, weights), (table_hbm, table)]
    pairs = [pairs[i] for i in (4, 0, 1, 2, 3, 5, 6)]
    loads = [pltpu.make_async_copy(source, target, in_sem.at[i]) for i, (source, target) in enumerate(pairs)]
    for load in loads[:3]:
        load.start()
    expected = greet_all(planes, z, me)
    for load in loads[3:6]:
        load.start()
    shifts(offsets, turn_f, turn_g)
    for slot in range(SLOTS):
        near_col[slot, 128:, :] = jnp.zeros((128, 128), F32)
        far_col[slot, :128, :] = jnp.zeros((128, 128), F32)
    left = lax.broadcasted_iota(jnp.int32, (64, 128), 1) < 64

    def at_ends(down, up, do):
        @pl.when(z > 0)
        def _():
            do(down)

        @pl.when(z + 1 < planes)
        def _():
            do(up)

    @pl.when(z + 1 == planes)
    def _():
        def clear(to, carry):
            for part in range(PARTS):
                got_far[part, to] = jnp.zeros((SIDE * 16, 128), BF16)
            return carry

        lax.fori_loop(0, PLANE, clear, 0)

    def bins_copy(half, to, source):
        return pltpu.make_async_remote_copy(
            src_ref=send.at[half, to],
            dst_ref=recv.at[half, source],
            send_sem=s_send.at[half],
            recv_sem=s_recv.at[half],
            device_id=device(z, to),
            device_id_type=MESH,
        )

    def all_bins(half):
        return pltpu.make_async_remote_copy(
            src_ref=send.at[half, pl.ds(0, PLANE - 1)],
            dst_ref=recv.at[half, pl.ds(0, PLANE - 1)],
            send_sem=s_send.at[half],
            recv_sem=s_recv.at[half],
            device_id=device(z, (me + 1) % PLANE),
            device_id_type=MESH,
        )

    def own_copy(half):
        return pltpu.make_async_copy(send.at[half, me], recv.at[half, me], own_sem.at[half])

    for half in range(HALVES):
        for load in loads[:3] if half == 0 else loads[3:5]:
            load.wait()
        first_stage(half, offsets, raw, tables, lhs, turn_f, means)
        if half == 0:
            loads[5].wait()
        factor = whitening(second_stage_of(half, lhs, weights, kept, turn_g), mask)
        if half == 0:
            pl.semaphore_wait(pltpu.get_barrier_semaphore(), expected)

        for f in range(RADIX):
            value = kept[f] * factor
            top, bottom = value[:32], value[32:]
            send[half, 2 * f] = jnp.where(left[:32], top, pltpu.roll(bottom, 64, 1)).astype(BF16)
            send[half, 2 * f + 1] = jnp.where(left[:32], pltpu.roll(top, 64, 1), bottom).astype(BF16)
        if half:
            all_bins(half - 1).wait_send()
        own_copy(half).start()

        for far_x, far_y in FARTHEST_FIRST:

            def launch(j, carry, half=half, far_x=far_x, far_y=far_y):
                to = ((my_v // 4 + far_x) % 2 * 4 + (my_v + far_y) % 4) * QUAD + (my_q + j) % QUAD
                bins_copy(half, to, me).start()
                return carry

            lax.fori_loop(0 if far_x + far_y else 1, QUAD, launch, 0)

    def halo_copy(way, half, chunk):
        span = pl.ds(chunk * CHUNK, CHUNK)
        return pltpu.make_async_remote_copy(
            src_ref=own.at[half, span],
            dst_ref=halo.at[way, half, span],
            send_sem=h_send.at[way, half, chunk],
            recv_sem=h_recv.at[way, half, chunk],
            device_id=device(below if way == 0 else above, me),
            device_id_type=MESH,
        )

    for half in range(HALVES):
        own_copy(half).wait()
        all_bins(half).wait_recv()

        def one_block(v, carry, half=half):
            parts = [recv[half, v * QUAD + q, p * 16 : (p + 1) * 16, :] for p in range(2) for q in range(QUAD)]
            block = jnp.concatenate([part.astype(F32) for part in parts], 0).T
            for h in range(4):
                wh, ri = h // 2, h % 2
                start = pl.multiple_of(((half * 2 + ri) * 16 + v * 2 + wh) * REL_PITCH, 8)
                turned[pl.ds(start, 32), :] = block[h * 32 : (h + 1) * 32]
            return carry

        lax.fori_loop(0, WIN, one_block, 0, unroll=4)

        def gather(chunk, carry, half=half):
            for j in range(CHUNK):
                g = chunk * CHUNK + j
                real = turned[pl.ds(half * 32 * REL_PITCH + g, 16, stride=REL_PITCH), :]
                imag = turned[pl.ds((half * 32 + 16) * REL_PITCH + g, 16, stride=REL_PITCH), :]
                own[half, g] = jnp.concatenate([real, imag], 0).astype(BF16)
            at_ends(0, 1, lambda way: halo_copy(way, half, chunk).start())
            return carry

        lax.fori_loop(0, CHUNKS, gather, 0)

    all_bins(HALVES - 1).wait_send()

    def operand(x, rx):
        def turn(u):
            return jnp.concatenate([u[16:32], -u[:16], u[48:], -u[32:48]], 0)

        return jnp.concatenate([jnp.where(left, x, turn(rx)), jnp.where(left, rx, turn(x))], 0).T.astype(BF16)

    def own_rows(g):
        return jnp.concatenate([own[half, g].astype(F32) for half in range(HALVES)], 0)

    def keep(ref, g, value):
        for part in range(2):
            start = pl.multiple_of((g * 2 + part) * OUT_PITCH, 8)
            ref[pl.ds(start, 64), :] = value[part * 64 : (part + 1) * 64]

    def own_operand(g, carry):
        a = own_rows(g)
        ra = pltpu.roll(a, 64, 1)
        mine = operand(a, ra)
        own_left[g] = mine
        keep(near, g, jnp.dot(mine, jnp.concatenate([a, ra], 0).astype(BF16), preferred_element_type=F32))
        return carry

    lax.fori_loop(0, BINS, own_operand, 0, unroll=4)

    def cross(chunk, carry):
        for half in range(HALVES):
            at_ends(1, 0, lambda way, half=half: halo_copy(way, half, chunk).wait_recv())
        for j in range(CHUNK):
            g = chunk * CHUNK + j
            a = own_rows(g)
            e = jnp.concatenate([halo[0, half, g].astype(F32) for half in range(HALVES)], 0)
            m = jnp.concatenate([halo[1, half, g].astype(F32) for half in range(HALVES)], 0)
            e = jnp.where(z + 1 < planes, e, 0.0)
            m = jnp.where(z > 0, m, 0.0)
            ra, re, rm = (pltpu.roll(x, 64, 1) for x in (a, e, m))
            right = jnp.concatenate([jnp.where(left, a, re), jnp.where(left, ra, e)], 0).astype(BF16)
            last = jnp.concatenate([e, re], 0).astype(BF16)
            keep(near, g, jnp.dot(own_left[g], right, preferred_element_type=F32))
            keep(far, g, jnp.dot(operand(m, rm), last, preferred_element_type=F32))
        return carry

    def far_copy(part, to):
        return pltpu.make_async_remote_copy(
            src_ref=send_far.at[part, to],
            dst_ref=got_far.at[part, to],
            send_sem=f_send.at[part, to],
            recv_sem=f_recv.at[part, to],
            device_id=device(below, me),
            device_id_type=MESH,
        )

    def offsets_copy(ref, part, to):
        return pltpu.make_async_remote_copy(
            src_ref=ref.at[part, to],
            dst_ref=got.at[part, me],
            send_sem=x_send.at[part],
            recv_sem=x_recv.at[part],
            device_id=device(z, to),
            device_id_type=MESH,
        )

    def all_offsets(part):
        return pltpu.make_async_remote_copy(
            src_ref=send_near.at[part, pl.ds(0, PLANE - 1)],
            dst_ref=got.at[part, pl.ds(0, PLANE - 1)],
            send_sem=x_send.at[part],
            recv_sem=x_recv.at[part],
            device_id=device(z, (me + 1) % PLANE),
            device_id_type=MESH,
        )

    def own_packet(ref, part):
        return pltpu.make_async_copy(ref.at[part, me], got.at[part, me], own_sem.at[HALVES + part])

    def ship(ref, part, to):
        @pl.when(to != me)
        def _():
            offsets_copy(ref, part, to).start()

        @pl.when(to == me)
        def _():
            own_packet(ref, part).start()

    lane = lax.broadcasted_iota(jnp.int32, (128, 128), 1)

    def packets_of(ref, column, base, size, target, part, q):
        def one_group(i, carry):
            c = q * 16 + i
            start = part * (2 * BINS // PARTS) * OUT_PITCH
            block = jnp.concatenate(
                [
                    ref[pl.ds(start + c + SIDE * k, 2 * BINS // PARTS, stride=OUT_PITCH), :]
                    for k in range(2 * PARTS)
                ],
                0,
            )
            column[i, base : base + size, :] = block.T[:size]
            value = column[i, pl.ds(c + SIDE * (2 * PARTS - 1) + 1, 128), :]
            for k in reversed(range(2 * PARTS - 1)):
                here = column[i, pl.ds(c + SIDE * k + 1, 128), :]
                value = jnp.where(lane < (k + 1) * (2 * BINS // PARTS), here, value)
            value = value.astype(BF16)
            rows = pl.ds(pl.multiple_of(i * 16, 16), 16)
            for v in range(WIN):
                target[part, v * QUAD + q, rows, :] = value[v * 16 : (v + 1) * 16]
            return carry

        lax.fori_loop(0, SIDE, one_group, 0, unroll=True)

    def early_part(part, carry):
        def early_quarter(q, carry):
            packets_of(near, near_col, 0, 128, send_own, part, q)
            for far_x, far_y in FARTHEST_FIRST:
                v = (my_v // 4 + far_x) % 2 * 4 + (my_v + far_y) % 4

                @pl.when(v + q < 3)
                def _(v=v):
                    ship(send_own, part, v * QUAD + q)

            return carry

        return lax.fori_loop(0, 3, early_quarter, carry)

    lax.fori_loop(0, PARTS, early_part, 0)
    loads[6].start()

    def late_part(part, carry):
        def late_quarter(j, carry):
            q = (my_q + j) % QUAD

            def one_send(k, carry):
                to = (WIN - 1 - k) * QUAD + q

                @pl.when(z + 1 < planes)
                def _():
                    far_copy(part, to).wait_recv()


                @pl.when(k == q)
                def _():
                    send_near[part, to] = (
                        send_near[part, to].astype(F32) + got_far[part, to].astype(F32)
                    ).astype(BF16)
                    ship(send_near, part, to)

                @pl.when(k != q)
                def _():
                    ship(got_far, part, to)

                return carry

            return lax.fori_loop(0, q + 1, one_send, carry)

        return lax.fori_loop(0, QUAD, late_quarter, carry)

    def one_part(part, carry):
        lax.fori_loop(part * (CHUNKS // PARTS), (part + 1) * (CHUNKS // PARTS), cross, 0)

        def far_quarter(j, carry):
            q = (my_q + j) % QUAD
            packets_of(far, far_col, 128, 64, send_far, part, q)

            def one_send(k, carry):

                @pl.when(z > 0)
                def _():
                    far_copy(part, (WIN - 1 - k) * QUAD + q).start()

                return carry

            return lax.fori_loop(0, q + 1, one_send, carry)

        lax.fori_loop(0, QUAD, far_quarter, 0)

        def near_quarter(j, carry):
            q = (my_q + j) % QUAD
            packets_of(near, near_col, 0, 128, send_near, part, q)

            for far_x, far_y in FARTHEST_FIRST:
                v = (my_v // 4 + far_x) % 2 * 4 + (my_v + far_y) % 4

                @pl.when((v + q > 2) & (v + q < WIN - 1))
                def _(v=v):
                    ship(send_near, part, v * QUAD + q)

            return carry

        lax.fori_loop(0, QUAD, near_quarter, 0)
        return late_part(part, carry)

    lax.fori_loop(0, PARTS, one_part, 0)


    def drain_halo(chunk, carry):
        for half in range(HALVES):
            at_ends(0, 1, lambda way, half=half: halo_copy(way, half, chunk).wait_send())
        return carry

    lax.fori_loop(0, CHUNKS, drain_halo, 0)

    def drain_far(q, carry):
        def one(k, carry):
            for part in range(PARTS):
                far_copy(part, (WIN - 1 - k) * QUAD + q).wait_send()
            return carry

        return lax.fori_loop(0, q + 1, one, carry)

    @pl.when(z > 0)
    def _():
        lax.fori_loop(0, QUAD, drain_far, 0)


    loads[6].wait()
    row_lane = lax.broadcasted_iota(jnp.int32, (SIDE * 16, 128), 1)

    def swap(one, two, width):
        even = (row_lane // width) % 2 == 0
        return (
            jnp.where(even, one, pltpu.roll(two, width, 1)),
            jnp.where(even, pltpu.roll(one, 128 - width, 1), two),
        )

    count = 2 * PARTS
    depth = 2 * NB // PARTS
    for part in range(PARTS):
        own_packet(send_near, part).wait()
        all_offsets(part).wait_recv()
        for f in range(PLANE // count):
            blocks = [got[part, count * f + k].astype(F32) for k in range(count)]
            step = count // 2
            while step:
                for k in range(count):
                    if not k & step:
                        blocks[k], blocks[k + step] = swap(blocks[k], blocks[k + step], step * (128 // count))
                step //= 2
            span = slice(part * depth + f * 128, part * depth + (f + 1) * 128)
            for k in range(count):
                lag_lhs[k * SIDE * 16 : (k + 1) * SIDE * 16, span] = blocks[k].astype(BF16)
        if part == PARTS - 2:
            first_lags[...] = jnp.dot(
                lag_lhs[:, : (part + 1) * depth], table[: (part + 1) * depth, :], preferred_element_type=F32
            )
    last = (PARTS - 1) * depth
    lags = jnp.dot(lag_lhs[:, last:], table[last:, :], preferred_element_type=F32)
    lags = (lags + first_lags[...]) * scale
    for c in range(16):
        out[:, c, :] = lags[c * 16 : (c + 1) * 16]
    for part in range(PARTS):
        all_offsets(part).wait_send()


def body(planes, raw, offsets, mask):
    operands = [offsets, mask, raw, first_tables(), second_stage(), lag_rows()]
    smem = pl.BlockSpec(memory_space=pltpu.SMEM)
    far_away = pl.BlockSpec(memory_space=pltpu.HBM)
    dma = pltpu.SemaphoreType.DMA
    vmem = pltpu.VMEM
    packets = vmem((PARTS, PLANE, SIDE * 16, 128), BF16)
    spectra = vmem(((2 * BINS + 1) * OUT_PITCH, 128), F32)
    return pl.pallas_call(
        functools.partial(main_kernel, planes, 1.0 / math.sqrt(NB * 8 * WIN)),
        out_shape=jax.ShapeDtypeStruct((16, 16, LAGS), F32),
        in_specs=[smem, smem] + [far_away] * 4,
        out_specs=pl.BlockSpec(memory_space=pltpu.VMEM),
        scratch_shapes=[vmem(x.shape, x.dtype) for x in operands[2:]]
        + [
            vmem((RADIX, ROWS, 4 * TAIL), BF16),
            vmem((RADIX, ROWS, 128), F32),
            vmem((2, 8, RADIX, 128), F32),
            vmem((2, 8, 128), F32),
            vmem((ROWS // 16, 16, 128), F32),
            vmem((HALVES, PLANE, 32, 128), BF16),
            vmem((HALVES, PLANE, 32, 128), BF16),
            vmem((65 * REL_PITCH, 128), F32),
            vmem((HALVES, BINS, 32, 128), BF16),
            vmem((2, HALVES, BINS, 32, 128), BF16),
            spectra,
            spectra,
            vmem((SLOTS, 256, 128), F32),
            vmem((SLOTS, 256, 128), F32),
            packets,
            packets,
            packets,
            packets,
            packets,
            vmem((256, 2 * NB), BF16),
            vmem((256, LAGS), F32),
            vmem((BINS, 128, 128), BF16),
            dma((7,)),
            dma((HALVES + PARTS,)),
            dma((HALVES,)),
            dma((HALVES,)),
            dma((2, HALVES, CHUNKS)),
            dma((2, HALVES, CHUNKS)),
            dma((PARTS,)),
            dma((PARTS,)),
            dma((PARTS, PLANE)),
            dma((PARTS, PLANE)),
        ],
        compiler_params=pltpu.CompilerParams(
            collective_id=0, has_side_effects=True, vmem_limit_bytes=48 * 2**20
        ),
        name="main",
    )(*(pltpu.with_memory_space_constraint(jnp.asarray(x), pltpu.HBM) for x in operands))


def solution(mesh):
    planes = mesh.shape["fibre"] // QUAD
    return jax.shard_map(
        functools.partial(body, planes),
        mesh=mesh,
        in_specs=(P("win", "fibre", None), P("win"), P("fibre")),
        out_specs=P("win", "fibre", None),
        check_vma=False,
    )
```
